32 devices in a mesh: dp: 16 (over z, y, core), head: 2 (over x).
Axes of the slice: x: 2, y: 2, z: 4, core: 2. Of those that a mesh axis runs over, the one named last changes fastest.
Arguments:
- media_tokens: bfloat16 [256, 256, 1024], P('dp'), may hold values from -6 to 6
- latents: bfloat16 [256, 64, 1024], P('dp'), may hold values from -6 to 6
- cotangent: bfloat16 [256, 64, 1024], P('dp'), may hold values from -6 to 6
- image_counts: int32 [128], P('dp'), may hold values from 1 to 2, as said below
- media_gain: float32 [1024], replicated, may hold values from 0.1 to 1.9
- media_bias: float32 [1024], replicated, may hold values from -3 to 3
- latent_gain: float32 [1024], replicated, may hold values from 0.1 to 1.9
- latent_bias: float32 [1024], replicated, may hold values from -3 to 3
- ff_gain: float32 [1024], replicated, may hold values from 0.1 to 1.9
- ff_bias: float32 [1024], replicated, may hold values from -3 to 3
- w_query: bfloat16 [1024, 512], P('dp', 'head'), may hold values from -0.1875 to 0.1875
- w_keyval: bfloat16 [1024, 2, 512], P('dp', None, 'head'), may hold values from -0.1875 to 0.1875
- w_attn_out: bfloat16 [512, 1024], P('head', 'dp'), may hold values from -1 to 1
- w_up: bfloat16 [1024, 4096], P('dp', 'head'), may hold values from -0.1875 to 0.1875
- w_down: bfloat16 [4096, 1024], P('head', 'dp'), may hold values from -0.09375 to 0.09375
Outputs:
- latents_out: float32 [256, 64, 1024], P('dp', 'head')
- media_grad: float32 [256, 256, 1024], P('dp', 'head')
- latent_grad: float32 [256, 64, 1024], P('dp', 'head')
- grad_query: float32 [1024, 512], P('dp', 'head')
- grad_keyval: float32 [1024, 2, 512], P('dp', None, 'head')
- grad_attn_out: float32 [512, 1024], P('head', 'dp')
- grad_up: float32 [1024, 4096], P('dp', 'head')
- grad_down: float32 [4096, 1024], P('head', 'dp')
- norm_grads: float32 [6, 1024], replicated
The draws below stay inside these ranges and needn't reach their ends.
Inputs may be any that keep to these rules, and one draw needn't show every extreme that they name: `image_counts`: samples are stored in order, 8 to each index of dp. The images of a dp index's samples fill its 16 slots from slot 0 on, sample after sample; the other slots of that index are empty. In every draw some sample has 2 images and some dp index has all its slots filled.
All inputs are finite; a program needn't handle non-finite values.
Results may differ from the reference program's by a relative error of at most 0.019.
Values may be sent and summed in bfloat16 or wider, within the bound.
No kernel may reach another device: no remote copies, remote signals or barrier semaphores. Data moves between devices by JAX's collectives and lax.ppermute only.
A program may use at most 192 MiB of HBM per device.

```python
import math
import jax
import jax.numpy as jnp
from jax import lax

D = 1024
H = 8
HD = 64
LAT = 64
FF = 4096
PATCH = 256
IMG_MOST = 2
SAMP_DEV = 8
IMG_DEV = 16
SAMPLES = 128
IMAGES = 256


def draw_image_counts(key, part):
    device_count = SAMPLES // SAMP_DEV
    first_key, second_key = jax.random.split(jax.random.fold_in(key, 11))
    counts = jax.random.randint(first_key, (device_count, SAMP_DEV), 1, IMG_MOST + 1)
    full_device = jax.random.randint(second_key, (), 0, device_count)
    device_rows = jnp.arange(device_count)[:, None]
    counts = jnp.where(device_rows == full_device, IMG_MOST, counts)
    return counts.reshape(SAMPLES).astype(jnp.int32)


def block_scale(rng, dims, shards, low, high):
    def one(position, shards_of):
        steps = jax.random.uniform(jax.random.fold_in(jax.random.fold_in(rng, 6), position), (shards_of,), jnp.float32, low / len(shards), high / len(shards))
        return jnp.repeat(jnp.exp(steps), dims[position] // shards_of).reshape((-1,) + (1,) * (len(dims) - position - 1))

    level = one(*shards[0])
    for cut in shards[1:]:
        level = level * one(*cut)
    return level


def gaussian(rng, dims, scale, reach, cuts=(), kind=jnp.bfloat16):
    result = scale * jax.random.normal(rng, dims, jnp.float32)
    if cuts:
        result = result * block_scale(rng, dims, cuts, -0.22, 0.18)
    return jnp.clip(result, -reach, reach).astype(kind)


def setup_inputs(seed: int = 0) -> dict:
    key_of = jax.random.split(jax.random.key(seed), 16)
    return {
        "media_tokens": gaussian(key_of[0], (IMAGES, PATCH, D), 1.0, 6.0, ((0, 16),)),
        "latents": gaussian(key_of[1], (IMAGES, LAT, D), 1.0, 6.0, ((0, 16),)),
        "cotangent": gaussian(key_of[2], (IMAGES, LAT, D), 1.0, 6.0, ((0, 16),)),
        "image_counts": draw_image_counts(jax.random.fold_in(key_of[15], 71), 0),
        "media_gain": jnp.clip(1.0 + 0.18 * jax.random.normal(key_of[4], (D,), jnp.float32), 0.1, 1.9),
        "media_bias": gaussian(key_of[5], (D,), 0.5, 3.0, (), jnp.float32),
        "latent_gain": jnp.clip(1.0 + 0.18 * jax.random.normal(key_of[6], (D,), jnp.float32), 0.1, 1.9),
        "latent_bias": gaussian(key_of[7], (D,), 0.5, 3.0, (), jnp.float32),
        "ff_gain": jnp.clip(1.0 + 0.18 * jax.random.normal(key_of[8], (D,), jnp.float32), 0.1, 1.9),
        "ff_bias": gaussian(key_of[9], (D,), 0.5, 3.0, (), jnp.float32),
        "w_query": gaussian(key_of[10], (D, H * HD), D ** -0.5, 0.1875, ((0, 16), (1, 2))),
        "w_keyval": gaussian(key_of[11], (D, 2, H * HD), D ** -0.5, 0.1875, ((0, 16), (2, 2))),
        "w_attn_out": gaussian(key_of[12], (H * HD, D), (H * HD // 16) ** -0.5, 1.0, ((0, 2), (1, 16))),
        "w_up": gaussian(key_of[13], (D, FF), D ** -0.5, 0.1875, ((0, 16), (1, 2))),
        "w_down": gaussian(key_of[14], (FF, D), FF ** -0.5, 0.09375, ((0, 2), (1, 16))),
    }


@jax.custom_vjp
def low(v):
    return lax.optimization_barrier(v.astype(jnp.bfloat16)).astype(jnp.float32)

@jax.custom_vjp
def low_back(v):
    return v

def low_keep(v):
    return (low(v), None)

def low_pass(kept, grad):
    return (grad,)

def back_keep(v):
    return (v, None)

def back_low(kept, grad):
    return (low(grad),)
low.defvjp(low_keep, low_pass)
low_back.defvjp(back_keep, back_low)

def layer_norm(values, gain, bias):
    centre = values - lax.optimization_barrier(jnp.mean(values, axis=-1, keepdims=True))
    spread = lax.optimization_barrier(jnp.mean(centre * centre, axis=-1, keepdims=True))
    return centre * lax.rsqrt(spread + 1e-05) * gain + bias

def product(form, left, right):
    return jnp.einsum(form, left, right, precision=lax.Precision.HIGHEST)

def forward(params, media_part, latent_part, live_part):
    media_gain, media_bias, latent_gain, latent_bias, ff_gain, ff_bias, w_query, w_keyval, w_attn_out, w_up, w_down = params
    image_count = latent_part.shape[0]
    lat_rows = latent_part.shape[1]
    normed_media = low(layer_norm(media_part, media_gain, media_bias))
    normed_lat = low(layer_norm(latent_part, latent_gain, latent_bias))
    sources = jnp.concatenate([normed_media, normed_lat], axis=1)
    src_rows = sources.shape[1]
    query_act = low_back(low(product('ild,dc->ilc', normed_lat, w_query)))
    keyval = low_back(low(product('ird,dkc->ikrc', sources, w_keyval)))
    query_blocks = query_act.reshape(image_count, lat_rows, H, HD)
    key_blocks = keyval[:, 0].reshape(image_count, src_rows, H, HD)
    value_blocks = keyval[:, 1].reshape(image_count, src_rows, H, HD)
    scores = low_back(product('ilhe,irhe->ihlr', query_blocks, key_blocks) * (1.0 / math.sqrt(HD)))
    row_top = lax.optimization_barrier(jnp.max(scores, axis=-1, keepdims=True))
    exp_terms = jnp.exp(scores - row_top)
    attn_probs = low(exp_terms / lax.optimization_barrier(jnp.sum(exp_terms, axis=-1, keepdims=True)))
    mixed_raw = product('ihlr,irhe->ilhe', attn_probs, value_blocks).reshape(image_count, lat_rows, H * HD)
    mixed_heads = low_back(low(mixed_raw))
    middle = latent_part + low_back(product('ilc,cd->ild', mixed_heads, w_attn_out))
    normed_mid = low(layer_norm(middle, ff_gain, ff_bias))
    up_act = low_back(product('ild,df->ilf', normed_mid, w_up))
    hidden = low(jax.nn.gelu(up_act, approximate=False))
    final_lat = middle + low_back(product('ilf,fd->ild', hidden, w_down))
    return jnp.where(live_part[:, None, None] > 0, final_lat, latent_part)

def reference(media_tokens, latents, cotangent, image_counts, media_gain, media_bias, latent_gain, latent_bias, ff_gain, ff_bias, w_query, w_keyval, w_attn_out, w_up, w_down):
    params = tuple((item.astype(jnp.float32) for item in (media_gain, media_bias, latent_gain, latent_bias, ff_gain, ff_bias, w_query, w_keyval, w_attn_out, w_up, w_down)))
    per_device = lax.optimization_barrier(jnp.sum(image_counts.reshape(SAMPLES // SAMP_DEV, SAMP_DEV), axis=1))
    slot_index = jnp.arange(IMG_DEV, dtype=jnp.int32)
    live_mask = (slot_index[None, :] < per_device[:, None]).astype(jnp.float32).reshape(IMAGES)
    group_size = math.gcd(IMAGES, 8)
    steps_total = IMAGES // group_size

    def split_groups(array):
        return array.reshape((steps_total, group_size) + array.shape[1:])

    def one_group(carry, items):
        media_part, latent_part, cot_part, live_part = items

        def run(param_set, media_in, latent_in):
            return forward(param_set, media_in, latent_in, live_part)
        outputs, pull = jax.vjp(run, params, media_part.astype(jnp.float32), latent_part.astype(jnp.float32))
        param_grads, media_part_grad, latent_part_grad = pull(cot_part.astype(jnp.float32))
        carry = jax.tree.map(lambda total, term: total + term, carry, param_grads)
        return (carry, (outputs, media_part_grad, latent_part_grad))
    zero_grads = jax.tree.map(jnp.zeros_like, params)
    sums, stacked = lax.scan(one_group, zero_grads, (split_groups(media_tokens), split_groups(latents), split_groups(cotangent), split_groups(live_mask)))
    latents_out = stacked[0].reshape(IMAGES, LAT, D)
    media_grad = stacked[1].reshape(IMAGES, PATCH, D)
    latent_grad = stacked[2].reshape(IMAGES, LAT, D)
    norm_grads = jnp.stack(sums[:6])
    return (latents_out, media_grad, latent_grad, sums[6], sums[7], sums[8], sums[9], sums[10], norm_grads)
```

```python
import functools

import jax
import jax.numpy as jnp
from jax import lax
from jax.experimental import pallas as pl
from jax.experimental.pallas import tpu as pltpu
from jax.sharding import PartitionSpec as P

HD = 64
HEADS = 8
CHUNKS = 2
EPS = 1e-05
BF = jnp.bfloat16
F32 = jnp.float32
MIB = 1024 * 1024

NN = (((1,), (0,)), ((), ()))
NT = (((1,), (1,)), ((), ()))
TN = (((0,), (0,)), ((), ()))


def dot(left, right, form=NN):
    return lax.dot_general(left, right, form, preferred_element_type=F32)


def struct(shape, dtype):
    return jax.ShapeDtypeStruct(shape, dtype)


def call(kernel, grid, in_specs, out_specs, out_shape, scratch, ids, args, flops, name, vmem=48):
    outs = out_shape if isinstance(out_shape, (list, tuple)) else [out_shape]
    moved = sum(a.size * a.dtype.itemsize for a in args)
    moved += sum(o.size * jnp.dtype(o.dtype).itemsize for o in outs)
    return pl.pallas_call(
        kernel,
        grid_spec=pltpu.PrefetchScalarGridSpec(
            num_scalar_prefetch=1,
            grid=grid,
            in_specs=in_specs,
            out_specs=out_specs,
            scratch_shapes=scratch,
        ),
        out_shape=out_shape,
        compiler_params=pltpu.CompilerParams(
            vmem_limit_bytes=vmem * MIB, dimension_semantics=("arbitrary",) * len(grid)
        ),
        cost_estimate=pl.CostEstimate(
            flops=int(flops), bytes_accessed=int(moved), transcendentals=0
        ),
        name=name,
    )(ids, *args)


def whole(array):
    zeros = (0,) * array.ndim
    return pl.BlockSpec(array.shape, lambda *_: zeros)


def rows_of(block, width):
    return pl.BlockSpec((block, width), lambda i, ids: (i, 0))


def norm_parts(values):
    centre = values - jnp.mean(values, axis=-1, keepdims=True)
    rstd = lax.rsqrt(jnp.mean(centre * centre, axis=-1, keepdims=True) + EPS)
    return centre * rstd, rstd


def norm_back(values, gain, grad):
    xhat, rstd = norm_parts(values)
    scaled = grad * gain
    first = jnp.mean(scaled, axis=-1, keepdims=True)
    second = jnp.mean(scaled * xhat, axis=-1, keepdims=True)
    back = rstd * (scaled - first - xhat * second)
    return (
        back,
        jnp.sum(grad * xhat, axis=0, keepdims=True),
        jnp.sum(grad, axis=0, keepdims=True),
    )


def norm_kernel(
    imgs, lat, share, patch, ids, media, latents, m_gain, m_bias, l_gain, l_bias, src, nlat, keep
):
    start = pl.multiple_of(ids[0] * share, share)
    step = patch + share
    for i in range(imgs):
        xhat, _ = norm_parts(media[i].astype(F32))
        src[i * step : i * step + patch, :] = (xhat * m_gain[...] + m_bias[...]).astype(BF)
        xhat, _ = norm_parts(latents[i].astype(F32))
        normed = xhat * l_gain[...] + l_bias[...]
        nlat[i * lat : (i + 1) * lat, :] = normed.astype(BF)
        keep[...] = normed
        src[i * step + patch : (i + 1) * step, :] = keep[pl.ds(start, share), :].astype(BF)


def assemble(entries, pieces, depth, ids, rows, groups, width, name):
    def kernel(ids_ref, *refs):
        out, sems = refs[len(pieces)], refs[len(pieces) + 1]
        copies = []
        for e, (op, lead, group, s, yf, cf) in enumerate(entries):
            block = lax.rem(ids_ref[1] + s, depth) * 4
            block += lax.rem(ids_ref[2] + yf, 2) * 2 + lax.rem(ids_ref[3] + cf, 2)
            start = pl.multiple_of(block * rows, rows)
            source = refs[op] if lead is None else refs[op].at[lead]
            copies.append(
                pltpu.make_async_copy(source, out.at[group, pl.ds(start, rows), :], sems.at[e])
            )
        for copy in copies:
            copy.start()
        for copy in copies:
            copy.wait()

    return call(
        kernel,
        (1,),
        [pl.BlockSpec(memory_space=pl.ANY)] * len(pieces),
        pl.BlockSpec(memory_space=pl.ANY),
        struct((groups, depth * 4 * rows, width), BF),
        [pltpu.SemaphoreType.DMA((len(entries),))],
        ids,
        pieces,
        0,
        name,
        vmem=4,
    )


def diag_mask(heads, width, dtype):
    row = lax.broadcasted_iota(jnp.int32, (heads * HD, width), 0) // HD
    col = lax.broadcasted_iota(jnp.int32, (heads * HD, width), 1) // HD
    return jnp.where(row == col, 1.0, 0.0).astype(dtype)


def spread(block, heads, mask):
    return jnp.concatenate([block] * heads, axis=0) * mask


def fold(full, heads, lat, mask):
    full = full * mask
    total = full[:lat]
    for h in range(1, heads):
        total = total + full[h * lat : (h + 1) * lat]
    return total


def project_kernel(groups, cw, imgs, step, lat, ids, src, nlat, w, q, kv, stats):
    heads = cw // HD
    for j in range(groups):
        kv[:, j * 2 * cw : (j + 1) * 2 * cw] = dot(src[...], w[j, :, cw : 3 * cw]).astype(BF)
        q[:, j * cw : (j + 1) * cw] = (dot(nlat[...], w[j, :, :cw]) * (HD**-0.5)).astype(BF)
    mask = diag_mask(heads, cw, BF)
    for i in range(imgs):
        for j in range(groups):
            keys = kv[i * step : (i + 1) * step, j * 2 * cw : j * 2 * cw + cw]
            qbd = spread(q[i * lat : (i + 1) * lat, j * cw : (j + 1) * cw], heads, mask)
            score = dot(keys, qbd, NT)
            top = jnp.max(score, axis=0, keepdims=True)
            stats[i, 0:1, j * cw : (j + 1) * cw] = top
            stats[i, 1:2, j * cw : (j + 1) * cw] = jnp.sum(
                jnp.exp(score - top), axis=0, keepdims=True
            )


def send_rows(groups, share, ids, scratch, i, keep, send):
    for s in range(groups):
        start = pl.multiple_of(lax.rem(ids[0] + s, groups) * share, share)
        rows = scratch[pl.ds(start, share), :]
        if s == 0:
            keep[i * share : (i + 1) * share, :] = rows
        else:
            send[s - 1, i * share : (i + 1) * share, :] = rows.astype(BF)


def mix_kernel(groups, cw, imgs, step, lat, share, ids, q, kv, lse, keep, send, scratch):
    heads = cw // HD
    mask, fmask = diag_mask(heads, cw, BF), diag_mask(heads, cw, F32)
    for i in range(imgs):
        for j in range(groups):
            keys = kv[i * step : (i + 1) * step, j * 2 * cw : j * 2 * cw + cw]
            values = kv[i * step : (i + 1) * step, j * 2 * cw + cw : (j + 1) * 2 * cw]
            qbd = spread(q[i * lat : (i + 1) * lat, j * cw : (j + 1) * cw], heads, mask)
            probs = jnp.exp(dot(keys, qbd, NT) - lse[i, 0:1, j * cw : (j + 1) * cw])
            full = dot(probs.astype(BF), values, TN)
            scratch[i, :, j * cw : (j + 1) * cw] = fold(full, heads, lat, fmask)
        send_rows(groups, share, ids, scratch.at[i], i, keep, send)


def back_probs_kernel(
    groups, cw, imgs, step, lat, share, ids, q, kv, lse, grad_keep, *refs
):
    recv, (grad_all, delta, scratch) = refs[: groups - 1], refs[groups - 1 :]
    heads = cw // HD
    mask = diag_mask(heads, cw, BF)
    for i in range(imgs):
        for s in range(groups):
            start = pl.multiple_of(lax.rem(ids[0] + s, groups) * share, share)
            block = grad_keep if s == 0 else recv[s - 1]
            block = lane_roll(block[i * share : (i + 1) * share, :].astype(F32), s, groups, cw)
            scratch[i, pl.ds(start, share), :] = block
        grad_all[i * lat : (i + 1) * lat, :] = scratch[i].astype(BF)
        for j in range(groups):
            keys = kv[i * step : (i + 1) * step, j * 2 * cw : j * 2 * cw + cw]
            values = kv[i * step : (i + 1) * step, j * 2 * cw + cw : (j + 1) * 2 * cw]
            qbd = spread(q[i * lat : (i + 1) * lat, j * cw : (j + 1) * cw], heads, mask)
            gbd = spread(grad_all[i * lat : (i + 1) * lat, j * cw : (j + 1) * cw], heads, mask)
            probs = jnp.exp(dot(keys, qbd, NT) - lse[i, 0:1, j * cw : (j + 1) * cw])
            delta[i, 0:1, j * cw : (j + 1) * cw] = jnp.sum(
                probs * dot(values, gbd, NT), axis=0, keepdims=True
            )


def back_scores_kernel(
    groups, cw, imgs, step, lat, share, ids, q, kv, lse, grad_all, delta, gkv, gq, keep, send, scratch
):
    heads = cw // HD
    mask, fmask = diag_mask(heads, cw, BF), diag_mask(heads, cw, F32)
    for i in range(imgs):
        for j in range(groups):
            keys = kv[i * step : (i + 1) * step, j * 2 * cw : j * 2 * cw + cw]
            values = kv[i * step : (i + 1) * step, j * 2 * cw + cw : (j + 1) * 2 * cw]
            qbd = spread(q[i * lat : (i + 1) * lat, j * cw : (j + 1) * cw], heads, mask)
            gbd = spread(grad_all[i * lat : (i + 1) * lat, j * cw : (j + 1) * cw], heads, mask)
            probs = jnp.exp(dot(keys, qbd, NT) - lse[i, 0:1, j * cw : (j + 1) * cw])
            grad = dot(values, gbd, NT) - delta[i, 0:1, j * cw : (j + 1) * cw]
            grad = (probs * grad).astype(BF)
            gkv[i * step : (i + 1) * step, j * 2 * cw : j * 2 * cw + cw] = dot(grad, qbd).astype(BF)
            gkv[i * step : (i + 1) * step, j * 2 * cw + cw : (j + 1) * 2 * cw] = dot(
                probs.astype(BF), gbd
            ).astype(BF)
            full = dot(grad, keys, TN)
            scratch[i, :, j * cw : (j + 1) * cw] = fold(full, heads, lat, fmask) * (HD**-0.5)
        gq[i * lat : (i + 1) * lat, :] = scratch[i].astype(BF)
        send_rows(groups, share, ids, scratch.at[i], i, keep, send)


def lane_roll(values, s, groups, cw):
    if s == 0:
        return values
    if cw % 128 == 0:
        cut = (groups - s) * cw
        return jnp.concatenate([values[:, cut:], values[:, :cut]], axis=1)
    return pltpu.roll(values, s * cw, 1)


def middle_kernel(groups, cw, ids, keep, *refs):
    recv = refs[: groups - 1]
    latents, w, gain, bias, mixed, middle, normed = refs[groups - 1 :]
    total = keep[...]
    for s in range(1, groups):
        total = total + lane_roll(recv[s - 1][...].astype(F32), s, groups, cw)
    low = total.astype(BF)
    mixed[...] = low
    rows, width = middle.shape
    value = latents[...].astype(F32).reshape(rows, width)
    for j in range(groups):
        value = value + dot(low[:, j * cw : (j + 1) * cw], w[j, :, 3 * cw :], NT)
    middle[...] = value
    xhat, _ = norm_parts(value)
    normed[...] = (xhat * gain[...] + bias[...]).astype(BF)


def gelu_parts(value):
    cdf = 0.5 * (1.0 + lax.erf(value * (0.5**0.5)))
    pdf = jnp.exp(value * value * -0.5) * 0.3989422804014327
    return value * cdf, cdf + value * pdf


def forward_kernel(ids, normed, final, up, down, hidden, up_low, ff, mid, ff_total, mid_total):
    step = pl.program_id(0)

    @pl.when(step == 0)
    def _():
        ff_total[...] = jnp.zeros_like(ff_total)
        mid_total[...] = jnp.zeros_like(mid_total)

    act, slope = gelu_parts(dot(normed[...], up[...]))
    low = act.astype(BF)
    hidden[...] = low
    ff_total[...] += dot(low, down[...], NT)
    low = (dot(final[...], down[...]) * slope).astype(BF)
    up_low[...] = low
    mid_total[...] += dot(low, up[...], NT)

    @pl.when(step == pl.num_programs(0) - 1)
    def _():
        ff[...] = ff_total[...].astype(BF)
        mid[...] = mid_total[...].astype(BF)


def middle_back_kernel(groups, cw, ids, part, *refs):
    recv = refs[: groups - 1]
    middle, final, w, gain, grad_mid, mid_low, grad_mixed, gains = refs[groups - 1 :]
    total = part[...].astype(F32)
    for other in recv:
        total = total + other[...].astype(F32)
    back, gain_grad, bias_grad = norm_back(middle[...], gain[...], total)
    gains[0:1, :] = gain_grad
    gains[1:2, :] = bias_grad
    value = final[...].astype(F32) + back
    grad_mid[...] = value
    low = value.astype(BF)
    mid_low[...] = low
    for j in range(groups):
        grad_mixed[:, j * cw : (j + 1) * cw] = dot(low, w[j, :, 3 * cw :]).astype(BF)


def weight_grad_kernel(terms, rows, ids, *refs):
    left, right = refs[:terms], refs[terms : 2 * terms]
    keep, send, total = refs[2 * terms :]
    value = dot(left[0][...], right[0][...], TN)
    for k in range(1, terms):
        value = value + dot(left[k][...], right[k][...], TN)
    total[...] = value
    for b in range(keep.shape[0]):
        for ref, core in ((keep, ids[3]), (send, 1 - ids[3])):
            start = pl.multiple_of((b * 2 + core) * rows, rows)
            ref[b] = total[pl.ds(start, rows), :].astype(BF)


def weight_grad(ids, left, right, rows, block, name):
    depth, width = left[0].shape[1], right[0].shape[1]
    blocks = depth // rows // 2
    out = struct((blocks, rows, width), BF)
    spec = pl.BlockSpec((blocks, rows, block), lambda i, ids: (0, 0, i))
    return call(
        functools.partial(weight_grad_kernel, len(left), rows),
        (width // block,),
        [whole(a) for a in left]
        + [pl.BlockSpec((a.shape[0], block), lambda i, ids: (0, i)) for a in right],
        [spec, spec],
        [out, out],
        [pltpu.VMEM((depth, block), F32)],
        ids,
        list(left) + list(right),
        2 * sum(a.shape[0] for a in left) * depth * width,
        name,
    )


def source_back_kernel(
    groups, cw, imgs, patch, share, ids, live, gkv, w, media, latents, cot, keep, *refs
):
    recv = refs[: groups - 1]
    grad_mid, m_gain, l_gain, media_grad, latent_grad, gains = refs[groups - 1 :]
    first = pl.program_id(0) * imgs
    step = patch + share
    total = dot(gkv[:, : 2 * cw], w[0, :, cw : 3 * cw], NT)
    for j in range(1, groups):
        total = total + dot(gkv[:, j * 2 * cw : (j + 1) * 2 * cw], w[j, :, cw : 3 * cw], NT)
    query = keep[...]
    for s in range(1, groups):
        query = query + lane_roll(recv[s - 1][...].astype(F32), s, groups, cw)
    query = query.astype(BF)
    lat = dot(query[:, :cw], w[0, :, :cw], NT)
    for j in range(1, groups):
        lat = lat + dot(query[:, j * cw : (j + 1) * cw], w[j, :, :cw], NT)

    @pl.when(pl.program_id(0) == 0)
    def _():
        gains[...] = jnp.zeros_like(gains)

    for i in range(imgs):
        back, gain_grad, bias_grad = norm_back(
            media[i].astype(F32), m_gain[...], total[i * step : i * step + patch]
        )
        media_grad[i] = back
        gains[0:1, :] += gain_grad
        gains[1:2, :] += bias_grad
        rows = slice(i * share, (i + 1) * share)
        back, gain_grad, bias_grad = norm_back(
            latents[i].astype(F32), l_gain[...], total[i * step + patch : (i + 1) * step] + lat[rows]
        )
        gains[2:3, :] += gain_grad
        gains[3:4, :] += bias_grad
        latent_grad[i] = jnp.where(
            live[first + i] > 0, grad_mid[rows, :] + back, cot[i].astype(F32)
        )


def make_local(depth_z, groups):
    dp_size = depth_z * 4

    def from_dp(value, s=0, yf=0, cf=0):
        pairs = []
        for dst in range(dp_size):
            z, y, c = dst // 4, dst // 2 % 2, dst % 2
            pairs.append(((z + s) % depth_z * 4 + (y ^ yf) * 2 + (c ^ cf), dst))
        return lax.ppermute(value, "dp", pairs)

    def from_head(value, s):
        return lax.ppermute(value, "head", [((x + s) % groups, x) for x in range(groups)])

    def to_head(value, s):
        return lax.ppermute(value, "head", [(x, (x + s) % groups) for x in range(groups)])

    def plane(value, sx, yf, back):
        pairs = []
        for dst in range(dp_size):
            for x in range(groups):
                other = (dst ^ (2 * yf)) * groups + (x + sx) % groups
                mine = dst * groups + x
                pairs.append((mine, other) if back else (other, mine))
        return lax.ppermute(value, ("dp", "head"), pairs)

    def local(
        media_tokens,
        latents,
        cotangent,
        image_counts,
        media_gain,
        media_bias,
        latent_gain,
        latent_bias,
        ff_gain,
        ff_bias,
        w_query,
        w_keyval,
        w_attn_out,
        w_up,
        w_down,
    ):
        images, patches, width = media_tokens.shape
        lat = latents.shape[1]
        rows, cw = w_query.shape
        units = w_up.shape[1]
        patch, share = patches // groups, lat // groups
        step = patch + share
        heads_w = cw * groups
        me = lax.axis_index("head").astype(jnp.int32)
        place = lax.axis_index("dp").astype(jnp.int32)
        z, y, c = place // 4, place // 2 % 2, place % 2
        ids = jnp.stack([me, z, y, c])
        live = (jnp.arange(images, dtype=jnp.int32) < jnp.sum(image_counts)).astype(jnp.int32)
        gains = [
            g.reshape(1, width)
            for g in (media_gain, media_bias, latent_gain, latent_bias, ff_gain, ff_bias)
        ]

        attn_shard = jnp.concatenate([w_query, w_keyval[:, 0], w_keyval[:, 1], w_attn_out.T], axis=1)
        ff_shard = jnp.concatenate([w_up, w_down.T], axis=1)
        line = jnp.stack([attn_shard] + [from_dp(attn_shard, s) for s in range(1, depth_z)])
        pieces, entries = [], []
        for sx in range(groups):
            for yf in range(2):
                part = line if sx == yf == 0 else plane(line, sx, yf, False)
                for cf, piece in ((0, part), (1, from_dp(part, cf=1))):
                    for s in range(depth_z):
                        entries.append((len(pieces), s, sx, s, yf, cf))
                    pieces.append(piece)
        w_attn = assemble(entries, pieces, depth_z, ids, rows, groups, 4 * cw, "place_attn")
        pieces, entries = [], []
        for s in range(depth_z):
            part = ff_shard if s == 0 else from_dp(ff_shard, s)
            for yf, row in ((0, part), (1, from_dp(part, yf=1))):
                for cf, piece in ((0, row), (1, from_dp(row, cf=1))):
                    entries.append((len(pieces), None, 0, s, yf, cf))
                    pieces.append(piece)
        w_ff = assemble(entries, pieces, depth_z, ids, rows, 1, 2 * units, "place_ff")[0]

        imgs = 2
        media4 = media_tokens.reshape(images, groups, patch, width)
        lat4 = latents.reshape(images, groups, share, width)
        cot4 = cotangent.reshape(images, groups, share, width)
        src, nlat = call(
            functools.partial(norm_kernel, imgs, lat, share, patch),
            (images // imgs,),
            [
                pl.BlockSpec((imgs, None, patch, width), lambda i, ids: (i, ids[0], 0, 0)),
                pl.BlockSpec((imgs, lat, width), lambda i, ids: (i, 0, 0)),
            ]
            + [whole(gains[0])] * 4,
            [rows_of(imgs * step, width), rows_of(imgs * lat, width)],
            [struct((images * step, width), BF), struct((images * lat, width), BF)],
            [pltpu.VMEM((lat, width), F32)],
            ids,
            [media4, latents] + gains[:4],
            images * step * width * 12,
            "input_norms",
        )
        final4 = jnp.stack(
            [
                lax.dynamic_index_in_dim(cot4, (me + s) % groups, 1, keepdims=False)
                for s in range(groups)
            ]
        ) * live.astype(BF).reshape(1, images, 1, 1)

        imgs = 4
        attn_macs = images * step * lat * heads_w
        q, kv, stats = call(
            functools.partial(project_kernel, groups, cw, imgs, step, lat),
            (images // imgs,),
            [rows_of(imgs * step, width), rows_of(imgs * lat, width), whole(w_attn)],
            [
                rows_of(imgs * lat, heads_w),
                rows_of(imgs * step, 2 * heads_w),
                pl.BlockSpec((imgs, 2, heads_w), lambda i, ids: (i, 0, 0)),
            ],
            [
                struct((images * lat, heads_w), BF),
                struct((images * step, 2 * heads_w), BF),
                struct((images, 2, heads_w), F32),
            ],
            [],
            ids,
            [src, nlat, w_attn],
            2 * images * (step * width * 2 * heads_w + lat * width * heads_w) + 8 * attn_macs,
            "project",
        )
        tops, sums = [stats[:, :1]], [stats[:, 1:]]
        for s in range(1, groups):
            other = jnp.roll(from_head(stats, s), s * cw, axis=2)
            tops.append(other[:, :1])
            sums.append(other[:, 1:])
        top = functools.reduce(jnp.maximum, tops)
        lse = top + jnp.log(sum(t * jnp.exp(m - top) for m, t in zip(tops, sums)))

        part = images // CHUNKS
        count = part // imgs
        own = part * share
        lat_block = part * lat

        def chunk_rows(ch, size):
            return pl.BlockSpec((imgs * size[0], size[1]), lambda i, ids: (i + ch * count, 0))

        def chunk_images(ch):
            return pl.BlockSpec((imgs, 1, heads_w), lambda i, ids: (i + ch * count, 0, 0))

        def attn_specs(ch):
            return [
                chunk_rows(ch, (lat, heads_w)),
                chunk_rows(ch, (step, 2 * heads_w)),
                chunk_images(ch),
            ]

        row_sends = [
            rows_of(imgs * share, heads_w),
            pl.BlockSpec((groups - 1, imgs * share, heads_w), lambda i, ids: (0, i, 0)),
        ]
        row_outs = [struct((own, heads_w), F32), struct((groups - 1, own, heads_w), BF)]
        share_spec = pl.BlockSpec
        mixed, middle, normed, final, hidden, up_low, ff_sum, mid_sum = ([] for _ in range(8))
        for ch in range(CHUNKS):
            keep, send = call(
                functools.partial(mix_kernel, groups, cw, imgs, step, lat, share),
                (count,),
                attn_specs(ch),
                row_sends,
                row_outs,
                [pltpu.VMEM((imgs, lat, heads_w), F32)],
                ids,
                [q, kv, lse],
                8 * attn_macs / CHUNKS,
                f"mix{ch}",
            )
            recv = [to_head(send[s - 1], s) for s in range(groups - 1, 0, -1)]
            lat_spec = share_spec(
                (part, None, share, width), lambda i, ids, ch=ch: (ch, ids[0], 0, 0)
            )
            outs = call(
                functools.partial(middle_kernel, groups, cw),
                (1,),
                [whole(keep)]
                + [whole(r) for r in recv]
                + [lat_spec, whole(w_attn), whole(gains[4]), whole(gains[5])],
                [rows_of(own, heads_w), rows_of(own, width), rows_of(own, width)],
                [struct((own, heads_w), BF), struct((own, width), F32), struct((own, width), BF)],
                [],
                ids,
                [keep] + recv + [lat4, w_attn, gains[4], gains[5]],
                2 * own * heads_w * width,
                f"middle{ch}",
            )
            mixed.append(outs[0])
            middle.append(outs[1])
            normed.append(
                jnp.concatenate([outs[2]] + [from_head(outs[2], s) for s in range(1, groups)])
            )
            final.append(final4[:, ch * part : (ch + 1) * part].reshape(groups * own, width))
        block = min(512, units)
        full = groups * own
        for ch in range(CHUNKS):
            outs = call(
                forward_kernel,
                (units // block,),
                [
                    whole(normed[ch]),
                    whole(final[ch]),
                    pl.BlockSpec((width, block), lambda i, ids: (0, i)),
                    pl.BlockSpec((width, block), lambda i, ids: (0, i + units // block)),
                ],
                [
                    pl.BlockSpec((full, block), lambda i, ids: (0, i)),
                    pl.BlockSpec((full, block), lambda i, ids: (0, i)),
                    pl.BlockSpec((full, width), lambda i, ids: (0, 0)),
                    pl.BlockSpec((full, width), lambda i, ids: (0, 0)),
                ],
                [
                    struct((full, units), BF),
                    struct((full, units), BF),
                    struct((full, width), BF),
                    struct((full, width), BF),
                ],
                [pltpu.VMEM((full, width), F32)] * 2,
                ids,
                [normed[ch], final[ch], w_ff, w_ff],
                8 * full * width * units,
                f"feed_forward{ch}",
            )
            hidden.append(outs[0])
            up_low.append(outs[1])
            for total, terms in ((outs[2], ff_sum), (outs[3], mid_sum)):
                total = total.reshape(groups, own, width)
                terms.append(
                    [total[0]] + [to_head(total[s], s) for s in range(groups - 1, 0, -1)]
                )

        down_parts = weight_grad(ids, final, hidden, rows, block, "grad_down")
        up_parts = weight_grad(ids, normed, up_low, rows, block, "grad_up")

        mid_low, grad_mid, gain_terms, grad_mixed = [], [], [], []
        for ch in range(CHUNKS):
            outs = call(
                functools.partial(middle_back_kernel, groups, cw),
                (1,),
                [whole(t) for t in mid_sum[ch]]
                + [whole(middle[ch]), pl.BlockSpec((own, width), lambda i, ids: (0, 0))]
                + [whole(w_attn), whole(gains[4])],
                [
                    rows_of(own, width),
                    rows_of(own, width),
                    rows_of(own, heads_w),
                    pl.BlockSpec((2, width), lambda i, ids: (0, 0)),
                ],
                [
                    struct((own, width), F32),
                    struct((own, width), BF),
                    struct((own, heads_w), BF),
                    struct((2, width), F32),
                ],
                [],
                ids,
                mid_sum[ch] + [middle[ch], final[ch], w_attn, gains[4]],
                2 * own * heads_w * width,
                f"middle_back{ch}",
            )
            grad_mid.append(outs[0])
            mid_low.append(outs[1])
            grad_mixed.append([outs[2]] + [from_head(outs[2], s) for s in range(1, groups)])
            gain_terms.append(outs[3])
        out_parts = weight_grad(ids, mid_low, mixed, rows, heads_w, "grad_attn_out")

        grad_all, delta = [], []
        for ch in range(CHUNKS):
            outs = call(
                functools.partial(back_probs_kernel, groups, cw, imgs, step, lat, share),
                (count,),
                attn_specs(ch) + [rows_of(imgs * share, heads_w)] * groups,
                [
                    rows_of(imgs * lat, heads_w),
                    pl.BlockSpec((imgs, 1, heads_w), lambda i, ids: (i, 0, 0)),
                ],
                [struct((lat_block, heads_w), BF), struct((part, 1, heads_w), F32)],
                [pltpu.VMEM((imgs, lat, heads_w), F32)],
                ids,
                [q, kv, lse] + grad_mixed[ch],
                8 * attn_macs / CHUNKS,
                f"back_probs{ch}",
            )
            grad_all.append(outs[0])
            total = outs[1]
            for s in range(1, groups):
                total = total + jnp.roll(from_head(outs[1], s), s * cw, axis=2)
            delta.append(total)
        gkv, gq, query_terms = [], [], []
        for ch in range(CHUNKS):
            outs = call(
                functools.partial(back_scores_kernel, groups, cw, imgs, step, lat, share),
                (count,),
                attn_specs(ch)
                + [
                    rows_of(imgs * lat, heads_w),
                    pl.BlockSpec((imgs, 1, heads_w), lambda i, ids: (i, 0, 0)),
                ],
                [rows_of(imgs * step, 2 * heads_w), rows_of(imgs * lat, heads_w)] + row_sends,
                [struct((part * step, 2 * heads_w), BF), struct((lat_block, heads_w), BF)]
                + row_outs,
                [pltpu.VMEM((imgs, lat, heads_w), F32)],
                ids,
                [q, kv, lse, grad_all[ch], delta[ch]],
                20 * attn_macs / CHUNKS,
                f"back_scores{ch}",
            )
            gkv.append(outs[0])
            gq.append(outs[1])
            query_terms.append(
                [outs[2]] + [to_head(outs[3][s - 1], s) for s in range(groups - 1, 0, -1)]
            )
        src_chunks = [src[ch * part * step : (ch + 1) * part * step] for ch in range(CHUNKS)]
        nlat_chunks = [nlat[ch * lat_block : (ch + 1) * lat_block] for ch in range(CHUNKS)]
        kv_parts = weight_grad(ids, src_chunks, gkv, rows, min(512, 2 * heads_w), "grad_keyval")
        q_parts = weight_grad(ids, nlat_chunks, gq, rows, heads_w, "grad_query")

        imgs = min(4, part)
        count = part // imgs
        media_grad, latent_grad = [], []
        for ch in range(CHUNKS):

            def share_rows(size, ch=ch):
                return pl.BlockSpec(
                    (imgs, None, size, width), lambda i, ids, live: (i + ch * count, ids[0], 0, 0)
                )

            def own_rows(block, size):
                return pl.BlockSpec((block, size), lambda i, ids, live: (i, 0))

            def fixed(array):
                zeros = (0,) * array.ndim
                return pl.BlockSpec(array.shape, lambda *_: zeros)

            args = [gkv[ch], w_attn, media4, lat4, cot4] + query_terms[ch]
            args += [grad_mid[ch], gains[0], gains[2]]
            outs = pl.pallas_call(
                functools.partial(source_back_kernel, groups, cw, imgs, patch, share),
                grid_spec=pltpu.PrefetchScalarGridSpec(
                    num_scalar_prefetch=2,
                    grid=(count,),
                    in_specs=[own_rows(imgs * step, 2 * heads_w), fixed(w_attn)]
                    + [share_rows(patch), share_rows(share), share_rows(share)]
                    + [own_rows(imgs * share, heads_w)] * groups
                    + [own_rows(imgs * share, width), fixed(gains[0]), fixed(gains[2])],
                    out_specs=[
                        pl.BlockSpec((imgs, patch, width), lambda i, ids, live: (i, 0, 0)),
                        pl.BlockSpec((imgs, share, width), lambda i, ids, live: (i, 0, 0)),
                        pl.BlockSpec((4, width), lambda i, ids, live: (0, 0)),
                    ],
                ),
                out_shape=[
                    struct((part, patch, width), F32),
                    struct((part, share, width), F32),
                    struct((4, width), F32),
                ],
                compiler_params=pltpu.CompilerParams(
                    vmem_limit_bytes=48 * MIB, dimension_semantics=("arbitrary",)
                ),
                cost_estimate=pl.CostEstimate(
                    flops=2 * part * step * width * 2 * heads_w,
                    bytes_accessed=part * step * width * 8,
                    transcendentals=0,
                ),
                name=f"source_back{ch}",
            )(ids, live[ch * part : (ch + 1) * part], *args)
            media_grad.append(outs[0])
            latent_grad.append(outs[1])
            gain_terms[ch] = jnp.concatenate([outs[2], gain_terms[ch]])

        def pick(block, index):
            return lax.dynamic_index_in_dim(block, index, 0, keepdims=False).astype(F32)

        def scatter_plane(keep, send):
            recv = from_dp(send, cf=1)
            grid = [a.reshape((depth_z, 2) + a.shape[1:]) for a in (keep, recv)]

            def at(yy, zz):
                return sum(pick(pick(a, zz), yy) for a in grid)

            away = jnp.stack([at(1 - y, k) for k in range(depth_z)]).astype(BF)
            near = from_dp(away, yf=1)
            total = at(y, z) + pick(near, z)
            for s in range(1, depth_z):
                block = (at(y, (z + s) % depth_z) + pick(near, (z + s) % depth_z)).astype(BF)
                total = total + from_dp(block, depth_z - s).astype(F32)
            return total

        def scatter_all(keep, send, cols):
            recv = from_dp(send, cf=1)
            grid = [a.reshape((depth_z, 2) + a.shape[1:]) for a in (keep, recv)]

            def at(sx, yy):
                lanes = slice(sx * cols, (sx + 1) * cols)
                return sum(
                    lax.dynamic_index_in_dim(a[..., lanes], yy, 1, keepdims=False).astype(F32)
                    for a in grid
                )

            terms = []
            for sx in range(groups):
                for yf in range(2):
                    if sx or yf:
                        terms.append(plane(at(sx, y ^ yf).astype(BF), sx, yf, True))
            base = at(0, y)

            def sum_at(zz):
                return pick(base, zz) + sum(pick(t, zz) for t in terms)

            total = sum_at(z)
            for s in range(1, depth_z):
                block = sum_at((z + s) % depth_z).astype(BF)
                total = total + from_dp(block, depth_z - s).astype(F32)
            return total

        grad_down = scatter_plane(*down_parts).T
        grad_up = scatter_plane(*up_parts)
        grad_attn = scatter_all(*out_parts, cw).T
        grad_keyval = scatter_all(*kv_parts, 2 * cw).reshape(rows, 2, cw)
        grad_query = scatter_all(*q_parts, cw)

        total = sum(gain_terms)
        total = total + from_dp(total, cf=1)
        around = [total]
        for sx in range(groups):
            for yf in range(2):
                if sx or yf:
                    around.append(plane(total, sx, yf, False))
        total = sum(around)
        norm_grads = total + sum(from_dp(total, s) for s in range(1, depth_z))

        final_lat = jnp.concatenate(
            [
                mid + sum(t.astype(F32) for t in terms)
                for mid, terms in zip(middle, ff_sum)
            ]
        ).reshape(images, share, width)
        lat_own = lax.dynamic_index_in_dim(lat4, me, 1, keepdims=False).astype(F32)
        latents_out = jnp.where(live[:, None, None] > 0, final_lat, lat_own)
        return (
            latents_out,
            jnp.concatenate(media_grad),
            jnp.concatenate(latent_grad),
            grad_query,
            grad_keyval,
            grad_attn,
            grad_up,
            grad_down,
            norm_grads,
        )

    return local


def solution(mesh):
    return jax.shard_map(
        make_local(mesh.shape["dp"] // 4, mesh.shape["head"]),
        mesh=mesh,
        in_specs=(
            P("dp", None, None),
            P("dp", None, None),
            P("dp", None, None),
            P("dp"),
            P(),
            P(),
            P(),
            P(),
            P(),
            P(),
            P("dp", "head"),
            P("dp", None, "head"),
            P("head", "dp"),
            P("dp", "head"),
            P("head", "dp"),
        ),
        out_specs=(
            P("dp", "head", None),
            P("dp", "head", None),
            P("dp", "head", None),
            P("dp", "head"),
            P("dp", None, "head"),
            P("head", "dp"),
            P("dp", "head"),
            P("head", "dp"),
            P(),
        ),
        check_vma=False,
    )
```

```python
import functools

import jax
import jax.numpy as jnp
from jax import lax
from jax.experimental import pallas as pl
from jax.experimental.pallas import tpu as pltpu
from jax.sharding import PartitionSpec as P

HD = 64
HEADS = 8
CHUNKS = 2
EPS = 1e-05
BF = jnp.bfloat16
F32 = jnp.float32
MIB = 1024 * 1024
VMEM = 56
COST = 1
COST = 50

NN = (((1,), (0,)), ((), ()))
NT = (((1,), (1,)), ((), ()))
TN = (((0,), (0,)), ((), ()))


def dot(left, right, form=NN):
    return lax.dot_general(left, right, form, preferred_element_type=F32)


def struct(shape, dtype):
    return jax.ShapeDtypeStruct(shape, dtype)


def call(kernel, grid, in_specs, out_specs, out_shape, scratch, ids, args, flops, name, alias=None):
    scalars = ids if isinstance(ids, (list, tuple)) else [ids]
    moved = sum(a.size * a.dtype.itemsize for a in args if a.ndim < 4)
    moved += sum(o.size * jnp.dtype(o.dtype).itemsize for o in out_shape)
    return pl.pallas_call(
        kernel,
        grid_spec=pltpu.PrefetchScalarGridSpec(
            num_scalar_prefetch=len(scalars),
            grid=grid,
            in_specs=in_specs,
            out_specs=out_specs,
            scratch_shapes=scratch,
        ),
        out_shape=out_shape,
        input_output_aliases={len(scalars) + k: v for k, v in (alias or {}).items()},
        compiler_params=pltpu.CompilerParams(
            vmem_limit_bytes=VMEM * MIB, dimension_semantics=("arbitrary",) * len(grid)
        ),
        cost_estimate=pl.CostEstimate(
            flops=int(flops) // COST, bytes_accessed=int(moved) // COST, transcendentals=0
        ),
        name=name,
    )(*scalars, *args)


def whole(array):
    zeros = (0,) * array.ndim
    return pl.BlockSpec(array.shape, lambda *_: zeros)


def rows_of(block, width, first=0):
    return pl.BlockSpec((block, width), lambda i, *_: (i + first, 0))


def fixed_rows(block, width, at=0):
    return pl.BlockSpec((block, width), lambda *_: (at, 0))


def images_of(block, rows, width, first=0):
    return pl.BlockSpec((block, rows, width), lambda i, *_: (i + first, 0, 0))


def third(array, width, at):
    if width % 128:
        return whole(array)
    return pl.BlockSpec(array.shape[:2] + (width,), lambda *_: (0, 0, at))


def columns(ref, group, width, at):
    if ref.shape[2] == width:
        return ref[group]
    return ref[group, :, at * width : (at + 1) * width]


def anywhere():
    return pl.BlockSpec(memory_space=pl.ANY)


def tie(values, *first):
    flat, tree = jax.tree.flatten(values)
    out = lax.optimization_barrier(tuple(flat) + tuple(jax.tree.leaves(first)))
    return jax.tree.unflatten(tree, out[: len(flat)])


def norm_parts(values):
    centre = values - jnp.mean(values, axis=-1, keepdims=True)
    rstd = lax.rsqrt(jnp.mean(centre * centre, axis=-1, keepdims=True) + EPS)
    return centre * rstd, rstd


def norm_back(values, gain, grad):
    xhat, rstd = norm_parts(values)
    scaled = grad * gain
    first = jnp.mean(scaled, axis=-1, keepdims=True)
    second = jnp.mean(scaled * xhat, axis=-1, keepdims=True)
    return rstd * (scaled - first - xhat * second), grad * xhat


def fold_rows(value):
    return jnp.sum(value.reshape(value.shape[0] // 8, 8, value.shape[1]), axis=0)


def norm_kernel(
    imgs, lat, share, patch, ids, media, latents, m_gain, m_bias, l_gain, l_bias, src, nlat, keep
):
    start = pl.multiple_of(ids[0] * share, share)
    step = patch + share
    for i in range(imgs):
        xhat, _ = norm_parts(media[i].astype(F32))
        src[i * step : i * step + patch, :] = (xhat * m_gain[...] + m_bias[...]).astype(BF)
        xhat, _ = norm_parts(latents[i].astype(F32))
        normed = xhat * l_gain[...] + l_bias[...]
        nlat[i * lat : (i + 1) * lat, :] = normed.astype(BF)
        keep[...] = normed
        src[i * step + patch : (i + 1) * step, :] = keep[pl.ds(start, share), :].astype(BF)


def assemble(entries, pieces, depth, ids, rows, groups, width, name):
    def kernel(ids_ref, *refs):
        out, sems = refs[len(pieces)], refs[len(pieces) + 1]
        copies = []
        for e, (op, lead, group, s, yf, cf) in enumerate(entries):
            block = lax.rem(ids_ref[1] + s, depth) * 4
            block += lax.rem(ids_ref[2] + yf, 2) * 2 + lax.rem(ids_ref[3] + cf, 2)
            start = pl.multiple_of(block * rows, rows)
            source = refs[op] if lead is None else refs[op].at[lead]
            copies.append(
                pltpu.make_async_copy(source, out.at[group, pl.ds(start, rows), :], sems.at[e])
            )
        for copy in copies:
            copy.start()
        for copy in copies:
            copy.wait()

    return call(
        kernel,
        (1,),
        [anywhere()] * len(pieces),
        [pl.BlockSpec((groups, depth * 4 * rows, width), lambda *_: (0, 0, 0))],
        [struct((groups, depth * 4 * rows, width), BF)],
        [pltpu.SemaphoreType.DMA((len(entries),))],
        ids,
        pieces,
        0,
        name,
    )[0]


def diag_mask(heads, width, dtype):
    row = lax.broadcasted_iota(jnp.int32, (heads * HD, width), 0) // HD
    col = lax.broadcasted_iota(jnp.int32, (heads * HD, width), 1) // HD
    return jnp.where(row == col, 1.0, 0.0).astype(dtype)


def spread(block, heads, mask):
    return jnp.concatenate([block] * heads, axis=0) * mask


def fold(full, heads, lat, mask):
    full = full * mask
    total = full[:lat]
    for h in range(1, heads):
        total = total + full[h * lat : (h + 1) * lat]
    return total


def lane_roll(values, s, groups, cw):
    if s == 0:
        return values
    if cw % 128 == 0:
        cut = (groups - s) * cw
        return jnp.concatenate([values[:, cut:], values[:, :cut]], axis=1)
    return pltpu.roll(values, s * cw, 1)


def project_kernel(groups, cw, imgs, step, lat, ids, src, nlat, w, q, k, stats):
    heads = cw // HD
    for j in range(groups):
        k[:, j * cw : (j + 1) * cw] = dot(src[...], w[j, :, cw:]).astype(BF)
        q[:, j * cw : (j + 1) * cw] = (dot(nlat[...], w[j, :, :cw]) * (HD**-0.5)).astype(BF)
    mask = diag_mask(heads, cw, BF)
    for i in range(imgs):
        for j in range(groups):
            cols = slice(j * cw, (j + 1) * cw)
            qbd = spread(q[i * lat : (i + 1) * lat, cols], heads, mask)
            score = dot(k[i * step : (i + 1) * step, cols], qbd, NT)
            top = jnp.max(score, axis=0, keepdims=True)
            stats[i, 0:1, cols] = top
            stats[i, 1:2, cols] = jnp.sum(jnp.exp(score - top), axis=0, keepdims=True)


def values_kernel(groups, cw, ids, src, w, v):
    for j in range(groups):
        v[:, j * cw : (j + 1) * cw] = dot(src[...], columns(w, j, cw, 0)).astype(BF)


def send_rows(groups, share, ids, scratch, i, keep, send):
    for s in range(groups):
        start = pl.multiple_of(lax.rem(ids[0] + s, groups) * share, share)
        rows = scratch[pl.ds(start, share), :]
        if s == 0:
            keep[i * share : (i + 1) * share, :] = rows
        else:
            send[s - 1, i * share : (i + 1) * share, :] = rows.astype(BF)


def mix_kernel(groups, cw, imgs, step, lat, share, ids, q, k, v, lse, keep, send, scratch):
    heads = cw // HD
    mask, fmask = diag_mask(heads, cw, BF), diag_mask(heads, cw, F32)
    for i in range(imgs):
        rows = slice(i * step, (i + 1) * step)
        for j in range(groups):
            cols = slice(j * cw, (j + 1) * cw)
            qbd = spread(q[i * lat : (i + 1) * lat, cols], heads, mask)
            probs = jnp.exp(dot(k[rows, cols], qbd, NT) - lse[i, 0:1, cols])
            full = dot(probs.astype(BF), v[rows, cols], TN)
            scratch[i, :, cols] = fold(full, heads, lat, fmask)
        send_rows(groups, share, ids, scratch.at[i], i, keep, send)


def back_probs_kernel(groups, cw, imgs, step, lat, share, first, ids, q, k, v, lse, grad_keep, *refs):
    recv, refs = refs[: groups - 1], refs[groups - 1 :]
    gv, grad_all, delta, scratch = refs if first else refs[1:]
    heads = cw // HD
    mask = diag_mask(heads, cw, BF)
    for i in range(imgs):
        for s in range(groups):
            start = pl.multiple_of(lax.rem(ids[0] + s, groups) * share, share)
            block = grad_keep if s == 0 else recv[s - 1]
            block = lane_roll(block[i * share : (i + 1) * share, :].astype(F32), s, groups, cw)
            scratch[i, pl.ds(start, share), :] = block
        grad_all[i * lat : (i + 1) * lat, :] = scratch[i].astype(BF)
        rows = slice(i * step, (i + 1) * step)
        for j in range(groups):
            cols = slice(j * cw, (j + 1) * cw)
            qbd = spread(q[i * lat : (i + 1) * lat, cols], heads, mask)
            gbd = spread(grad_all[i * lat : (i + 1) * lat, cols], heads, mask)
            probs = jnp.exp(dot(k[rows, cols], qbd, NT) - lse[i, 0:1, cols])
            delta[i, 0:1, cols] = jnp.sum(probs * dot(v[rows, cols], gbd, NT), axis=0, keepdims=True)
            gv[rows, cols] = dot(probs.astype(BF), gbd).astype(BF)


def back_scores_kernel(
    groups, cw, imgs, step, lat, share, first, ids, q, k, v, lse, grad_all, delta, *refs
):
    gk, gq, keep, send, scratch = refs if first else refs[2:]
    heads = cw // HD
    mask, fmask = diag_mask(heads, cw, BF), diag_mask(heads, cw, F32)
    for i in range(imgs):
        rows = slice(i * step, (i + 1) * step)
        for j in range(groups):
            cols = slice(j * cw, (j + 1) * cw)
            qbd = spread(q[i * lat : (i + 1) * lat, cols], heads, mask)
            gbd = spread(grad_all[i * lat : (i + 1) * lat, cols], heads, mask)
            probs = jnp.exp(dot(k[rows, cols], qbd, NT) - lse[i, 0:1, cols])
            grad = dot(v[rows, cols], gbd, NT) - delta[i, 0:1, cols]
            grad = (probs * grad).astype(BF)
            gk[rows, cols] = dot(grad, qbd).astype(BF)
            full = dot(grad, k[rows, cols], TN)
            scratch[i, :, cols] = fold(full, heads, lat, fmask) * (HD**-0.5)
        gq[i * lat : (i + 1) * lat, :] = scratch[i].astype(BF)
        send_rows(groups, share, ids, scratch.at[i], i, keep, send)


def middle_kernel(groups, cw, ids, keep, *refs):
    recv = refs[: groups - 1]
    latents, w, gain, bias, mixed, middle, normed = refs[groups - 1 :]
    total = keep[...]
    for s in range(1, groups):
        total = total + lane_roll(recv[s - 1][...].astype(F32), s, groups, cw)
    low = total.astype(BF)
    mixed[...] = low
    value = latents[...].astype(F32).reshape(middle.shape)
    for j in range(groups):
        value = value + dot(low[:, j * cw : (j + 1) * cw], columns(w, j, cw, 1), NT)
    middle[...] = value
    xhat, _ = norm_parts(value)
    normed[...] = (xhat * gain[...] + bias[...]).astype(BF)


def gelu_parts(value):
    cdf = 0.5 * (1.0 + lax.erf(value * (0.5**0.5)))
    pdf = jnp.exp(value * value * -0.5) * 0.3989422804014327
    return value * cdf, cdf + value * pdf


def forward_kernel(terms, ids, *refs):
    normed, final = refs[:terms], refs[terms : 2 * terms]
    up, down, hidden, up_low, ff, mid, normed_all, final_all, ff_total, mid_total = refs[2 * terms :]
    step = pl.program_id(0)

    @pl.when(step == 0)
    def _():
        at = 0
        for left, right in zip(normed, final):
            normed_all[at : at + left.shape[0], :] = left[...]
            final_all[at : at + left.shape[0], :] = right[...]
            at += left.shape[0]

    act, slope = gelu_parts(dot(normed_all[...], up[...]))
    low = act.astype(BF)
    hidden[...] = low
    ff_part = dot(low, down[...], NT)
    low = (dot(final_all[...], down[...]) * slope).astype(BF)
    up_low[...] = low
    mid_part = dot(low, up[...], NT)
    last = pl.num_programs(0) - 1

    @pl.when(step == 0)
    def _():
        ff_total[...] = ff_part
        mid_total[...] = mid_part

    @pl.when(step > 0)
    def _():
        ff_total[...] += ff_part
        mid_total[...] += mid_part

    @pl.when(step == last)
    def _():
        ff[...] = ff_total[...].astype(BF)
        mid[...] = mid_total[...].astype(BF)


def middle_back_kernel(groups, cw, ids, part, *refs):
    recv = refs[: groups - 1]
    middle, final, w, gain, grad_mid, mid_low, grad_mixed, gains = refs[groups - 1 :]
    total = part[...].astype(F32)
    for other in recv:
        total = total + other[...].astype(F32)
    back, terms = norm_back(middle[...], gain[...], total)
    gains[0:1, :] = jnp.sum(terms, axis=0, keepdims=True)
    gains[1:2, :] = jnp.sum(total, axis=0, keepdims=True)
    value = final[...].astype(F32) + back
    grad_mid[...] = value
    low = value.astype(BF)
    mid_low[...] = low
    for j in range(groups):
        grad_mixed[:, j * cw : (j + 1) * cw] = dot(low, columns(w, j, cw, 1)).astype(BF)


def weight_grad_kernel(plan, rows, split, ids, *refs):
    count = sum(n + m for n, m, _ in plan)
    if split:
        keep, send, total, turned = refs[count:]
    else:
        out, turned = refs[count:]
    first = step = 0
    for n, m, steps in plan:
        left, right = refs[first : first + n], refs[first + n : first + n + m]
        first += n + m
        size = sum(a.shape[0] for a in left)

        @pl.when(pl.program_id(0) == step)
        def _(left=left):
            at = 0
            for a in left:
                turned[:, at : at + a.shape[0]] = a[...].T
                at += a.shape[0]

        @pl.when((pl.program_id(0) >= step) & (pl.program_id(0) < step + steps))
        def _(right=right):
            at, value = 0, None
            for a in right:
                term = dot(turned[:, at : at + a.shape[0]], a[...])
                value = term if value is None else value + term
                at += a.shape[0]
            if split:
                total[...] = value
            else:
                out[...] = value.astype(BF)

        step += steps
    if not split:
        return
    for b in range(keep.shape[0]):
        for ref, core in ((keep, ids[3]), (send, 1 - ids[3])):
            start = pl.multiple_of((b * 2 + core) * rows, rows)
            ref[b] = total[pl.ds(start, rows), :].astype(BF)


def weight_grad(ids, results, rows, depth, block, name, split=True):
    plan, specs, args, step, most, flops = [], [], [], 0, 0, 0
    for left, right in results:
        width = right[0][0].shape[1]
        steps = width // block
        size = 0
        for array, spec in left:
            args.append(array)
            specs.append(spec)
        for array, count, at in right:

            def place(i, *_, at=at, step=step, steps=steps):
                return at, jnp.clip(i - step, 0, steps - 1)

            args.append(array)
            specs.append(pl.BlockSpec((count, block), place))
            size += count
        plan.append((len(left), len(right), steps))
        step += steps
        most = max(most, size)
        flops += 2 * size * depth * width
    blocks = depth // rows // 2
    turned = pltpu.VMEM((depth, most), BF)
    if split:
        outs = [struct((blocks, rows, step * block), BF)] * 2
        out_specs = [pl.BlockSpec((blocks, rows, block), lambda i, *_: (0, 0, i))] * 2
        scratch = [pltpu.VMEM((depth, block), F32), turned]
    else:
        outs = [struct((depth, step * block), BF)]
        out_specs = [pl.BlockSpec((depth, block), lambda i, *_: (0, i))]
        scratch = [turned]
    return call(
        functools.partial(weight_grad_kernel, plan, rows, split),
        (step,),
        specs,
        out_specs,
        outs,
        scratch,
        ids,
        args,
        flops,
        name,
    )


def source_back_kernel(
    groups, cw, imgs, patch, share, first, ids, live, gk, gv, wk, wv, media, latents, cot, keep, *refs
):
    recv, refs = refs[: groups - 1], refs[groups - 1 :]
    grad_mid, m_gain, l_gain = refs[:3]
    refs = refs[3:] if first == 0 else refs[5:]
    media_grad, latent_grad, gains, total, lat_total, query = refs
    base = (pl.program_id(0) + first) * imgs
    step = patch + share
    value = dot(gk[:, :cw], wk[0, :, cw:], NT) + dot(gv[:, :cw], columns(wv, 0, cw, 0), NT)
    for j in range(1, groups):
        cols = slice(j * cw, (j + 1) * cw)
        value = value + dot(gk[:, cols], wk[j, :, cw:], NT)
        value = value + dot(gv[:, cols], columns(wv, j, cw, 0), NT)
    total[...] = value
    asked = keep[...]
    for s in range(1, groups):
        asked = asked + lane_roll(recv[s - 1][...].astype(F32), s, groups, cw)
    query[...] = asked.astype(BF)
    value = dot(query[:, :cw], wk[0, :, :cw], NT)
    for j in range(1, groups):
        value = value + dot(query[:, j * cw : (j + 1) * cw], wk[j, :, :cw], NT)
    lat_total[...] = value

    @pl.when(pl.program_id(0) == 0)
    def _():
        gains[...] = jnp.zeros_like(gains)

    sums = [0.0] * 4
    for i in range(imgs):
        grad = total[i * step : i * step + patch, :]
        back, terms = norm_back(media[i].astype(F32), m_gain[...], grad)
        media_grad[i] = back
        sums[0] += fold_rows(terms)
        sums[1] += fold_rows(grad)
        rows = slice(i * share, (i + 1) * share)
        grad = total[i * step + patch : (i + 1) * step, :] + lat_total[rows, :]
        back, terms = norm_back(latents[i].astype(F32), l_gain[...], grad)
        sums[2] += fold_rows(terms)
        sums[3] += fold_rows(grad)
        latent_grad[i] = jnp.where(
            live[base + i] > 0, grad_mid[rows, :] + back, cot[i].astype(F32)
        )
    for k in range(4):
        gains[k : k + 1, :] += jnp.sum(sums[k], axis=0, keepdims=True)


def make_local(depth_z, groups):
    dp_size = depth_z * 4

    def from_dp(value, s=0, yf=0, cf=0):
        pairs = []
        for dst in range(dp_size):
            z, y, c = dst // 4, dst // 2 % 2, dst % 2
            pairs.append(((z + s) % depth_z * 4 + (y ^ yf) * 2 + (c ^ cf), dst))
        return lax.ppermute(value, "dp", pairs)

    def from_head(value, s):
        return lax.ppermute(value, "head", [((x + s) % groups, x) for x in range(groups)])

    def to_head(value, s):
        return lax.ppermute(value, "head", [(x, (x + s) % groups) for x in range(groups)])

    def plane(value, sx, yf, back, cf=0):
        pairs = []
        for dst in range(dp_size):
            for x in range(groups):
                other = (dst ^ (2 * yf + cf)) * groups + (x + sx) % groups
                mine = dst * groups + x
                pairs.append((mine, other) if back else (other, mine))
        return lax.ppermute(value, ("dp", "head"), pairs)

    others = [(sx, yf) for sx in range(groups) for yf in range(2) if sx or yf]

    def local(
        media_tokens,
        latents,
        cotangent,
        image_counts,
        media_gain,
        media_bias,
        latent_gain,
        latent_bias,
        ff_gain,
        ff_bias,
        w_query,
        w_keyval,
        w_attn_out,
        w_up,
        w_down,
    ):
        images, patches, width = media_tokens.shape
        lat = latents.shape[1]
        rows, cw = w_query.shape
        units = w_up.shape[1]
        patch, share = patches // groups, lat // groups
        step = patch + share
        heads_w = cw * groups
        me = lax.axis_index("head").astype(jnp.int32)
        place = lax.axis_index("dp").astype(jnp.int32)
        z, y, c = place // 4, place // 2 % 2, place % 2
        ids = jnp.stack([me, z, y, c])
        live = (jnp.arange(images, dtype=jnp.int32) < jnp.sum(image_counts)).astype(jnp.int32)
        gains = [
            g.reshape(1, width)
            for g in (media_gain, media_bias, latent_gain, latent_bias, ff_gain, ff_bias)
        ]
        media4 = media_tokens.reshape(images, groups, patch, width)
        lat4 = latents.reshape(images, groups, share, width)
        cot4 = cotangent.reshape(images, groups, share, width)

        shard_qk = jnp.concatenate([w_query, w_keyval[:, 0]], axis=1)
        shard_vo = jnp.concatenate([w_keyval[:, 1], w_attn_out.T], axis=1)
        got_qk = [from_dp(shard_qk, s) for s in range(1, depth_z)]
        shard_vo = tie(shard_vo, shard_qk)
        got_vo = [from_dp(shard_vo, s) for s in range(1, depth_z)]
        w_up_all = lax.all_gather(w_up, "dp", axis=0, tiled=True)
        w_down_all = lax.all_gather(w_down.T, "dp", axis=0, tiled=True)

        def spread_line(line):
            return {(0, 0): line} | {at: plane(line, *at, False) for at in others}

        def cores(parts):
            pieces, entries = [], []
            for (sx, yf), part in parts.items():
                for cf, piece in ((0, part), (1, from_dp(part, cf=1))):
                    for s in range(depth_z):
                        entries.append((len(pieces), s, sx, s, yf, cf))
                    pieces.append(piece)
            return entries, pieces

        line_qk = jnp.stack([shard_qk] + got_qk)
        parts_qk = spread_line(line_qk)
        imgs = 2
        src, nlat = call(
            functools.partial(norm_kernel, imgs, lat, share, patch),
            (images // imgs,),
            [
                pl.BlockSpec((imgs, None, patch, width), lambda i, ids: (i, ids[0], 0, 0)),
                images_of(imgs, lat, width),
            ]
            + [whole(gains[0])] * 4,
            [rows_of(imgs * step, width), rows_of(imgs * lat, width)],
            [struct((images * step, width), BF), struct((images * lat, width), BF)],
            [pltpu.VMEM((lat, width), F32)],
            tie(ids, line_qk),
            [media4, latents] + gains[:4],
            images * step * width * 12,
            "input_norms",
        )

        line_vo = jnp.stack([shard_vo] + tie(got_vo, line_qk))
        parts_vo = spread_line(line_vo)
        w_qk = assemble(*cores(parts_qk), depth_z, ids, rows, groups, 2 * cw, "place_qk")
        final4 = jnp.stack(
            [
                lax.dynamic_index_in_dim(cot4, (me + s) % groups, 1, keepdims=False)
                for s in range(groups)
            ]
        ) * live.astype(BF).reshape(1, images, 1, 1)
        final4 = final4.reshape(groups, images * share, width)

        imgs = 4
        attn_macs = images * step * lat * heads_w
        q, k, stats = call(
            functools.partial(project_kernel, groups, cw, imgs, step, lat),
            (images // imgs,),
            [rows_of(imgs * step, width), rows_of(imgs * lat, width), whole(w_qk)],
            [
                rows_of(imgs * lat, heads_w),
                rows_of(imgs * step, heads_w),
                images_of(imgs, 2, heads_w),
            ],
            [
                struct((images * lat, heads_w), BF),
                struct((images * step, heads_w), BF),
                struct((images, 2, heads_w), F32),
            ],
            [],
            ids,
            [src, nlat, w_qk],
            2 * images * (step * width * heads_w + lat * width * heads_w) + 8 * attn_macs,
            "project",
        )
        tops, sums = [stats[:, :1]], [stats[:, 1:]]
        for s in range(1, groups):
            other = jnp.roll(from_head(stats, s), s * cw, axis=2)
            tops.append(other[:, :1])
            sums.append(other[:, 1:])
        w_vo = assemble(*cores(parts_vo), depth_z, tie(ids, q), rows, groups, 2 * cw, "place_vo")
        v = call(
            functools.partial(values_kernel, groups, cw),
            (images // imgs,),
            [rows_of(imgs * step, width), third(w_vo, cw, 0)],
            [rows_of(imgs * step, heads_w)],
            [struct((images * step, heads_w), BF)],
            [],
            ids,
            [src, w_vo],
            2 * images * step * width * heads_w,
            "values",
        )[0]
        top = functools.reduce(jnp.maximum, tops)
        lse = top + jnp.log(sum(t * jnp.exp(m - top) for m, t in zip(tops, sums)))

        part = images // CHUNKS
        imgs = min(imgs, part)
        count = part // imgs
        own = part * share

        def attn_specs(ch):
            return [
                rows_of(imgs * lat, heads_w, ch * count),
                rows_of(imgs * step, heads_w, ch * count),
                rows_of(imgs * step, heads_w, ch * count),
                images_of(imgs, 1, heads_w, ch * count),
            ]

        row_sends = [
            rows_of(imgs * share, heads_w),
            pl.BlockSpec((groups - 1, imgs * share, heads_w), lambda i, ids: (0, i, 0)),
        ]
        row_outs = [struct((own, heads_w), F32), struct((groups - 1, own, heads_w), BF)]

        def exchanged(keep, send):
            return [keep] + [to_head(send[s - 1], s) for s in range(groups - 1, 0, -1)]

        mixes, mixed, middle, normed = [], [], [], []
        for ch in range(CHUNKS):
            keep, send = call(
                functools.partial(mix_kernel, groups, cw, imgs, step, lat, share),
                (count,),
                attn_specs(ch),
                row_sends,
                row_outs,
                [pltpu.VMEM((imgs, lat, heads_w), F32)],
                tie(ids, [a[0] for a in mixes]),
                [q, k, v, lse],
                8 * attn_macs / CHUNKS,
                f"mix{ch}",
            )
            mixes.append(exchanged(keep, send))
        for ch in range(CHUNKS):
            lat_spec = pl.BlockSpec(
                (part, None, share, width), lambda i, ids, ch=ch: (ch, ids[0], 0, 0)
            )
            outs = call(
                functools.partial(middle_kernel, groups, cw),
                (1,),
                [whole(a) for a in mixes[ch]]
                + [lat_spec, third(w_vo, cw, 1), whole(gains[4]), whole(gains[5])],
                [fixed_rows(own, heads_w), fixed_rows(own, width), fixed_rows(own, width)],
                [struct((own, heads_w), BF), struct((own, width), F32), struct((own, width), BF)],
                [],
                tie(ids, [a[0] for a in normed]),
                mixes[ch] + [lat4, w_vo, gains[4], gains[5]],
                2 * own * heads_w * width,
                f"middle{ch}",
            )
            mixed.append(outs[0])
            middle.append(outs[1])
            normed.append([outs[2]] + [from_head(outs[2], s) for s in range(1, groups)])
        block = min(512, units)

        def feed_forward(terms, ids, name):
            size = len(terms) * own
            return call(
                functools.partial(forward_kernel, len(terms)),
                (units // block,),
                [whole(a) for a, _ in terms]
                + [spec for _, spec in terms]
                + [
                    pl.BlockSpec((width, block), lambda i, ids: (0, i)),
                    pl.BlockSpec((width, block), lambda i, ids: (0, i)),
                ],
                [pl.BlockSpec((size, block), lambda i, ids: (0, i))] * 2
                + [fixed_rows(size, width)] * 2,
                [struct((size, units), BF)] * 2 + [struct((size, width), BF)] * 2,
                [pltpu.VMEM((size, width), BF)] * 2 + [pltpu.VMEM((size, width), F32)] * 2,
                ids,
                [a for a, _ in terms] + [final4] * len(terms) + [w_up_all, w_down_all],
                8 * size * width * units,
                name,
            )

        def final_rows(s, ch):
            return pl.BlockSpec((None, own, width), lambda *_: (s, ch, 0))

        own_ff = feed_forward(
            [(normed[ch][0], final_rows(0, ch)) for ch in range(CHUNKS)],
            tie(ids, normed[-1][0]),
            "feed_forward_own",
        )
        away_ff, ff_back, mid_back = [], [], []
        for ch in range(CHUNKS):
            outs = feed_forward(
                [(normed[ch][s], final_rows(s, ch)) for s in range(1, groups)],
                tie(ids, (away_ff or [own_ff])[-1]),
                f"feed_forward_away{ch}",
            )
            away_ff.append(outs[:2])
            sends = [a.reshape(groups - 1, own, width) for a in outs[2:]]
            mid_back.append(
                [to_head(sends[1][s - 1], s) for s in range(groups - 1, 0, -1)]
            )
            ff_back.append(sends[0])

        def ff_terms(lefts, which):
            rights = [(own_ff[which], CHUNKS * own, 0)]
            rights += [(a[which], (groups - 1) * own, 0) for a in away_ff]
            return [(lefts, rights)]

        finals = [(final4, pl.BlockSpec((None, CHUNKS * own, width), lambda *_: (0, 0, 0)))]
        finals += [(final4, final_rows(s, ch)) for ch in range(CHUNKS) for s in range(1, groups)]
        norms = [normed[ch][0] for ch in range(CHUNKS)]
        norms += [normed[ch][s] for ch in range(CHUNKS) for s in range(1, groups)]
        norms = [(a, whole(a)) for a in norms]
        down_part = weight_grad(
            tie(ids, away_ff), ff_terms(finals, 0), rows, width, block, "grad_down", False
        )[0]
        up_part = weight_grad(
            tie(ids, down_part), ff_terms(norms, 1), rows, width, block, "grad_up", False
        )[0]
        grad_down = lax.psum_scatter(down_part, "dp", scatter_dimension=0, tiled=True)
        grad_up = lax.psum_scatter(up_part, "dp", scatter_dimension=0, tiled=True)
        ff_back = tie(ff_back, mid_back)
        ff_back = [[to_head(a[s - 1], s) for s in range(groups - 1, 0, -1)] for a in ff_back]

        def pick(block, index, axis=0):
            return lax.dynamic_index_in_dim(block, index, axis, keepdims=False).astype(F32)

        def lanes(block, cols):
            if len(cols) == 1 and cols[0] == slice(0, block.shape[-1]):
                return block
            return jnp.concatenate([block[..., c] for c in cols], axis=-1)

        class Sum:
            def __init__(self, parts, cols):
                self.cols = cols
                self.routes = others
                self.grid = [a.reshape((depth_z, 2) + a.shape[1:]) for a in (parts[0], from_dp(parts[1], cf=1))]

            def at(self, sx, yy):
                return sum(pick(lanes(a, self.cols[sx]), yy, 1) for a in self.grid)

            def second(self):
                self.away = [self.at(sx, y ^ yf).astype(BF) for sx, yf in self.routes]
                return self.away

            def sent(self):
                self.near = [plane(a, *to, True) for a, to in zip(self.away, self.routes)]

            def third(self):
                base = self.at(0, y)

                def block(zz):
                    return pick(base, zz) + sum(pick(a, zz) for a in self.near)

                self.mine = block
                self.away = [block((z + s) % depth_z).astype(BF) for s in range(1, depth_z)]
                return self.away

            def last(self, late=()):
                got = [from_dp(a, depth_z - s) for s, a in zip(range(1, depth_z), self.away)]
                got = tie(got, late)
                return self.mine(z) + sum(a.astype(F32) for a in got)

        def groups_of(*starts):
            return [[slice(a + sx * cw, a + (sx + 1) * cw) for a in starts] for sx in range(groups)]

        grad_mid, mid_low, gain_terms, grad_mixed = [], [], [], []
        for ch in range(CHUNKS):
            outs = call(
                functools.partial(middle_back_kernel, groups, cw),
                (1,),
                [fixed_rows(own, width, ch)]
                + [whole(t) for t in mid_back[ch]]
                + [whole(middle[ch]), final_rows(0, ch), third(w_vo, cw, 1), whole(gains[4])],
                [
                    fixed_rows(own, width),
                    fixed_rows(own, width),
                    fixed_rows(own, heads_w),
                    fixed_rows(2, width),
                ],
                [
                    struct((own, width), F32),
                    struct((own, width), BF),
                    struct((own, heads_w), BF),
                    struct((2, width), F32),
                ],
                [],
                tie(ids, up_part, mid_low),
                [own_ff[3]] + mid_back[ch] + [middle[ch], final4, w_vo, gains[4]],
                2 * own * heads_w * width,
                f"middle_back{ch}",
            )
            grad_mid.append(outs[0])
            mid_low.append(outs[1])
            grad_mixed.append([outs[2]] + [from_head(outs[2], s) for s in range(1, groups)])
            gain_terms.append(outs[3])
        whole_of = lambda arrays: [(a, whole(a)) for a in arrays]
        full_of = lambda arrays: [(a, a.shape[0], 0) for a in arrays]
        out_parts = weight_grad(
            tie(ids, mid_low), [(whole_of(mid_low), full_of(mixed))], rows, width, heads_w, "grad_attn_out"
        )
        sum_out = Sum(out_parts, groups_of(0))

        grad_all, delta, gv = [], [], None
        for ch in range(CHUNKS):
            first = gv is None
            before = [out_parts[0]] if first else sum_out.second()
            outs = call(
                functools.partial(back_probs_kernel, groups, cw, imgs, step, lat, share, first),
                (count,),
                attn_specs(ch)
                + [rows_of(imgs * share, heads_w)] * groups
                + ([] if first else [anywhere()]),
                [
                    rows_of(imgs * step, heads_w, ch * count),
                    rows_of(imgs * lat, heads_w),
                    images_of(imgs, 1, heads_w),
                ],
                [
                    struct((images * step, heads_w), BF),
                    struct((part * lat, heads_w), BF),
                    struct((part, 1, heads_w), F32),
                ],
                [pltpu.VMEM((imgs, lat, heads_w), F32)],
                tie(ids, before),
                [q, k, v, lse] + grad_mixed[ch] + ([] if first else [gv]),
                12 * attn_macs / CHUNKS,
                f"back_probs{ch}",
                None if first else {4 + groups: 0},
            )
            gv = outs[0]
            grad_all.append(outs[1])
            delta.append([outs[2]] + [from_head(outs[2], s) for s in range(1, groups)])
        sum_out.sent()
        source = lambda block: [(src, whole(src))]
        value_parts = weight_grad(
            tie(ids, gv), [(source(src), [(gv, images * step, 0)])], rows, width, heads_w, "grad_values"
        )
        sum_value = Sum(value_parts, groups_of(0))
        gk = gq = None
        query_terms = []
        for ch in range(CHUNKS):
            first = gk is None
            total = sum(jnp.roll(a, s * cw, axis=2) for s, a in enumerate(delta[ch]))
            before = [value_parts[0]] if first else [gk, sum_value.second()]
            outs = call(
                functools.partial(back_scores_kernel, groups, cw, imgs, step, lat, share, first),
                (count,),
                attn_specs(ch)
                + [rows_of(imgs * lat, heads_w), images_of(imgs, 1, heads_w)]
                + ([] if first else [anywhere()] * 2),
                [
                    rows_of(imgs * step, heads_w, ch * count),
                    rows_of(imgs * lat, heads_w, ch * count),
                ]
                + row_sends,
                [struct((images * step, heads_w), BF), struct((images * lat, heads_w), BF)]
                + row_outs,
                [pltpu.VMEM((imgs, lat, heads_w), F32)],
                tie(ids, before),
                [q, k, v, lse, grad_all[ch], total] + ([] if first else [gk, gq]),
                16 * attn_macs / CHUNKS,
                f"back_scores{ch}",
                None if first else {6: 0, 7: 1},
            )
            gk, gq = outs[:2]
            query_terms.append(exchanged(*outs[2:]))
        sum_value.sent()
        key_parts = weight_grad(
            tie(ids, gk, sum_out.third()),
            [
                (source(src), [(gk, images * step, 0)]),
                ([(nlat, whole(nlat))], [(gq, images * lat, 0)]),
            ],
            rows,
            width,
            heads_w,
            "grad_query_keys",
        )
        sum_key = Sum(key_parts, groups_of(0, heads_w))

        ff_back = tie(ff_back, key_parts[0])
        final_lat = [mid + sum(t.astype(F32) for t in terms) for mid, terms in zip(middle, ff_back)]
        final_lat = jnp.concatenate(final_lat) + own_ff[2].astype(F32)
        final_lat = final_lat.reshape(images, share, width)
        lat_own = lax.dynamic_index_in_dim(lat4, me, 1, keepdims=False).astype(F32)
        latents_out = jnp.where(live[:, None, None] > 0, final_lat, lat_own)

        media_grad = latent_grad = None
        imgs = min(4, part)
        count = part // imgs
        for ch in range(CHUNKS):
            first = media_grad is None

            def share_rows(size, ch=ch):
                return pl.BlockSpec(
                    (imgs, None, size, width), lambda i, ids, live: (i + ch * count, ids[0], 0, 0)
                )

            before = [sum_key.second(), latents_out, sum_value.third()] if first else [media_grad]
            outs = call(
                functools.partial(
                    source_back_kernel, groups, cw, imgs, patch, share, ch * count
                ),
                (count,),
                [rows_of(imgs * step, heads_w, ch * count)] * 2
                + [whole(w_qk), third(w_vo, cw, 0)]
                + [share_rows(patch), share_rows(share), share_rows(share)]
                + [rows_of(imgs * share, heads_w)] * groups
                + [rows_of(imgs * share, width), whole(gains[0]), whole(gains[2])]
                + ([] if first else [anywhere()] * 2),
                [
                    images_of(imgs, patch, width, ch * count),
                    images_of(imgs, share, width, ch * count),
                    fixed_rows(4, width),
                ],
                [
                    struct((images, patch, width), F32),
                    struct((images, share, width), F32),
                    struct((4, width), F32),
                ],
                [
                    pltpu.VMEM((imgs * step, width), F32),
                    pltpu.VMEM((imgs * share, width), F32),
                    pltpu.VMEM((imgs * share, heads_w), BF),
                ],
                [tie(ids, before), live],
                [gk, gv, w_qk, w_vo, media4, lat4, cot4]
                + query_terms[ch]
                + [grad_mid[ch], gains[0], gains[2]]
                + ([] if first else [media_grad, latent_grad]),
                2 * part * step * width * 2 * heads_w,
                f"source_back{ch}",
                None if first else {10 + groups: 0, 11 + groups: 1},
            )
            media_grad, latent_grad = outs[:2]
            gain_terms[ch] = jnp.concatenate([outs[2], gain_terms[ch]])
            if first:
                sum_key.sent()
        sum_key.third()
        query_key = sum_key.last()
        grad_value = sum_value.last(media_grad)
        grad_attn = sum_out.last(media_grad)

        total = sum(gain_terms)
        near = [from_dp(total, cf=1)] + [plane(total, *at, False) for at in others]
        near += [plane(total, *at, False, 1) for at in others]
        total = total + sum(near)
        norm_grads = total + sum(from_dp(total, s) for s in range(1, depth_z))

        return (
            latents_out,
            media_grad,
            latent_grad,
            query_key[:, cw:],
            jnp.stack([query_key[:, :cw], grad_value], axis=1),
            grad_attn.T,
            grad_up.astype(F32),
            grad_down.T.astype(F32),
            norm_grads,
        )

    return local


def solution(mesh):
    return jax.shard_map(
        make_local(mesh.shape["dp"] // 4, mesh.shape["head"]),
        mesh=mesh,
        in_specs=(
            P("dp", None, None),
            P("dp", None, None),
            P("dp", None, None),
            P("dp"),
            P(),
            P(),
            P(),
            P(),
            P(),
            P(),
            P("dp", "head"),
            P("dp", None, "head"),
            P("head", "dp"),
            P("dp", "head"),
            P("head", "dp"),
        ),
        out_specs=(
            P("dp", "head", None),
            P("dp", "head", None),
            P("dp", "head", None),
            P("dp", "head"),
            P("dp", None, "head"),
            P("head", "dp"),
            P("dp", "head"),
            P("head", "dp"),
            P(),
        ),
        check_vma=False,
    )
```

```python
import functools
import math

import jax
import jax.numpy as jnp
from jax import lax
from jax.experimental import pallas as pl
from jax.experimental.pallas import tpu as pltpu
from jax.sharding import PartitionSpec as P

HD = 64
HEADS = 8
CHUNKS = 2
EPS = 1e-05
BF = jnp.bfloat16
F32 = jnp.float32
MIB = 1024 * 1024
VMEM = 58
SMALL = 40
STREAMED = ("feed_forward_own", "feed_forward_away", "grad_up", "grad_down", "middle_back", "source_back")

NN = (((1,), (0,)), ((), ()))
NT = (((1,), (1,)), ((), ()))
TN = (((0,), (0,)), ((), ()))


def dot(left, right, form=NN):
    return lax.dot_general(left, right, form, preferred_element_type=F32)


def struct(shape, dtype):
    return jax.ShapeDtypeStruct(shape, dtype)


def call(kernel, grid, in_specs, out_specs, out_shape, scratch, ids, args, flops, name, alias=None):
    scalars = ids if isinstance(ids, (list, tuple)) else [ids]
    moved = sum(a.size * a.dtype.itemsize for a in args if a.ndim < 4)
    moved += sum(o.size * jnp.dtype(o.dtype).itemsize for o in out_shape)
    return pl.pallas_call(
        kernel,
        grid_spec=pltpu.PrefetchScalarGridSpec(
            num_scalar_prefetch=len(scalars),
            grid=grid,
            in_specs=in_specs,
            out_specs=out_specs,
            scratch_shapes=scratch,
        ),
        out_shape=out_shape,
        input_output_aliases={len(scalars) + k: v for k, v in (alias or {}).items()},
        compiler_params=pltpu.CompilerParams(
            vmem_limit_bytes=(VMEM if name in STREAMED else SMALL) * MIB,
            dimension_semantics=("arbitrary",) * len(grid)
        ),
        cost_estimate=pl.CostEstimate(
            flops=int(flops), bytes_accessed=int(moved), transcendentals=0
        ),
        name=name,
    )(*scalars, *args)


def whole(array):
    zeros = (0,) * array.ndim
    return pl.BlockSpec(array.shape, lambda *_: zeros)


def rows_of(block, width, first=0):
    return pl.BlockSpec((block, width), lambda i, *_: (i + first, 0))


def fixed_rows(block, width, at=0):
    return pl.BlockSpec((block, width), lambda *_: (at, 0))


def images_of(block, rows, width, first=0):
    return pl.BlockSpec((block, rows, width), lambda i, *_: (i + first, 0, 0))


def third(array, width, at):
    if width % 128:
        return whole(array)
    return pl.BlockSpec(array.shape[:2] + (width,), lambda *_: (0, 0, at))


def columns(ref, group, width, at):
    if ref.shape[2] == width:
        return ref[group]
    return ref[group, :, at * width : (at + 1) * width]


def anywhere():
    return pl.BlockSpec(memory_space=pl.ANY)


def tie(values, *first):
    flat, tree = jax.tree.flatten(values)
    out = lax.optimization_barrier(tuple(flat) + tuple(jax.tree.leaves(first)))
    return jax.tree.unflatten(tree, out[: len(flat)])


def norm_parts(values):
    centre = values - jnp.mean(values, axis=-1, keepdims=True)
    rstd = lax.rsqrt(jnp.mean(centre * centre, axis=-1, keepdims=True) + EPS)
    return centre * rstd, rstd


def norm_back(values, gain, grad):
    xhat, rstd = norm_parts(values)
    scaled = grad * gain
    first = jnp.mean(scaled, axis=-1, keepdims=True)
    second = jnp.mean(scaled * xhat, axis=-1, keepdims=True)
    return rstd * (scaled - first - xhat * second), grad * xhat


def fold_rows(value):
    return jnp.sum(value.reshape(value.shape[0] // 8, 8, value.shape[1]), axis=0)


def norm_kernel(
    imgs, lat, share, patch, ids, media, latents, m_gain, m_bias, l_gain, l_bias, *refs
):
    src, nlat, src_t, nlat_t, keep = refs
    start = pl.multiple_of(ids[0] * share, share)
    step = patch + share
    for i in range(imgs):
        xhat, _ = norm_parts(media[i].astype(F32))
        src[i * step : i * step + patch, :] = (xhat * m_gain[...] + m_bias[...]).astype(BF)
        xhat, _ = norm_parts(latents[i].astype(F32))
        normed = xhat * l_gain[...] + l_bias[...]
        nlat[i * lat : (i + 1) * lat, :] = normed.astype(BF)
        keep[...] = normed
        src[i * step + patch : (i + 1) * step, :] = keep[pl.ds(start, share), :].astype(BF)
    src_t[...] = src[...].T
    nlat_t[...] = nlat[...].T


def assemble(entries, pieces, depth, ids, rows, groups, width, name):
    def kernel(ids_ref, *refs):
        out, sems = refs[len(pieces)], refs[len(pieces) + 1]
        copies = []
        for e, (op, lead, group, s, yf, cf) in enumerate(entries):
            block = lax.rem(ids_ref[1] + s, depth) * 4
            block += lax.rem(ids_ref[2] + yf, 2) * 2 + lax.rem(ids_ref[3] + cf, 2)
            start = pl.multiple_of(block * rows, rows)
            source = refs[op] if lead is None else refs[op].at[lead]
            copies.append(
                pltpu.make_async_copy(source, out.at[group, pl.ds(start, rows), :], sems.at[e])
            )
        for copy in copies:
            copy.start()
        for copy in copies:
            copy.wait()

    return call(
        kernel,
        (1,),
        [anywhere()] * len(pieces),
        [pl.BlockSpec((groups, depth * 4 * rows, width), lambda *_: (0, 0, 0))],
        [struct((groups, depth * 4 * rows, width), BF)],
        [pltpu.SemaphoreType.DMA((len(entries),))],
        ids,
        pieces,
        0,
        name,
    )[0]


def diag_mask(heads, width, dtype):
    row = lax.broadcasted_iota(jnp.int32, (heads * HD, width), 0) // HD
    col = lax.broadcasted_iota(jnp.int32, (heads * HD, width), 1) // HD
    return jnp.where(row == col, 1.0, 0.0).astype(dtype)


def spread(block, heads, mask):
    return jnp.concatenate([block] * heads, axis=0) * mask


def fold(full, heads, lat, mask):
    full = full * mask
    total = full[:lat]
    for h in range(1, heads):
        total = total + full[h * lat : (h + 1) * lat]
    return total


def lane_roll(values, s, groups, cw):
    if s == 0:
        return values
    if cw % 128 == 0:
        cut = (groups - s) * cw
        return jnp.concatenate([values[:, cut:], values[:, :cut]], axis=1)
    return pltpu.roll(values, s * cw, 1)


def project_kernel(groups, cw, imgs, step, lat, ids, src, nlat, w, q, k, stats):
    heads = cw // HD
    for j in range(groups):
        k[:, j * cw : (j + 1) * cw] = dot(src[...], w[j, :, cw : 2 * cw]).astype(BF)
        q[:, j * cw : (j + 1) * cw] = (dot(nlat[...], w[j, :, :cw]) * (HD**-0.5)).astype(BF)
    mask = diag_mask(heads, cw, BF)
    for i in range(imgs):
        for j in range(groups):
            cols = slice(j * cw, (j + 1) * cw)
            qbd = spread(q[i * lat : (i + 1) * lat, cols], heads, mask)
            score = dot(k[i * step : (i + 1) * step, cols], qbd, NT)
            top = jnp.max(score, axis=0, keepdims=True)
            stats[i, 0:1, cols] = top
            stats[i, 1:2, cols] = jnp.sum(jnp.exp(score - top), axis=0, keepdims=True)


def values_kernel(groups, cw, ids, src, w, v):
    for j in range(groups):
        v[:, j * cw : (j + 1) * cw] = dot(src[...], columns(w, j, cw, 2)).astype(BF)


def send_rows(groups, share, ids, scratch, i, keep, send):
    for s in range(groups):
        start = pl.multiple_of(lax.rem(ids[0] + s, groups) * share, share)
        rows = scratch[pl.ds(start, share), :]
        if s == 0:
            keep[i * share : (i + 1) * share, :] = rows
        else:
            send[s - 1, i * share : (i + 1) * share, :] = rows.astype(BF)


def mix_kernel(groups, cw, imgs, step, lat, share, ids, q, k, v, lse, keep, send, scratch):
    heads = cw // HD
    mask, fmask = diag_mask(heads, cw, BF), diag_mask(heads, cw, F32)
    for i in range(imgs):
        rows = slice(i * step, (i + 1) * step)
        for j in range(groups):
            cols = slice(j * cw, (j + 1) * cw)
            qbd = spread(q[i * lat : (i + 1) * lat, cols], heads, mask)
            probs = jnp.exp(dot(k[rows, cols], qbd, NT) - lse[i, 0:1, cols])
            full = dot(probs.astype(BF), v[rows, cols], TN)
            scratch[i, :, cols] = fold(full, heads, lat, fmask)
        send_rows(groups, share, ids, scratch.at[i], i, keep, send)


def back_probs_kernel(groups, cw, imgs, step, lat, share, ids, q, k, v, lse, grad_keep, *refs):
    recv, (gv, grad_all, delta, scratch) = refs[: groups - 1], refs[groups - 1 :]
    heads = cw // HD
    mask = diag_mask(heads, cw, BF)
    for i in range(imgs):
        for s in range(groups):
            start = pl.multiple_of(lax.rem(ids[0] + s, groups) * share, share)
            block = grad_keep if s == 0 else recv[s - 1]
            block = lane_roll(block[i * share : (i + 1) * share, :].astype(F32), s, groups, cw)
            scratch[i, pl.ds(start, share), :] = block
        grad_all[i * lat : (i + 1) * lat, :] = scratch[i].astype(BF)
        rows = slice(i * step, (i + 1) * step)
        for j in range(groups):
            cols = slice(j * cw, (j + 1) * cw)
            qbd = spread(q[i * lat : (i + 1) * lat, cols], heads, mask)
            gbd = spread(grad_all[i * lat : (i + 1) * lat, cols], heads, mask)
            probs = jnp.exp(dot(k[rows, cols], qbd, NT) - lse[i, 0:1, cols])
            delta[i, 0:1, cols] = jnp.sum(probs * dot(v[rows, cols], gbd, NT), axis=0, keepdims=True)
            gv[rows, cols] = dot(probs.astype(BF), gbd).astype(BF)


def back_scores_kernel(
    groups, cw, imgs, step, lat, share, ids, q, k, v, lse, grad_all, delta, gk, gq, keep, send, scratch
):
    heads = cw // HD
    mask, fmask = diag_mask(heads, cw, BF), diag_mask(heads, cw, F32)
    for i in range(imgs):
        rows = slice(i * step, (i + 1) * step)
        for j in range(groups):
            cols = slice(j * cw, (j + 1) * cw)
            qbd = spread(q[i * lat : (i + 1) * lat, cols], heads, mask)
            gbd = spread(grad_all[i * lat : (i + 1) * lat, cols], heads, mask)
            probs = jnp.exp(dot(k[rows, cols], qbd, NT) - lse[i, 0:1, cols])
            grad = dot(v[rows, cols], gbd, NT) - delta[i, 0:1, cols]
            grad = (probs * grad).astype(BF)
            gk[rows, cols] = dot(grad, qbd).astype(BF)
            full = dot(grad, k[rows, cols], TN)
            scratch[i, :, cols] = fold(full, heads, lat, fmask) * (HD**-0.5)
        gq[i * lat : (i + 1) * lat, :] = scratch[i].astype(BF)
        send_rows(groups, share, ids, scratch.at[i], i, keep, send)


def middle_kernel(groups, cw, ids, keep, *refs):
    recv = refs[: groups - 1]
    latents, w, gain, bias = refs[groups - 1 : groups + 3]
    mixed, middle, normed = refs[-3:]
    total = keep[...]
    for s in range(1, groups):
        total = total + lane_roll(recv[s - 1][...].astype(F32), s, groups, cw)
    low = total.astype(BF)
    mixed[...] = low
    value = latents[...].astype(F32).reshape(middle.shape)
    for j in range(groups):
        value = value + dot(low[:, j * cw : (j + 1) * cw], columns(w, j, cw, 3), NT)
    middle[...] = value
    xhat, _ = norm_parts(value)
    normed[...] = (xhat * gain[...] + bias[...]).astype(BF)


def gelu_parts(value):
    cdf = 0.5 * (1.0 + lax.erf(value * (0.5**0.5)))
    pdf = jnp.exp(value * value * -0.5) * 0.3989422804014327
    return value * cdf, cdf + value * pdf


def forward_kernel(terms, ids, *refs):
    normed, final = refs[:terms], refs[terms : 2 * terms]
    up, down, hidden, up_low, ff, mid, normed_t = refs[2 * terms : 2 * terms + 7]
    normed_all, final_all, ff_total, mid_total = refs[2 * terms + 7 :]
    step = pl.program_id(0)

    @pl.when(step == 0)
    def _():
        at = 0
        for left, right in zip(normed, final):
            normed_all[at : at + left.shape[0], :] = left[...]
            final_all[at : at + left.shape[0], :] = right[...]
            at += left.shape[0]

    act, slope = gelu_parts(dot(normed_all[...], up[...]))
    low = act.astype(BF)
    hidden[...] = low
    ff_part = dot(low, down[...], NT)
    low = (dot(final_all[...], down[...]) * slope).astype(BF)
    up_low[...] = low
    mid_part = dot(low, up[...], NT)
    last = pl.num_programs(0) - 1
    width = normed_t.shape[0]
    normed_t[...] = normed_all[:, pl.ds(pl.multiple_of(step * width, width), width)].T

    @pl.when(step == 0)
    def _():
        ff_total[...] = ff_part
        mid_total[...] = mid_part

    @pl.when(step > 0)
    def _():
        ff_total[...] += ff_part
        mid_total[...] += mid_part

    @pl.when(step == last)
    def _():
        ff[...] = ff_total[...].astype(BF)
        mid[...] = mid_total[...].astype(BF)


def middle_back_kernel(groups, cw, ids, part, *refs):
    recv = refs[: groups - 1]
    middle, final, w, gain, grad_mid, mid_low, grad_mixed, gains = refs[groups - 1 :]
    total = part[...].astype(F32)
    for other in recv:
        total = total + other[...].astype(F32)
    back, terms = norm_back(middle[...], gain[...], total)
    gains[0:1, :] = jnp.sum(terms, axis=0, keepdims=True)
    gains[1:2, :] = jnp.sum(total, axis=0, keepdims=True)
    value = final[...].astype(F32) + back
    grad_mid[...] = value
    low = value.astype(BF)
    mid_low[...] = low.T
    for j in range(groups):
        grad_mixed[:, j * cw : (j + 1) * cw] = dot(low, columns(w, j, cw, 3)).astype(BF)


def weight_grad_kernel(terms, rows, ids, *refs):
    left, right, outs = refs[:terms], refs[terms : 2 * terms], refs[2 * terms :]
    value = dot(left[0][...], right[0][...])
    for a, b in zip(left[1:], right[1:]):
        value = value + dot(a[...], b[...])
    if len(outs) == 1:
        outs[0][...] = value.astype(BF)
    else:
        keep, send, total = outs
        total[...] = value
        split_rows(rows, ids, total, keep, send)


def split_rows(rows, ids, total, keep, send):
    for b in range(keep.shape[0]):
        for ref, core in ((keep, ids[3]), (send, 1 - ids[3])):
            start = pl.multiple_of((b * 2 + core) * rows, rows)
            ref[b] = total[pl.ds(start, rows), :].astype(BF)


def weight_grad(ids, left, right, rows, block, split, name):
    depth, width = left[0].shape[0], right[0].shape[1]
    if split:
        outs = [struct((depth // rows // 2, rows, width), BF)] * 2
        spec = pl.BlockSpec((depth // rows // 2, rows, block), lambda i, *_: (0, 0, i))
        specs, scratch = [spec, spec], [pltpu.VMEM((depth, block), F32)]
    else:
        outs = [struct((depth, width), BF)]
        specs, scratch = [pl.BlockSpec((depth, block), lambda i, *_: (0, i))], []
    return call(
        functools.partial(weight_grad_kernel, len(left), rows),
        (width // block,),
        [whole(a) for a in left]
        + [pl.BlockSpec((a.shape[0], block), lambda i, *_: (0, i)) for a in right],
        specs,
        outs,
        scratch,
        ids,
        left + right,
        2 * sum(a.shape[0] for a in right) * depth * width,
        name,
    )


def sum_grad_kernel(plan, rows, ids, *refs):
    keep, send, total = refs[2 * sum(terms for _, _, terms in plan) :]
    first = 0
    for at, width, terms in plan:
        value = dot(refs[first][...], refs[first + 1][...])
        for k in range(first + 2, first + 2 * terms, 2):
            value = value + dot(refs[k][...], refs[k + 1][...])
        total[:, at : at + width] = value
        first += 2 * terms
    split_rows(rows, ids, total, keep, send)


def sum_grad(ids, results, rows, depth, name):
    blocks = max(1, 256 // rows)
    plan, specs, args, at, flops = [], [], [], 0, 0
    for terms in results:
        for left, right in terms:
            size, width = right.shape
            specs.append(pl.BlockSpec((blocks * 2 * rows, size), lambda i, ids: (i, 0)))
            specs.append(whole(right))
            args += [left, right]
            flops += 2 * size * width * depth
        plan.append((at, width, len(terms)))
        at += width
    spec = pl.BlockSpec((blocks, rows, at), lambda i, ids: (i, 0, 0))
    return call(
        functools.partial(sum_grad_kernel, plan, rows),
        (depth // (blocks * 2 * rows),),
        specs,
        [spec, spec],
        [struct((depth // rows // 2, rows, at), BF)] * 2,
        [pltpu.VMEM((blocks * 2 * rows, at), F32)],
        ids,
        args,
        flops,
        name,
    )


def source_back_kernel(
    groups, cw, imgs, patch, share, ids, live, gk, gv, wk, wv, media, latents, cot, keep, *refs
):
    recv, refs = refs[: groups - 1], refs[groups - 1 :]
    grad_mid, m_gain, l_gain, media_grad, latent_grad, gains, total, lat_total, query = refs
    base = pl.program_id(0) * imgs
    step = patch + share
    value = dot(gk[:, :cw], wk[0, :, cw : 2 * cw], NT) + dot(gv[:, :cw], columns(wv, 0, cw, 2), NT)
    for j in range(1, groups):
        cols = slice(j * cw, (j + 1) * cw)
        value = value + dot(gk[:, cols], wk[j, :, cw : 2 * cw], NT)
        value = value + dot(gv[:, cols], columns(wv, j, cw, 2), NT)
    total[...] = value
    asked = keep[...]
    for s in range(1, groups):
        asked = asked + lane_roll(recv[s - 1][...].astype(F32), s, groups, cw)
    query[...] = asked.astype(BF)
    value = dot(query[:, :cw], wk[0, :, :cw], NT)
    for j in range(1, groups):
        value = value + dot(query[:, j * cw : (j + 1) * cw], wk[j, :, :cw], NT)
    lat_total[...] = value

    @pl.when(pl.program_id(0) == 0)
    def _():
        gains[...] = jnp.zeros_like(gains)

    sums = [0.0] * 4
    for i in range(imgs):
        grad = total[i * step : i * step + patch, :]
        back, terms = norm_back(media[i].astype(F32), m_gain[...], grad)
        media_grad[i] = back
        sums[0] += fold_rows(terms)
        sums[1] += fold_rows(grad)
        rows = slice(i * share, (i + 1) * share)
        grad = total[i * step + patch : (i + 1) * step, :] + lat_total[rows, :]
        back, terms = norm_back(latents[i].astype(F32), l_gain[...], grad)
        sums[2] += fold_rows(terms)
        sums[3] += fold_rows(grad)
        latent_grad[i] = jnp.where(
            live[base + i] > 0, grad_mid[rows, :] + back, cot[i].astype(F32)
        )
    for k in range(4):
        gains[k : k + 1, :] += jnp.sum(sums[k], axis=0, keepdims=True)


def make_local(depth_z, groups):
    dp_size = depth_z * 4

    def from_dp(value, s=0, yf=0, cf=0):
        pairs = []
        for dst in range(dp_size):
            z, y, c = dst // 4, dst // 2 % 2, dst % 2
            pairs.append(((z + s) % depth_z * 4 + (y ^ yf) * 2 + (c ^ cf), dst))
        return lax.ppermute(value, "dp", pairs)

    def flip_z(value, bit):
        pairs = [(((dst // 4) ^ bit) * 4 + dst % 4, dst) for dst in range(dp_size)]
        return lax.ppermute(value, "dp", pairs)

    def from_head(value, s):
        return lax.ppermute(value, "head", [((x + s) % groups, x) for x in range(groups)])

    def to_head(value, s):
        return lax.ppermute(value, "head", [(x, (x + s) % groups) for x in range(groups)])

    def plane(value, sx, yf, back, cf=0):
        pairs = []
        for dst in range(dp_size):
            for x in range(groups):
                other = (dst ^ (2 * yf + cf)) * groups + (x + sx) % groups
                mine = dst * groups + x
                pairs.append((mine, other) if back else (other, mine))
        return lax.ppermute(value, ("dp", "head"), pairs)

    others = [(sx, yf) for sx in range(groups) for yf in range(2) if sx or yf]

    def local(
        media_tokens,
        latents,
        cotangent,
        image_counts,
        media_gain,
        media_bias,
        latent_gain,
        latent_bias,
        ff_gain,
        ff_bias,
        w_query,
        w_keyval,
        w_attn_out,
        w_up,
        w_down,
    ):
        images, patches, width = media_tokens.shape
        lat = latents.shape[1]
        rows, cw = w_query.shape
        units = w_up.shape[1]
        patch, share = patches // groups, lat // groups
        step = patch + share
        heads_w = cw * groups
        me = lax.axis_index("head").astype(jnp.int32)
        place = lax.axis_index("dp").astype(jnp.int32)
        z, y, c = place // 4, place // 2 % 2, place % 2
        ids = jnp.stack([me, z, y, c])
        live = (jnp.arange(images, dtype=jnp.int32) < jnp.sum(image_counts)).astype(jnp.int32)
        gains = [
            g.reshape(1, width)
            for g in (media_gain, media_bias, latent_gain, latent_bias, ff_gain, ff_bias)
        ]
        media4 = media_tokens.reshape(images, groups, patch, width)
        lat4 = latents.reshape(images, groups, share, width)
        cot4 = cotangent.reshape(images, groups, share, width)

        part = images // CHUNKS
        own = part * share

        shard = jnp.concatenate([w_query, w_keyval[:, 0], w_keyval[:, 1], w_attn_out.T], axis=1)
        got = [from_dp(shard, s) for s in range(1, depth_z)]
        w_up_all = lax.all_gather(w_up, "dp", axis=0, tiled=True)
        w_down_all = lax.all_gather(w_down.T, "dp", axis=0, tiled=True)
        live_low = live.astype(BF).reshape(images, 1, 1)
        final4 = [
            lax.dynamic_index_in_dim(cot4, (me + s) % groups, 1, keepdims=False) * live_low
            for s in range(groups)
        ]
        final4 = jnp.stack(final4).reshape(groups, images * share, width)
        own_t = final4[0].T
        away_t = final4[1:].reshape((groups - 1) * images * share, width).T
        final4, own_t, away_t = tie((final4, own_t, away_t), shard)
        line = jnp.stack([shard] + tie(got, final4, own_t, away_t))
        parts = {(0, 0): line} | {at: plane(line, *at, False) for at in others}

        imgs = math.gcd(images, math.lcm(128, step) // step)
        src, nlat, src_t, nlat_t = call(
            functools.partial(norm_kernel, imgs, lat, share, patch),
            (images // imgs,),
            [
                pl.BlockSpec((imgs, None, patch, width), lambda i, ids: (i, ids[0], 0, 0)),
                images_of(imgs, lat, width),
            ]
            + [whole(gains[0])] * 4,
            [
                rows_of(imgs * step, width),
                rows_of(imgs * lat, width),
                pl.BlockSpec((width, imgs * step), lambda i, ids: (0, i)),
                pl.BlockSpec((width, imgs * lat), lambda i, ids: (0, i)),
            ],
            [
                struct((images * step, width), BF),
                struct((images * lat, width), BF),
                struct((width, images * step), BF),
                struct((width, images * lat), BF),
            ],
            [pltpu.VMEM((lat, width), F32)],
            tie(ids, line),
            [media4, latents] + gains[:4],
            images * step * width * 12,
            "input_norms",
        )

        pieces, entries = [], []
        for (sx, yf), part_of in parts.items():
            for cf, piece in ((0, part_of), (1, from_dp(tie(part_of, src), cf=1))):
                for s in range(depth_z):
                    entries.append((len(pieces), s, sx, s, yf, cf))
                pieces.append(piece)
        w_attn = assemble(entries, pieces, depth_z, ids, rows, groups, 4 * cw, "place_attn")

        imgs = 4
        attn_macs = images * step * lat * heads_w
        q, k, stats = call(
            functools.partial(project_kernel, groups, cw, imgs, step, lat),
            (images // imgs,),
            [rows_of(imgs * step, width), rows_of(imgs * lat, width), third(w_attn, 2 * cw, 0)],
            [
                rows_of(imgs * lat, heads_w),
                rows_of(imgs * step, heads_w),
                images_of(imgs, 2, heads_w),
            ],
            [
                struct((images * lat, heads_w), BF),
                struct((images * step, heads_w), BF),
                struct((images, 2, heads_w), F32),
            ],
            [],
            ids,
            [src, nlat, w_attn],
            2 * images * (step * width * heads_w + lat * width * heads_w) + 8 * attn_macs,
            "project",
        )
        tops, sums = [stats[:, :1]], [stats[:, 1:]]
        for s in range(1, groups):
            other = jnp.roll(from_head(stats, s), s * cw, axis=2)
            tops.append(other[:, :1])
            sums.append(other[:, 1:])
        v = call(
            functools.partial(values_kernel, groups, cw),
            (images // imgs,),
            [rows_of(imgs * step, width), third(w_attn, cw, 2)],
            [rows_of(imgs * step, heads_w)],
            [struct((images * step, heads_w), BF)],
            [],
            tie(ids, q),
            [src, w_attn],
            2 * images * step * width * heads_w,
            "values",
        )[0]
        top = functools.reduce(jnp.maximum, tops)
        lse = top + jnp.log(sum(t * jnp.exp(m - top) for m, t in zip(tops, sums)))

        imgs = min(imgs, part)
        count = part // imgs

        def attn_specs(ch):
            return [
                rows_of(imgs * lat, heads_w, ch * count),
                rows_of(imgs * step, heads_w, ch * count),
                rows_of(imgs * step, heads_w, ch * count),
                images_of(imgs, 1, heads_w, ch * count),
            ]

        row_sends = [
            rows_of(imgs * share, heads_w),
            pl.BlockSpec((groups - 1, imgs * share, heads_w), lambda i, ids: (0, i, 0)),
        ]
        row_outs = [struct((own, heads_w), F32), struct((groups - 1, own, heads_w), BF)]

        def exchanged(keep, send):
            return [keep] + [to_head(send[s - 1], s) for s in range(groups - 1, 0, -1)]

        mixes, normed, mixed, middle = [], [], None, None
        for ch in range(CHUNKS):
            keep, send = call(
                functools.partial(mix_kernel, groups, cw, imgs, step, lat, share),
                (count,),
                attn_specs(ch),
                row_sends,
                row_outs,
                [pltpu.VMEM((imgs, lat, heads_w), F32)],
                tie(ids, [a[0] for a in mixes]),
                [q, k, v, lse],
                8 * attn_macs / CHUNKS,
                f"mix{ch}",
            )
            mixes.append(exchanged(keep, send))
        for ch in range(CHUNKS):
            lat_spec = pl.BlockSpec(
                (part, None, share, width), lambda i, ids, ch=ch: (ch, ids[0], 0, 0)
            )
            outs = call(
                functools.partial(middle_kernel, groups, cw),
                (1,),
                [whole(a) for a in mixes[ch]]
                + [lat_spec, third(w_attn, cw, 3), whole(gains[4]), whole(gains[5])]
                + ([anywhere()] * 2 if ch else []),
                [fixed_rows(own, heads_w, ch), fixed_rows(own, width, ch), fixed_rows(own, width)],
                [
                    struct((CHUNKS * own, heads_w), BF),
                    struct((CHUNKS * own, width), F32),
                    struct((own, width), BF),
                ],
                [],
                tie(ids, [a[0] for a in normed]),
                mixes[ch] + [lat4, w_attn, gains[4], gains[5]] + ([mixed, middle] if ch else []),
                2 * own * heads_w * width,
                f"middle{ch}",
                {groups + 4: 0, groups + 5: 1} if ch else None,
            )
            mixed, middle = outs[:2]
            normed.append([outs[2]] + [from_head(outs[2], s) for s in range(1, groups)])
        block = min(512, units)

        def feed_forward(terms, ids, name):
            size = len(terms) * own
            return call(
                functools.partial(forward_kernel, len(terms)),
                (units // block,),
                [whole(a) for a, _ in terms]
                + [spec for _, spec in terms]
                + [
                    pl.BlockSpec((width, block), lambda i, ids: (0, i)),
                    pl.BlockSpec((width, block), lambda i, ids: (0, i)),
                ],
                [pl.BlockSpec((size, block), lambda i, ids: (0, i))] * 2
                + [fixed_rows(size, width)] * 2
                + [pl.BlockSpec((width * block // units, size), lambda i, ids: (i, 0))],
                [struct((size, units), BF)] * 2
                + [struct((size, width), BF)] * 2
                + [struct((width, size), BF)],
                [pltpu.VMEM((size, width), BF)] * 2 + [pltpu.VMEM((size, width), F32)] * 2,
                ids,
                [a for a, _ in terms] + [final4] * len(terms) + [w_up_all, w_down_all],
                8 * size * width * units,
                name,
            )

        def final_rows(s, ch):
            return pl.BlockSpec((None, own, width), lambda *_: (s, ch, 0))

        size = CHUNKS * own
        away_ff = feed_forward(
            [(normed[ch][t], final_rows(t, ch)) for t in range(1, groups) for ch in range(CHUNKS)],
            ids,
            "feed_forward_away",
        )
        ff_back, mid_back = [a.reshape(groups - 1, size, width) for a in away_ff[2:4]]
        mid_back = [to_head(mid_back[s - 1], s) for s in range(groups - 1, 0, -1)]
        own_ff = feed_forward(
            [(normed[ch][0], final_rows(0, ch)) for ch in range(CHUNKS)],
            tie(ids, away_ff),
            "feed_forward_own",
        )

        def pick(block, index, axis=0):
            return lax.dynamic_index_in_dim(block, index, axis, keepdims=False).astype(F32)

        def lanes(block, cols):
            if len(cols) == 1 and cols[0] == slice(0, block.shape[-1]):
                return block
            return jnp.concatenate([block[..., c] for c in cols], axis=-1)

        class Sum:
            def __init__(self, keep, recv, cols):
                self.cols = cols
                self.grid = [a.reshape((depth_z, 2) + a.shape[1:]) for a in (keep, recv)]
                self.crossed, self.near = [], []

            def at(self, sx, yy):
                terms = [pick(lanes(a, self.cols[sx]), yy, 1) for a in self.grid]
                return sum(terms + [pick(a, yy, 1) for a in self.crossed])

            def cross(self, late):
                grid = tie(self.grid, late)
                self.away = [
                    sum(lanes(a, self.cols[sx]).astype(F32) for a in grid).astype(BF)
                    for sx in range(1, groups)
                ]
                return self.away

            def across(self):
                self.crossed = [to_head(a, sx) for sx, a in zip(range(1, groups), self.away)]

            def second(self, routes, late=()):
                self.grid, self.crossed = tie((self.grid, self.crossed), late)
                self.routes = routes
                self.away = [self.at(sx, y ^ yf).astype(BF) for sx, yf in routes]
                return self.away

            def sent(self):
                self.near = [plane(a, *to, True) for a, to in zip(self.away, self.routes)]

            def start_z(self):
                base = self.at(0, y)

                def block(zz):
                    return pick(base, zz) + sum(pick(a, zz) for a in self.near)

                self.block, self.left, self.bit = block, depth_z, 1

            def halve(self, late=()):
                turn = tie(z, late)
                mine, block = z // self.bit % 2, self.block
                away_at = 1 - turn // self.bit % 2
                self.left //= 2
                self.held = lambda k: block(2 * k + mine)
                away = [block(2 * k + away_at) for k in range(self.left)]
                self.away = jnp.stack(away).astype(BF)
                return self.away

            def halved(self, late=()):
                near, held = tie(flip_z(self.away, self.bit), late), self.held
                self.block, self.bit = (lambda k: held(k) + pick(near, k)), 2 * self.bit

            def rest(self):
                while self.left > 1:
                    self.halve()
                    self.halved()
                return self.block(0)

            def third(self):
                self.start_z()
                self.away = [self.block((z + s) % depth_z).astype(BF) for s in range(1, depth_z)]
                return self.away

            def last(self):
                got = [from_dp(a, depth_z - s) for s, a in zip(range(1, depth_z), self.away)]
                return self.block(z) + sum(a.astype(F32) for a in got)

        along_y = [(0, 1)]

        def groups_of(*starts):
            return [[slice(a + sx * cw, a + (sx + 1) * cw) for a in starts] for sx in range(groups)]

        up_part = weight_grad(
            tie(ids, own_ff[0]),
            [own_ff[4], away_ff[4]],
            [own_ff[1], away_ff[1]],
            rows,
            block,
            False,
            "grad_up",
        )[0]
        grad_mid, mid_low_t, grad_mixed, ff_gains = call(
            functools.partial(middle_back_kernel, groups, cw),
            (1,),
            [whole(own_ff[3])]
            + [whole(t) for t in mid_back]
            + [whole(middle), pl.BlockSpec((None, size, width), lambda *_: (0, 0, 0))]
            + [third(w_attn, cw, 3), whole(gains[4])],
            [
                fixed_rows(size, width),
                fixed_rows(width, size),
                fixed_rows(size, heads_w),
                fixed_rows(2, width),
            ],
            [
                struct((size, width), F32),
                struct((width, size), BF),
                struct((size, heads_w), BF),
                struct((2, width), F32),
            ],
            [],
            tie(ids, up_part),
            [own_ff[3]] + mid_back + [middle, final4, w_attn, gains[4]],
            2 * size * heads_w * width,
            "middle_back",
        )
        grad_mixed = [grad_mixed] + [from_head(grad_mixed, s) for s in range(1, groups)]

        grad_up = lax.psum_scatter(tie(up_part, mid_low_t), "dp", scatter_dimension=0, tiled=True)
        down_parts = weight_grad(
            tie(ids, mid_low_t),
            [own_t, away_t],
            [own_ff[0], away_ff[0]],
            rows,
            block,
            True,
            "grad_down",
        )

        count = images // imgs
        gv, grad_all, delta = call(
            functools.partial(back_probs_kernel, groups, cw, imgs, step, lat, share),
            (count,),
            attn_specs(0) + [rows_of(imgs * share, heads_w)] * groups,
            [rows_of(imgs * step, heads_w), rows_of(imgs * lat, heads_w), images_of(imgs, 1, heads_w)],
            [
                struct((images * step, heads_w), BF),
                struct((images * lat, heads_w), BF),
                struct((images, 1, heads_w), F32),
            ],
            [pltpu.VMEM((imgs, lat, heads_w), F32)],
            tie(ids, down_parts[0]),
            [q, k, v, lse] + grad_mixed,
            12 * attn_macs,
            "back_probs",
        )
        recv = from_dp(tie(down_parts[1], gv), cf=1)
        sum_down = Sum(down_parts[0], recv, [[slice(0, units)]])
        ordered = jnp.roll(jnp.concatenate([own_ff[2][None], tie(ff_back, gv)]), me, axis=0)
        ordered = tie(ordered, grad_up)
        ff_sum = lax.psum_scatter(ordered, "head", scatter_dimension=0, tiled=True)[0]
        total = delta
        for s in range(1, groups):
            total = total + jnp.roll(from_head(delta, s), s * cw, axis=2)
        value_parts = sum_grad(
            tie(ids, gv),
            [[(mid_low_t, mixed)], [(src_t, gv)]],
            rows,
            width,
            "grad_out_values",
        )
        sum_value = Sum(value_parts[0], from_dp(value_parts[1], cf=1), groups_of(0, heads_w))
        gk, gq, keep, send = call(
            functools.partial(back_scores_kernel, groups, cw, imgs, step, lat, share),
            (count,),
            attn_specs(0) + [rows_of(imgs * lat, heads_w), images_of(imgs, 1, heads_w)],
            [rows_of(imgs * step, heads_w), rows_of(imgs * lat, heads_w)] + row_sends,
            [
                struct((images * step, heads_w), BF),
                struct((images * lat, heads_w), BF),
                struct((size, heads_w), F32),
                struct((groups - 1, size, heads_w), BF),
            ],
            [pltpu.VMEM((imgs, lat, heads_w), F32)],
            tie(ids, value_parts[0], sum_down.second(along_y, value_parts[0])),
            [q, k, v, lse, grad_all, total],
            16 * attn_macs,
            "back_scores",
        )
        sum_down.sent()
        query_terms = exchanged(keep, send)
        key_parts = sum_grad(
            tie(ids, gk, sum_value.cross(gk)),
            [[(src_t, gk)], [(nlat_t, gq)]],
            rows,
            width,
            "grad_query_keys",
        )
        sum_value.across()
        sum_down.start_z()
        sum_key = Sum(key_parts[0], from_dp(key_parts[1], cf=1), groups_of(0, heads_w))

        def share_rows(size):
            return pl.BlockSpec((imgs, None, size, width), lambda i, ids, live: (i, ids[0], 0, 0))

        before = [sum_key.second(others), sum_value.second(along_y), sum_down.halve()]
        media_grad, latent_grad, gain_terms = call(
            functools.partial(source_back_kernel, groups, cw, imgs, patch, share),
            (count,),
            [rows_of(imgs * step, heads_w)] * 2
            + [third(w_attn, 2 * cw, 0), third(w_attn, cw, 2)]
            + [share_rows(patch), share_rows(share), share_rows(share)]
            + [rows_of(imgs * share, heads_w)] * groups
            + [rows_of(imgs * share, width), whole(gains[0]), whole(gains[2])],
            [images_of(imgs, patch, width), images_of(imgs, share, width), fixed_rows(4, width)],
            [
                struct((images, patch, width), F32),
                struct((images, share, width), F32),
                struct((4, width), F32),
            ],
            [
                pltpu.VMEM((imgs * step, width), F32),
                pltpu.VMEM((imgs * share, width), F32),
                pltpu.VMEM((imgs * share, heads_w), BF),
            ],
            [tie(ids, before, grad_up), live],
            [gk, gv, w_attn, w_attn, media4, lat4, cot4]
            + query_terms
            + [grad_mid, gains[0], gains[2]],
            2 * images * step * width * 2 * heads_w,
            "source_back",
        )
        sum_key.sent()
        sum_value.sent()
        sum_key.near = tie(sum_key.near, media_grad)
        sum_value.near = tie(sum_value.near, media_grad)
        sum_down.halved(media_grad)
        sum_value.start_z()
        sum_key.third()
        query_key = sum_key.last()

        final_lat = middle + ff_sum.astype(F32)
        final_lat = final_lat.reshape(images, share, width)
        lat_own = lax.dynamic_index_in_dim(lat4, me, 1, keepdims=False).astype(F32)
        latents_out = jnp.where(live[:, None, None] > 0, final_lat, lat_own)

        total = jnp.concatenate([gain_terms, ff_gains])
        grad_down, out_value = sum_down.rest(), sum_value.rest()
        near = [from_dp(total, cf=1)] + [plane(total, *at, False) for at in others]
        near += [plane(total, *at, False, 1) for at in others]
        total = total + sum(near)
        norm_grads = total + sum(from_dp(total, s) for s in range(1, depth_z))

        return (
            latents_out,
            media_grad,
            latent_grad,
            query_key[:, cw:],
            jnp.stack([query_key[:, :cw], out_value[:, cw:]], axis=1),
            out_value[:, :cw].T,
            grad_up.astype(F32),
            grad_down.T,
            norm_grads,
        )

    return local


def solution(mesh):
    return jax.shard_map(
        make_local(mesh.shape["dp"] // 4, mesh.shape["head"]),
        mesh=mesh,
        in_specs=(
            P("dp", None, None),
            P("dp", None, None),
            P("dp", None, None),
            P("dp"),
            P(),
            P(),
            P(),
            P(),
            P(),
            P(),
            P("dp", "head"),
            P("dp", None, "head"),
            P("head", "dp"),
            P("dp", "head"),
            P("head", "dp"),
        ),
        out_specs=(
            P("dp", "head", None),
            P("dp", "head", None),
            P("dp", "head", None),
            P("dp", "head"),
            P("dp", None, "head"),
            P("head", "dp"),
            P("dp", "head"),
            P("head", "dp"),
            P(),
        ),
        check_vma=False,
    )
```

```python
import functools
import math

import jax
import jax.numpy as jnp
from jax import lax
from jax.experimental import pallas as pl
from jax.experimental.pallas import tpu as pltpu
from jax.sharding import PartitionSpec as P

HD = 64
HEADS = 8
CHUNKS = 2
EPS = 1e-05
BF = jnp.bfloat16
F32 = jnp.float32
MIB = 1024 * 1024
VMEM = 58
SMALL = 40
STREAMED = ("feed_forward_own", "feed_forward_away", "grad_up", "grad_down", "middle_back", "source_back")

NN = (((1,), (0,)), ((), ()))
NT = (((1,), (1,)), ((), ()))
TN = (((0,), (0,)), ((), ()))


def dot(left, right, form=NN):
    return lax.dot_general(left, right, form, preferred_element_type=F32)


def struct(shape, dtype):
    return jax.ShapeDtypeStruct(shape, dtype)


def call(kernel, grid, in_specs, out_specs, out_shape, scratch, ids, args, flops, name, alias=None):
    scalars = ids if isinstance(ids, (list, tuple)) else [ids]
    moved = sum(a.size * a.dtype.itemsize for a in args if a.ndim < 4)
    moved += sum(o.size * jnp.dtype(o.dtype).itemsize for o in out_shape)
    return pl.pallas_call(
        kernel,
        grid_spec=pltpu.PrefetchScalarGridSpec(
            num_scalar_prefetch=len(scalars),
            grid=grid,
            in_specs=in_specs,
            out_specs=out_specs,
            scratch_shapes=scratch,
        ),
        out_shape=out_shape,
        input_output_aliases={len(scalars) + k: v for k, v in (alias or {}).items()},
        compiler_params=pltpu.CompilerParams(
            vmem_limit_bytes=(VMEM if name in STREAMED else SMALL) * MIB,
            dimension_semantics=("arbitrary",) * len(grid)
        ),
        cost_estimate=pl.CostEstimate(
            flops=int(flops), bytes_accessed=int(moved), transcendentals=0
        ),
        name=name,
    )(*scalars, *args)


def whole(array):
    zeros = (0,) * array.ndim
    return pl.BlockSpec(array.shape, lambda *_: zeros)


def rows_of(block, width, first=0):
    return pl.BlockSpec((block, width), lambda i, *_: (i + first, 0))


def fixed_rows(block, width, at=0):
    return pl.BlockSpec((block, width), lambda *_: (at, 0))


def images_of(block, rows, width, first=0):
    return pl.BlockSpec((block, rows, width), lambda i, *_: (i + first, 0, 0))


def third(array, width, at):
    if width % 128:
        return whole(array)
    return pl.BlockSpec(array.shape[:2] + (width,), lambda *_: (0, 0, at))


def columns(ref, group, width, at):
    if ref.shape[2] == width:
        return ref[group]
    return ref[group, :, at * width : (at + 1) * width]


def anywhere():
    return pl.BlockSpec(memory_space=pl.ANY)


def tie(values, *first):
    flat, tree = jax.tree.flatten(values)
    out = lax.optimization_barrier(tuple(flat) + tuple(jax.tree.leaves(first)))
    return jax.tree.unflatten(tree, out[: len(flat)])


def norm_parts(values):
    centre = values - jnp.mean(values, axis=-1, keepdims=True)
    rstd = lax.rsqrt(jnp.mean(centre * centre, axis=-1, keepdims=True) + EPS)
    return centre * rstd, rstd


def norm_back(values, gain, grad):
    xhat, rstd = norm_parts(values)
    scaled = grad * gain
    first = jnp.mean(scaled, axis=-1, keepdims=True)
    second = jnp.mean(scaled * xhat, axis=-1, keepdims=True)
    return rstd * (scaled - first - xhat * second), grad * xhat


def fold_rows(value):
    return jnp.sum(value.reshape(value.shape[0] // 8, 8, value.shape[1]), axis=0)


def norm_kernel(
    imgs, lat, share, patch, ids, media, latents, m_gain, m_bias, l_gain, l_bias, *refs
):
    src, nlat, src_t, nlat_t, keep = refs
    start = pl.multiple_of(ids[0] * share, share)
    step = patch + share
    for i in range(imgs):
        xhat, _ = norm_parts(media[i].astype(F32))
        src[i * step : i * step + patch, :] = (xhat * m_gain[...] + m_bias[...]).astype(BF)
        xhat, _ = norm_parts(latents[i].astype(F32))
        normed = xhat * l_gain[...] + l_bias[...]
        nlat[i * lat : (i + 1) * lat, :] = normed.astype(BF)
        keep[...] = normed
        src[i * step + patch : (i + 1) * step, :] = keep[pl.ds(start, share), :].astype(BF)
    src_t[...] = src[...].T
    nlat_t[...] = nlat[...].T


def assemble(entries, pieces, depth, ids, rows, groups, width, name):
    def kernel(ids_ref, *refs):
        out, sems = refs[len(pieces)], refs[len(pieces) + 1]
        copies = []
        for e, (op, lead, group, s, yf, cf) in enumerate(entries):
            block = lax.rem(ids_ref[1] + s, depth) * 4
            block += lax.rem(ids_ref[2] + yf, 2) * 2 + lax.rem(ids_ref[3] + cf, 2)
            start = pl.multiple_of(block * rows, rows)
            source = refs[op] if lead is None else refs[op].at[lead]
            copies.append(
                pltpu.make_async_copy(source, out.at[group, pl.ds(start, rows), :], sems.at[e])
            )
        for copy in copies:
            copy.start()
        for copy in copies:
            copy.wait()

    return call(
        kernel,
        (1,),
        [anywhere()] * len(pieces),
        [pl.BlockSpec((groups, depth * 4 * rows, width), lambda *_: (0, 0, 0))],
        [struct((groups, depth * 4 * rows, width), BF)],
        [pltpu.SemaphoreType.DMA((len(entries),))],
        ids,
        pieces,
        0,
        name,
    )[0]


def diag_mask(heads, width, dtype):
    row = lax.broadcasted_iota(jnp.int32, (heads * HD, width), 0) // HD
    col = lax.broadcasted_iota(jnp.int32, (heads * HD, width), 1) // HD
    return jnp.where(row == col, 1.0, 0.0).astype(dtype)


def spread(block, heads, mask):
    return jnp.concatenate([block] * heads, axis=0) * mask


def fold(full, heads, lat, mask):
    full = full * mask
    total = full[:lat]
    for h in range(1, heads):
        total = total + full[h * lat : (h + 1) * lat]
    return total


def lane_roll(values, s, groups, cw):
    if s == 0:
        return values
    if cw % 128 == 0:
        cut = (groups - s) * cw
        return jnp.concatenate([values[:, cut:], values[:, :cut]], axis=1)
    return pltpu.roll(values, s * cw, 1)


def project_kernel(groups, cw, imgs, step, lat, ids, src, nlat, w, q, k, stats):
    heads = cw // HD
    for j in range(groups):
        k[:, j * cw : (j + 1) * cw] = dot(src[...], w[j, :, cw : 2 * cw]).astype(BF)
        q[:, j * cw : (j + 1) * cw] = (dot(nlat[...], w[j, :, :cw]) * (HD**-0.5)).astype(BF)
    mask = diag_mask(heads, cw, BF)
    for i in range(imgs):
        for j in range(groups):
            cols = slice(j * cw, (j + 1) * cw)
            qbd = spread(q[i * lat : (i + 1) * lat, cols], heads, mask)
            score = dot(k[i * step : (i + 1) * step, cols], qbd, NT)
            top = jnp.max(score, axis=0, keepdims=True)
            stats[i, 0:1, cols] = top
            stats[i, 1:2, cols] = jnp.sum(jnp.exp(score - top), axis=0, keepdims=True)


def values_kernel(groups, cw, ids, src, w, v):
    for j in range(groups):
        v[:, j * cw : (j + 1) * cw] = dot(src[...], columns(w, j, cw, 2)).astype(BF)


def send_rows(groups, share, ids, scratch, i, keep, send):
    for s in range(groups):
        start = pl.multiple_of(lax.rem(ids[0] + s, groups) * share, share)
        rows = scratch[pl.ds(start, share), :]
        if s == 0:
            keep[i * share : (i + 1) * share, :] = rows
        else:
            send[s - 1, i * share : (i + 1) * share, :] = rows.astype(BF)


def mix_kernel(groups, cw, imgs, step, lat, share, ids, q, k, v, lse, keep, send, scratch):
    heads = cw // HD
    mask, fmask = diag_mask(heads, cw, BF), diag_mask(heads, cw, F32)
    for i in range(imgs):
        rows = slice(i * step, (i + 1) * step)
        for j in range(groups):
            cols = slice(j * cw, (j + 1) * cw)
            qbd = spread(q[i * lat : (i + 1) * lat, cols], heads, mask)
            probs = jnp.exp(dot(k[rows, cols], qbd, NT) - lse[i, 0:1, cols])
            full = dot(probs.astype(BF), v[rows, cols], TN)
            scratch[i, :, cols] = fold(full, heads, lat, fmask)
        send_rows(groups, share, ids, scratch.at[i], i, keep, send)


def back_probs_kernel(groups, cw, imgs, step, lat, share, ids, q, k, v, lse, grad_keep, *refs):
    recv, (gv, grad_all, delta, scratch) = refs[: groups - 1], refs[groups - 1 :]
    heads = cw // HD
    mask = diag_mask(heads, cw, BF)
    for i in range(imgs):
        for s in range(groups):
            start = pl.multiple_of(lax.rem(ids[0] + s, groups) * share, share)
            block = grad_keep if s == 0 else recv[s - 1]
            block = lane_roll(block[i * share : (i + 1) * share, :].astype(F32), s, groups, cw)
            scratch[i, pl.ds(start, share), :] = block
        grad_all[i * lat : (i + 1) * lat, :] = scratch[i].astype(BF)
        rows = slice(i * step, (i + 1) * step)
        for j in range(groups):
            cols = slice(j * cw, (j + 1) * cw)
            qbd = spread(q[i * lat : (i + 1) * lat, cols], heads, mask)
            gbd = spread(grad_all[i * lat : (i + 1) * lat, cols], heads, mask)
            probs = jnp.exp(dot(k[rows, cols], qbd, NT) - lse[i, 0:1, cols])
            delta[i, 0:1, cols] = jnp.sum(probs * dot(v[rows, cols], gbd, NT), axis=0, keepdims=True)
            gv[rows, cols] = dot(probs.astype(BF), gbd).astype(BF)


def back_scores_kernel(
    groups, cw, imgs, step, lat, share, ids, q, k, v, lse, grad_all, delta, gk, gq, keep, send, scratch
):
    heads = cw // HD
    mask, fmask = diag_mask(heads, cw, BF), diag_mask(heads, cw, F32)
    for i in range(imgs):
        rows = slice(i * step, (i + 1) * step)
        for j in range(groups):
            cols = slice(j * cw, (j + 1) * cw)
            qbd = spread(q[i * lat : (i + 1) * lat, cols], heads, mask)
            gbd = spread(grad_all[i * lat : (i + 1) * lat, cols], heads, mask)
            probs = jnp.exp(dot(k[rows, cols], qbd, NT) - lse[i, 0:1, cols])
            grad = dot(v[rows, cols], gbd, NT) - delta[i, 0:1, cols]
            grad = (probs * grad).astype(BF)
            gk[rows, cols] = dot(grad, qbd).astype(BF)
            full = dot(grad, k[rows, cols], TN)
            scratch[i, :, cols] = fold(full, heads, lat, fmask) * (HD**-0.5)
        gq[i * lat : (i + 1) * lat, :] = scratch[i].astype(BF)
        send_rows(groups, share, ids, scratch.at[i], i, keep, send)


def middle_kernel(groups, cw, ids, keep, *refs):
    recv = refs[: groups - 1]
    latents, w, gain, bias = refs[groups - 1 : groups + 3]
    mixed, middle, normed = refs[-3:]
    total = keep[...]
    for s in range(1, groups):
        total = total + lane_roll(recv[s - 1][...].astype(F32), s, groups, cw)
    low = total.astype(BF)
    mixed[...] = low
    value = latents[...].astype(F32).reshape(middle.shape)
    for j in range(groups):
        value = value + dot(low[:, j * cw : (j + 1) * cw], columns(w, j, cw, 3), NT)
    middle[...] = value
    xhat, _ = norm_parts(value)
    normed[...] = (xhat * gain[...] + bias[...]).astype(BF)


def gelu_parts(value):
    cdf = 0.5 * (1.0 + lax.erf(value * (0.5**0.5)))
    pdf = jnp.exp(value * value * -0.5) * 0.3989422804014327
    return value * cdf, cdf + value * pdf


def forward_kernel(terms, ids, *refs):
    normed, final = refs[:terms], refs[terms : 2 * terms]
    up, down, hidden, up_low, ff, mid, normed_t = refs[2 * terms : 2 * terms + 7]
    normed_all, final_all, ff_total, mid_total = refs[2 * terms + 7 :]
    step = pl.program_id(0)

    @pl.when(step == 0)
    def _():
        at = 0
        for left, right in zip(normed, final):
            normed_all[at : at + left.shape[0], :] = left[...]
            final_all[at : at + left.shape[0], :] = right[...]
            at += left.shape[0]

    act, slope = gelu_parts(dot(normed_all[...], up[...]))
    low = act.astype(BF)
    hidden[...] = low
    ff_part = dot(low, down[...], NT)
    low = (dot(final_all[...], down[...]) * slope).astype(BF)
    up_low[...] = low
    mid_part = dot(low, up[...], NT)
    last = pl.num_programs(0) - 1
    width = normed_t.shape[0]
    normed_t[...] = normed_all[:, pl.ds(pl.multiple_of(step * width, width), width)].T

    @pl.when(step == 0)
    def _():
        ff_total[...] = ff_part
        mid_total[...] = mid_part

    @pl.when(step > 0)
    def _():
        ff_total[...] += ff_part
        mid_total[...] += mid_part

    @pl.when(step == last)
    def _():
        ff[...] = ff_total[...].astype(BF)
        mid[...] = mid_total[...].astype(BF)


def middle_back_kernel(groups, cw, ids, part, *refs):
    recv = refs[: groups - 1]
    middle, final, w, gain, grad_mid, mid_low, grad_mixed, gains = refs[groups - 1 :]
    total = part[...].astype(F32)
    for other in recv:
        total = total + other[...].astype(F32)
    back, terms = norm_back(middle[...], gain[...], total)
    gains[0:1, :] = jnp.sum(terms, axis=0, keepdims=True)
    gains[1:2, :] = jnp.sum(total, axis=0, keepdims=True)
    value = final[...].astype(F32) + back
    grad_mid[...] = value
    low = value.astype(BF)
    mid_low[...] = low.T
    for j in range(groups):
        grad_mixed[:, j * cw : (j + 1) * cw] = dot(low, columns(w, j, cw, 3)).astype(BF)


def weight_grad_kernel(terms, rows, ids, *refs):
    left, right, outs = refs[:terms], refs[terms : 2 * terms], refs[2 * terms :]
    value = dot(left[0][...], right[0][...])
    for a, b in zip(left[1:], right[1:]):
        value = value + dot(a[...], b[...])
    if len(outs) == 1:
        outs[0][...] = value.astype(BF)
    else:
        keep, send, total = outs
        total[...] = value
        split_rows(rows, ids, total, keep, send)


def split_rows(rows, ids, total, keep, send):
    for b in range(keep.shape[0]):
        for ref, core in ((keep, ids[3]), (send, 1 - ids[3])):
            start = pl.multiple_of((b * 2 + core) * rows, rows)
            ref[b] = total[pl.ds(start, rows), :].astype(BF)


def weight_grad(ids, left, right, rows, block, split, name):
    depth, width = left[0].shape[0], right[0].shape[1]
    if split:
        outs = [struct((depth // rows // 2, rows, width), BF)] * 2
        spec = pl.BlockSpec((depth // rows // 2, rows, block), lambda i, *_: (0, 0, i))
        specs, scratch = [spec, spec], [pltpu.VMEM((depth, block), F32)]
    else:
        outs = [struct((depth, width), BF)]
        specs, scratch = [pl.BlockSpec((depth, block), lambda i, *_: (0, i))], []
    return call(
        functools.partial(weight_grad_kernel, len(left), rows),
        (width // block,),
        [whole(a) for a in left]
        + [pl.BlockSpec((a.shape[0], block), lambda i, *_: (0, i)) for a in right],
        specs,
        outs,
        scratch,
        ids,
        left + right,
        2 * sum(a.shape[0] for a in right) * depth * width,
        name,
    )


def sum_grad_kernel(plan, rows, ids, *refs):
    keep, send, total = refs[2 * sum(terms for _, _, terms in plan) :]
    first = 0
    for at, width, terms in plan:
        value = dot(refs[first][...], refs[first + 1][...])
        for k in range(first + 2, first + 2 * terms, 2):
            value = value + dot(refs[k][...], refs[k + 1][...])
        total[:, at : at + width] = value
        first += 2 * terms
    split_rows(rows, ids, total, keep, send)


def sum_grad(ids, results, rows, depth, name):
    blocks = max(1, 256 // rows)
    plan, specs, args, at, flops = [], [], [], 0, 0
    for terms in results:
        for left, right in terms:
            size, width = right.shape
            specs.append(pl.BlockSpec((blocks * 2 * rows, size), lambda i, ids: (i, 0)))
            specs.append(whole(right))
            args += [left, right]
            flops += 2 * size * width * depth
        plan.append((at, width, len(terms)))
        at += width
    spec = pl.BlockSpec((blocks, rows, at), lambda i, ids: (i, 0, 0))
    return call(
        functools.partial(sum_grad_kernel, plan, rows),
        (depth // (blocks * 2 * rows),),
        specs,
        [spec, spec],
        [struct((depth // rows // 2, rows, at), BF)] * 2,
        [pltpu.VMEM((blocks * 2 * rows, at), F32)],
        ids,
        args,
        flops,
        name,
    )


def source_back_kernel(
    groups, cw, imgs, patch, share, ids, live, gk, gv, wk, wv, media, latents, cot, keep, *refs
):
    recv, refs = refs[: groups - 1], refs[groups - 1 :]
    grad_mid, m_gain, l_gain, media_grad, latent_grad, gains, total, lat_total, query = refs
    base = pl.program_id(0) * imgs
    step = patch + share
    value = dot(gk[:, :cw], wk[0, :, cw : 2 * cw], NT) + dot(gv[:, :cw], columns(wv, 0, cw, 2), NT)
    for j in range(1, groups):
        cols = slice(j * cw, (j + 1) * cw)
        value = value + dot(gk[:, cols], wk[j, :, cw : 2 * cw], NT)
        value = value + dot(gv[:, cols], columns(wv, j, cw, 2), NT)
    total[...] = value
    asked = keep[...]
    for s in range(1, groups):
        asked = asked + lane_roll(recv[s - 1][...].astype(F32), s, groups, cw)
    query[...] = asked.astype(BF)
    value = dot(query[:, :cw], wk[0, :, :cw], NT)
    for j in range(1, groups):
        value = value + dot(query[:, j * cw : (j + 1) * cw], wk[j, :, :cw], NT)
    lat_total[...] = value

    @pl.when(pl.program_id(0) == 0)
    def _():
        gains[...] = jnp.zeros_like(gains)

    sums = [0.0] * 4
    for i in range(imgs):
        grad = total[i * step : i * step + patch, :]
        back, terms = norm_back(media[i].astype(F32), m_gain[...], grad)
        media_grad[i] = back
        sums[0] += fold_rows(terms)
        sums[1] += fold_rows(grad)
        rows = slice(i * share, (i + 1) * share)
        grad = total[i * step + patch : (i + 1) * step, :] + lat_total[rows, :]
        back, terms = norm_back(latents[i].astype(F32), l_gain[...], grad)
        sums[2] += fold_rows(terms)
        sums[3] += fold_rows(grad)
        latent_grad[i] = jnp.where(
            live[base + i] > 0, grad_mid[rows, :] + back, cot[i].astype(F32)
        )
    for k in range(4):
        gains[k : k + 1, :] += jnp.sum(sums[k], axis=0, keepdims=True)


def make_local(depth_z, groups):
    dp_size = depth_z * 4

    def from_dp(value, s=0, yf=0, cf=0):
        pairs = []
        for dst in range(dp_size):
            z, y, c = dst // 4, dst // 2 % 2, dst % 2
            pairs.append(((z + s) % depth_z * 4 + (y ^ yf) * 2 + (c ^ cf), dst))
        return lax.ppermute(value, "dp", pairs)

    def flip_z(value, bit):
        pairs = [(((dst // 4) ^ bit) * 4 + dst % 4, dst) for dst in range(dp_size)]
        return lax.ppermute(value, "dp", pairs)

    def from_head(value, s):
        return lax.ppermute(value, "head", [((x + s) % groups, x) for x in range(groups)])

    def to_head(value, s):
        return lax.ppermute(value, "head", [(x, (x + s) % groups) for x in range(groups)])

    def plane(value, sx, yf, back, cf=0):
        pairs = []
        for dst in range(dp_size):
            for x in range(groups):
                other = (dst ^ (2 * yf + cf)) * groups + (x + sx) % groups
                mine = dst * groups + x
                pairs.append((mine, other) if back else (other, mine))
        return lax.ppermute(value, ("dp", "head"), pairs)

    others = [(sx, yf) for sx in range(groups) for yf in range(2) if sx or yf]

    def local(
        media_tokens,
        latents,
        cotangent,
        image_counts,
        media_gain,
        media_bias,
        latent_gain,
        latent_bias,
        ff_gain,
        ff_bias,
        w_query,
        w_keyval,
        w_attn_out,
        w_up,
        w_down,
    ):
        images, patches, width = media_tokens.shape
        lat = latents.shape[1]
        rows, cw = w_query.shape
        units = w_up.shape[1]
        patch, share = patches // groups, lat // groups
        step = patch + share
        heads_w = cw * groups
        me = lax.axis_index("head").astype(jnp.int32)
        place = lax.axis_index("dp").astype(jnp.int32)
        z, y, c = place // 4, place // 2 % 2, place % 2
        ids = jnp.stack([me, z, y, c])
        live = (jnp.arange(images, dtype=jnp.int32) < jnp.sum(image_counts)).astype(jnp.int32)
        gains = [
            g.reshape(1, width)
            for g in (media_gain, media_bias, latent_gain, latent_bias, ff_gain, ff_bias)
        ]
        media4 = media_tokens.reshape(images, groups, patch, width)
        lat4 = latents.reshape(images, groups, share, width)
        cot4 = cotangent.reshape(images, groups, share, width)

        part = images // CHUNKS
        own = part * share

        shard = jnp.concatenate([w_query, w_keyval[:, 0], w_keyval[:, 1], w_attn_out.T], axis=1)
        got = [from_dp(shard, s) for s in range(1, depth_z)]
        w_up_all = lax.all_gather(w_up, "dp", axis=0, tiled=True)
        w_down_all = lax.all_gather(w_down.T, "dp", axis=0, tiled=True)
        live_low = live.astype(BF).reshape(images, 1, 1)
        final4 = [
            lax.dynamic_index_in_dim(cot4, (me + s) % groups, 1, keepdims=False) * live_low
            for s in range(groups)
        ]
        final4 = jnp.stack(final4).reshape(groups, images * share, width)
        own_t = final4[0].T
        away_t = final4[1:].reshape((groups - 1) * images * share, width).T
        final4, own_t, away_t = tie((final4, own_t, away_t), shard)
        line = jnp.stack([shard] + tie(got, final4, own_t, away_t))
        parts = {(0, 0): line} | {at: plane(line, *at, False) for at in others}

        imgs = math.gcd(images, math.lcm(128, step) // step)
        src, nlat, src_t, nlat_t = call(
            functools.partial(norm_kernel, imgs, lat, share, patch),
            (images // imgs,),
            [
                pl.BlockSpec((imgs, None, patch, width), lambda i, ids: (i, ids[0], 0, 0)),
                images_of(imgs, lat, width),
            ]
            + [whole(gains[0])] * 4,
            [
                rows_of(imgs * step, width),
                rows_of(imgs * lat, width),
                pl.BlockSpec((width, imgs * step), lambda i, ids: (0, i)),
                pl.BlockSpec((width, imgs * lat), lambda i, ids: (0, i)),
            ],
            [
                struct((images * step, width), BF),
                struct((images * lat, width), BF),
                struct((width, images * step), BF),
                struct((width, images * lat), BF),
            ],
            [pltpu.VMEM((lat, width), F32)],
            tie(ids, line),
            [media4, latents] + gains[:4],
            images * step * width * 12,
            "input_norms",
        )

        pieces, entries = [], []
        for (sx, yf), part_of in parts.items():
            for cf, piece in ((0, part_of), (1, from_dp(tie(part_of, src), cf=1))):
                for s in range(depth_z):
                    entries.append((len(pieces), s, sx, s, yf, cf))
                pieces.append(piece)
        w_attn = assemble(entries, pieces, depth_z, ids, rows, groups, 4 * cw, "place_attn")

        imgs = 4
        attn_macs = images * step * lat * heads_w
        q, k, stats = call(
            functools.partial(project_kernel, groups, cw, imgs, step, lat),
            (images // imgs,),
            [rows_of(imgs * step, width), rows_of(imgs * lat, width), third(w_attn, 2 * cw, 0)],
            [
                rows_of(imgs * lat, heads_w),
                rows_of(imgs * step, heads_w),
                images_of(imgs, 2, heads_w),
            ],
            [
                struct((images * lat, heads_w), BF),
                struct((images * step, heads_w), BF),
                struct((images, 2, heads_w), F32),
            ],
            [],
            ids,
            [src, nlat, w_attn],
            2 * images * (step * width * heads_w + lat * width * heads_w) + 8 * attn_macs,
            "project",
        )
        tops, sums = [stats[:, :1]], [stats[:, 1:]]
        for s in range(1, groups):
            other = jnp.roll(from_head(stats, s), s * cw, axis=2)
            tops.append(other[:, :1])
            sums.append(other[:, 1:])
        v = call(
            functools.partial(values_kernel, groups, cw),
            (images // imgs,),
            [rows_of(imgs * step, width), third(w_attn, cw, 2)],
            [rows_of(imgs * step, heads_w)],
            [struct((images * step, heads_w), BF)],
            [],
            tie(ids, q),
            [src, w_attn],
            2 * images * step * width * heads_w,
            "values",
        )[0]
        top = functools.reduce(jnp.maximum, tops)
        lse = top + jnp.log(sum(t * jnp.exp(m - top) for m, t in zip(tops, sums)))

        imgs = min(imgs, part)
        count = part // imgs

        def attn_specs(ch):
            return [
                rows_of(imgs * lat, heads_w, ch * count),
                rows_of(imgs * step, heads_w, ch * count),
                rows_of(imgs * step, heads_w, ch * count),
                images_of(imgs, 1, heads_w, ch * count),
            ]

        row_sends = [
            rows_of(imgs * share, heads_w),
            pl.BlockSpec((groups - 1, imgs * share, heads_w), lambda i, ids: (0, i, 0)),
        ]
        row_outs = [struct((own, heads_w), F32), struct((groups - 1, own, heads_w), BF)]

        def exchanged(keep, send):
            return [keep] + [to_head(send[s - 1], s) for s in range(groups - 1, 0, -1)]

        mixes, normed, mixed, middle = [], [], None, None
        for ch in range(CHUNKS):
            keep, send = call(
                functools.partial(mix_kernel, groups, cw, imgs, step, lat, share),
                (count,),
                attn_specs(ch),
                row_sends,
                row_outs,
                [pltpu.VMEM((imgs, lat, heads_w), F32)],
                tie(ids, [a[0] for a in mixes]),
                [q, k, v, lse],
                8 * attn_macs / CHUNKS,
                f"mix{ch}",
            )
            mixes.append(exchanged(keep, send))
        for ch in range(CHUNKS):
            lat_spec = pl.BlockSpec(
                (part, None, share, width), lambda i, ids, ch=ch: (ch, ids[0], 0, 0)
            )
            outs = call(
                functools.partial(middle_kernel, groups, cw),
                (1,),
                [whole(a) for a in mixes[ch]]
                + [lat_spec, third(w_attn, cw, 3), whole(gains[4]), whole(gains[5])]
                + ([anywhere()] * 2 if ch else []),
                [fixed_rows(own, heads_w, ch), fixed_rows(own, width, ch), fixed_rows(own, width)],
                [
                    struct((CHUNKS * own, heads_w), BF),
                    struct((CHUNKS * own, width), F32),
                    struct((own, width), BF),
                ],
                [],
                tie(ids, [a[0] for a in normed]),
                mixes[ch] + [lat4, w_attn, gains[4], gains[5]] + ([mixed, middle] if ch else []),
                2 * own * heads_w * width,
                f"middle{ch}",
                {groups + 4: 0, groups + 5: 1} if ch else None,
            )
            mixed, middle = outs[:2]
            normed.append([outs[2]] + [from_head(outs[2], s) for s in range(1, groups)])
        block = min(512, units)

        def feed_forward(terms, ids, name):
            size = len(terms) * own
            return call(
                functools.partial(forward_kernel, len(terms)),
                (units // block,),
                [whole(a) for a, _ in terms]
                + [spec for _, spec in terms]
                + [
                    pl.BlockSpec((width, block), lambda i, ids: (0, i)),
                    pl.BlockSpec((width, block), lambda i, ids: (0, i)),
                ],
                [pl.BlockSpec((size, block), lambda i, ids: (0, i))] * 2
                + [fixed_rows(size, width)] * 2
                + [pl.BlockSpec((width * block // units, size), lambda i, ids: (i, 0))],
                [struct((size, units), BF)] * 2
                + [struct((size, width), BF)] * 2
                + [struct((width, size), BF)],
                [pltpu.VMEM((size, width), BF)] * 2 + [pltpu.VMEM((size, width), F32)] * 2,
                ids,
                [a for a, _ in terms] + [final4] * len(terms) + [w_up_all, w_down_all],
                8 * size * width * units,
                name,
            )

        def final_rows(s, ch):
            return pl.BlockSpec((None, own, width), lambda *_: (s, ch, 0))

        size = CHUNKS * own
        away_ff = feed_forward(
            [(normed[ch][t], final_rows(t, ch)) for t in range(1, groups) for ch in range(CHUNKS)],
            ids,
            "feed_forward_away",
        )
        ff_back, mid_back = [a.reshape(groups - 1, size, width) for a in away_ff[2:4]]
        mid_back = [to_head(mid_back[s - 1], s) for s in range(groups - 1, 0, -1)]
        own_ff = feed_forward(
            [(normed[ch][0], final_rows(0, ch)) for ch in range(CHUNKS)],
            tie(ids, away_ff),
            "feed_forward_own",
        )

        def pick(block, index, axis=0):
            return lax.dynamic_index_in_dim(block, index, axis, keepdims=False).astype(F32)

        def lanes(block, cols):
            if len(cols) == 1 and cols[0] == slice(0, block.shape[-1]):
                return block
            return jnp.concatenate([block[..., c] for c in cols], axis=-1)

        class Sum:
            def __init__(self, keep, recv, cols):
                self.cols = cols
                self.grid = [a.reshape((depth_z, 2) + a.shape[1:]) for a in (keep, recv)]
                self.crossed, self.near = [], []

            def at(self, sx, yy):
                terms = [pick(lanes(a, self.cols[sx]), yy, 1) for a in self.grid]
                return sum(terms + [pick(a, yy, 1) for a in self.crossed])

            def cross(self, late):
                grid = tie(self.grid, late)
                self.away = [
                    sum(lanes(a, self.cols[sx]).astype(F32) for a in grid).astype(BF)
                    for sx in range(1, groups)
                ]
                return self.away

            def across(self):
                self.crossed = [to_head(a, sx) for sx, a in zip(range(1, groups), self.away)]

            def second(self, routes, late=()):
                self.grid, self.crossed = tie((self.grid, self.crossed), late)
                self.routes = routes
                self.away = [self.at(sx, y ^ yf).astype(BF) for sx, yf in routes]
                return self.away

            def sent(self):
                self.near = [plane(a, *to, True) for a, to in zip(self.away, self.routes)]

            def start_z(self):
                base = self.at(0, y)

                def block(zz):
                    return pick(base, zz) + sum(pick(a, zz) for a in self.near)

                self.block, self.left, self.bit = block, depth_z, 1

            def halve(self, late=()):
                turn = tie(z, late)
                mine, block = z // self.bit % 2, self.block
                away_at = 1 - turn // self.bit % 2
                self.left //= 2
                self.held = lambda k: block(2 * k + mine)
                away = [block(2 * k + away_at) for k in range(self.left)]
                self.away = jnp.stack(away).astype(BF)
                return self.away

            def halved(self, late=()):
                near, held = tie(flip_z(self.away, self.bit), late), self.held
                self.block, self.bit = (lambda k: held(k) + pick(near, k)), 2 * self.bit

            def rest(self):
                while self.left > 1:
                    self.halve()
                    self.halved()
                return self.block(0)

            def third(self):
                self.start_z()
                self.away = [self.block((z + s) % depth_z).astype(BF) for s in range(1, depth_z)]
                return self.away

            def last(self):
                got = [from_dp(a, depth_z - s) for s, a in zip(range(1, depth_z), self.away)]
                return self.block(z) + sum(a.astype(F32) for a in got)

        along_y = [(0, 1)]

        def groups_of(*starts):
            return [[slice(a + sx * cw, a + (sx + 1) * cw) for a in starts] for sx in range(groups)]

        up_part = weight_grad(
            tie(ids, own_ff[0]),
            [own_ff[4], away_ff[4]],
            [own_ff[1], away_ff[1]],
            rows,
            block,
            False,
            "grad_up",
        )[0]
        grad_mid, mid_low_t, grad_mixed, ff_gains = call(
            functools.partial(middle_back_kernel, groups, cw),
            (1,),
            [whole(own_ff[3])]
            + [whole(t) for t in mid_back]
            + [whole(middle), pl.BlockSpec((None, size, width), lambda *_: (0, 0, 0))]
            + [third(w_attn, cw, 3), whole(gains[4])],
            [
                fixed_rows(size, width),
                fixed_rows(width, size),
                fixed_rows(size, heads_w),
                fixed_rows(2, width),
            ],
            [
                struct((size, width), F32),
                struct((width, size), BF),
                struct((size, heads_w), BF),
                struct((2, width), F32),
            ],
            [],
            tie(ids, up_part),
            [own_ff[3]] + mid_back + [middle, final4, w_attn, gains[4]],
            2 * size * heads_w * width,
            "middle_back",
        )
        grad_mixed = [grad_mixed] + [from_head(grad_mixed, s) for s in range(1, groups)]

        grad_up = lax.psum_scatter(tie(up_part, mid_back), "dp", scatter_dimension=0, tiled=True)
        down_parts = weight_grad(
            tie(ids, mid_low_t),
            [own_t, away_t],
            [own_ff[0], away_ff[0]],
            rows,
            block,
            True,
            "grad_down",
        )

        count = images // imgs
        gv, grad_all, delta = call(
            functools.partial(back_probs_kernel, groups, cw, imgs, step, lat, share),
            (count,),
            attn_specs(0) + [rows_of(imgs * share, heads_w)] * groups,
            [rows_of(imgs * step, heads_w), rows_of(imgs * lat, heads_w), images_of(imgs, 1, heads_w)],
            [
                struct((images * step, heads_w), BF),
                struct((images * lat, heads_w), BF),
                struct((images, 1, heads_w), F32),
            ],
            [pltpu.VMEM((imgs, lat, heads_w), F32)],
            tie(ids, down_parts[0]),
            [q, k, v, lse] + grad_mixed,
            12 * attn_macs,
            "back_probs",
        )
        recv = from_dp(tie(down_parts[1], gv), cf=1)
        sum_down = Sum(down_parts[0], recv, [[slice(0, units)]])
        ordered = jnp.roll(jnp.concatenate([own_ff[2][None], tie(ff_back, gv)]), me, axis=0)
        ff_sum = lax.psum_scatter(tie(ordered, grad_up), "head", scatter_dimension=0, tiled=True)[0]
        total = delta
        for s in range(1, groups):
            total = total + jnp.roll(from_head(delta, s), s * cw, axis=2)
        value_parts = sum_grad(
            tie(ids, gv),
            [[(mid_low_t, mixed)], [(src_t, gv)]],
            rows,
            width,
            "grad_out_values",
        )
        sum_value = Sum(value_parts[0], from_dp(value_parts[1], cf=1), groups_of(0, heads_w))
        gk, gq, keep, send = call(
            functools.partial(back_scores_kernel, groups, cw, imgs, step, lat, share),
            (count,),
            attn_specs(0) + [rows_of(imgs * lat, heads_w), images_of(imgs, 1, heads_w)],
            [rows_of(imgs * step, heads_w), rows_of(imgs * lat, heads_w)] + row_sends,
            [
                struct((images * step, heads_w), BF),
                struct((images * lat, heads_w), BF),
                struct((size, heads_w), F32),
                struct((groups - 1, size, heads_w), BF),
            ],
            [pltpu.VMEM((imgs, lat, heads_w), F32)],
            tie(ids, value_parts[0], sum_down.second(along_y, value_parts[0]), ordered),
            [q, k, v, lse, grad_all, total],
            16 * attn_macs,
            "back_scores",
        )
        sum_down.sent()
        query_terms = exchanged(keep, send)
        key_parts = sum_grad(
            tie(ids, gk, sum_value.cross(gk)),
            [[(src_t, gk)], [(nlat_t, gq)]],
            rows,
            width,
            "grad_query_keys",
        )
        sum_value.across()
        sum_down.start_z()
        sum_key = Sum(key_parts[0], from_dp(key_parts[1], cf=1), groups_of(0, heads_w))

        def share_rows(size):
            return pl.BlockSpec((imgs, None, size, width), lambda i, ids, live: (i, ids[0], 0, 0))

        before = [sum_key.second(others), sum_value.second(along_y), sum_down.halve()]
        media_grad, latent_grad, gain_terms = call(
            functools.partial(source_back_kernel, groups, cw, imgs, patch, share),
            (count,),
            [rows_of(imgs * step, heads_w)] * 2
            + [third(w_attn, 2 * cw, 0), third(w_attn, cw, 2)]
            + [share_rows(patch), share_rows(share), share_rows(share)]
            + [rows_of(imgs * share, heads_w)] * groups
            + [rows_of(imgs * share, width), whole(gains[0]), whole(gains[2])],
            [images_of(imgs, patch, width), images_of(imgs, share, width), fixed_rows(4, width)],
            [
                struct((images, patch, width), F32),
                struct((images, share, width), F32),
                struct((4, width), F32),
            ],
            [
                pltpu.VMEM((imgs * step, width), F32),
                pltpu.VMEM((imgs * share, width), F32),
                pltpu.VMEM((imgs * share, heads_w), BF),
            ],
            [tie(ids, before, grad_up), live],
            [gk, gv, w_attn, w_attn, media4, lat4, cot4]
            + query_terms
            + [grad_mid, gains[0], gains[2]],
            2 * images * step * width * 2 * heads_w,
            "source_back",
        )
        sum_key.sent()
        sum_value.sent()
        sum_key.near = tie(sum_key.near, media_grad)
        sum_value.near = tie(sum_value.near, media_grad)
        sum_down.halved(media_grad)
        last = [jnp.concatenate(pair, axis=1) for pair in zip(sum_key.third(), sum_value.third())]
        last = [from_dp(a, depth_z - s).astype(F32) for s, a in zip(range(1, depth_z), last)]
        query_key = sum_key.block(z) + sum(a[:, : 2 * cw] for a in last)
        out_value = sum_value.block(z) + sum(a[:, 2 * cw :] for a in last)

        final_lat = middle + ff_sum.astype(F32)
        final_lat = final_lat.reshape(images, share, width)
        lat_own = lax.dynamic_index_in_dim(lat4, me, 1, keepdims=False).astype(F32)
        latents_out = jnp.where(live[:, None, None] > 0, final_lat, lat_own)

        total = jnp.concatenate([gain_terms, ff_gains])
        grad_down = sum_down.rest()
        near = [from_dp(total, cf=1)] + [plane(total, *at, False) for at in others]
        near += [plane(total, *at, False, 1) for at in others]
        total = total + sum(near)
        norm_grads = total + sum(from_dp(total, s) for s in range(1, depth_z))

        return (
            latents_out,
            media_grad,
            latent_grad,
            query_key[:, cw:],
            jnp.stack([query_key[:, :cw], out_value[:, cw:]], axis=1),
            out_value[:, :cw].T,
            grad_up.astype(F32),
            grad_down.T,
            norm_grads,
        )

    return local


def solution(mesh):
    return jax.shard_map(
        make_local(mesh.shape["dp"] // 4, mesh.shape["head"]),
        mesh=mesh,
        in_specs=(
            P("dp", None, None),
            P("dp", None, None),
            P("dp", None, None),
            P("dp"),
            P(),
            P(),
            P(),
            P(),
            P(),
            P(),
            P("dp", "head"),
            P("dp", None, "head"),
            P("head", "dp"),
            P("dp", "head"),
            P("head", "dp"),
        ),
        out_specs=(
            P("dp", "head", None),
            P("dp", "head", None),
            P("dp", "head", None),
            P("dp", "head"),
            P("dp", None, "head"),
            P("head", "dp"),
            P("dp", "head"),
            P("head", "dp"),
            P(),
        ),
        check_vma=False,
    )
```

```python
import functools
import math

import jax
import jax.numpy as jnp
from jax import lax
from jax.experimental import pallas as pl
from jax.experimental.pallas import tpu as pltpu
from jax.sharding import PartitionSpec as P

HD = 64
HEADS = 8
CHUNKS = 2
EPS = 1e-05
BF = jnp.bfloat16
F32 = jnp.float32
MIB = 1024 * 1024
VMEM = 58
SMALL = 40
STREAMED = ("feed_forward_own", "feed_forward_away", "grad_up", "grad_down", "middle_back", "source_back")

NN = (((1,), (0,)), ((), ()))
NT = (((1,), (1,)), ((), ()))
TN = (((0,), (0,)), ((), ()))


def dot(left, right, form=NN):
    return lax.dot_general(left, right, form, preferred_element_type=F32)


def struct(shape, dtype):
    return jax.ShapeDtypeStruct(shape, dtype)


def call(kernel, grid, in_specs, out_specs, out_shape, scratch, ids, args, flops, name, alias=None):
    scalars = ids if isinstance(ids, (list, tuple)) else [ids]
    moved = sum(a.size * a.dtype.itemsize for a in args if a.ndim < 4)
    moved += sum(o.size * jnp.dtype(o.dtype).itemsize for o in out_shape)
    return pl.pallas_call(
        kernel,
        grid_spec=pltpu.PrefetchScalarGridSpec(
            num_scalar_prefetch=len(scalars),
            grid=grid,
            in_specs=in_specs,
            out_specs=out_specs,
            scratch_shapes=scratch,
        ),
        out_shape=out_shape,
        input_output_aliases={len(scalars) + k: v for k, v in (alias or {}).items()},
        compiler_params=pltpu.CompilerParams(
            vmem_limit_bytes=(VMEM if name in STREAMED else SMALL) * MIB,
            dimension_semantics=("arbitrary",) * len(grid)
        ),
        cost_estimate=pl.CostEstimate(
            flops=int(flops), bytes_accessed=int(moved), transcendentals=0
        ),
        name=name,
    )(*scalars, *args)


def whole(array):
    zeros = (0,) * array.ndim
    return pl.BlockSpec(array.shape, lambda *_: zeros)


def rows_of(block, width, first=0):
    return pl.BlockSpec((block, width), lambda i, *_: (i + first, 0))


def fixed_rows(block, width, at=0):
    return pl.BlockSpec((block, width), lambda *_: (at, 0))


def images_of(block, rows, width, first=0):
    return pl.BlockSpec((block, rows, width), lambda i, *_: (i + first, 0, 0))


def third(array, width, at):
    if width % 128:
        return whole(array)
    return pl.BlockSpec(array.shape[:2] + (width,), lambda *_: (0, 0, at))


def columns(ref, group, width, at):
    if ref.shape[2] == width:
        return ref[group]
    return ref[group, :, at * width : (at + 1) * width]


def anywhere():
    return pl.BlockSpec(memory_space=pl.ANY)


def tie(values, *first):
    flat, tree = jax.tree.flatten(values)
    out = lax.optimization_barrier(tuple(flat) + tuple(jax.tree.leaves(first)))
    return jax.tree.unflatten(tree, out[: len(flat)])


def norm_parts(values):
    centre = values - jnp.mean(values, axis=-1, keepdims=True)
    rstd = lax.rsqrt(jnp.mean(centre * centre, axis=-1, keepdims=True) + EPS)
    return centre * rstd, rstd


def norm_back(values, gain, grad):
    xhat, rstd = norm_parts(values)
    scaled = grad * gain
    first = jnp.mean(scaled, axis=-1, keepdims=True)
    second = jnp.mean(scaled * xhat, axis=-1, keepdims=True)
    return rstd * (scaled - first - xhat * second), grad * xhat


def fold_rows(value):
    return jnp.sum(value.reshape(value.shape[0] // 8, 8, value.shape[1]), axis=0)


def norm_kernel(
    imgs, lat, share, patch, ids, media, latents, m_gain, m_bias, l_gain, l_bias, *refs
):
    src, nlat, src_t, nlat_t, keep = refs
    start = pl.multiple_of(ids[0] * share, share)
    step = patch + share
    for i in range(imgs):
        xhat, _ = norm_parts(media[i].astype(F32))
        src[i * step : i * step + patch, :] = (xhat * m_gain[...] + m_bias[...]).astype(BF)
        xhat, _ = norm_parts(latents[i].astype(F32))
        normed = xhat * l_gain[...] + l_bias[...]
        nlat[i * lat : (i + 1) * lat, :] = normed.astype(BF)
        keep[...] = normed
        src[i * step + patch : (i + 1) * step, :] = keep[pl.ds(start, share), :].astype(BF)
    src_t[...] = src[...].T
    nlat_t[...] = nlat[...].T


def assemble(entries, pieces, depth, ids, rows, groups, width, name):
    def kernel(ids_ref, *refs):
        out, sems = refs[len(pieces)], refs[len(pieces) + 1]
        copies = []
        for e, (op, lead, group, s, yf, cf) in enumerate(entries):
            block = lax.rem(ids_ref[1] + s, depth) * 4
            block += lax.rem(ids_ref[2] + yf, 2) * 2 + lax.rem(ids_ref[3] + cf, 2)
            start = pl.multiple_of(block * rows, rows)
            source = refs[op] if lead is None else refs[op].at[lead]
            copies.append(
                pltpu.make_async_copy(source, out.at[group, pl.ds(start, rows), :], sems.at[e])
            )
        for copy in copies:
            copy.start()
        for copy in copies:
            copy.wait()

    return call(
        kernel,
        (1,),
        [anywhere()] * len(pieces),
        [pl.BlockSpec((groups, depth * 4 * rows, width), lambda *_: (0, 0, 0))],
        [struct((groups, depth * 4 * rows, width), BF)],
        [pltpu.SemaphoreType.DMA((len(entries),))],
        ids,
        pieces,
        0,
        name,
    )[0]


def diag_mask(heads, width, dtype):
    row = lax.broadcasted_iota(jnp.int32, (heads * HD, width), 0) // HD
    col = lax.broadcasted_iota(jnp.int32, (heads * HD, width), 1) // HD
    return jnp.where(row == col, 1.0, 0.0).astype(dtype)


def spread(block, heads, mask):
    return jnp.concatenate([block] * heads, axis=0) * mask


def fold(full, heads, lat, mask):
    full = full * mask
    total = full[:lat]
    for h in range(1, heads):
        total = total + full[h * lat : (h + 1) * lat]
    return total


def lane_roll(values, s, groups, cw):
    if s == 0:
        return values
    if cw % 128 == 0:
        cut = (groups - s) * cw
        return jnp.concatenate([values[:, cut:], values[:, :cut]], axis=1)
    return pltpu.roll(values, s * cw, 1)


def project_kernel(groups, cw, imgs, step, lat, ids, src, nlat, w, q, k, stats):
    heads = cw // HD
    for j in range(groups):
        k[:, j * cw : (j + 1) * cw] = dot(src[...], w[j, :, cw : 2 * cw]).astype(BF)
        q[:, j * cw : (j + 1) * cw] = (dot(nlat[...], w[j, :, :cw]) * (HD**-0.5)).astype(BF)
    mask = diag_mask(heads, cw, BF)
    for i in range(imgs):
        for j in range(groups):
            cols = slice(j * cw, (j + 1) * cw)
            qbd = spread(q[i * lat : (i + 1) * lat, cols], heads, mask)
            score = dot(k[i * step : (i + 1) * step, cols], qbd, NT)
            top = jnp.max(score, axis=0, keepdims=True)
            stats[i, 0:1, cols] = top
            stats[i, 1:2, cols] = jnp.sum(jnp.exp(score - top), axis=0, keepdims=True)


def values_kernel(groups, cw, ids, src, w, v):
    for j in range(groups):
        v[:, j * cw : (j + 1) * cw] = dot(src[...], columns(w, j, cw, 2)).astype(BF)


def send_rows(groups, share, ids, scratch, i, keep, send):
    for s in range(groups):
        start = pl.multiple_of(lax.rem(ids[0] + s, groups) * share, share)
        rows = scratch[pl.ds(start, share), :]
        if s == 0:
            keep[i * share : (i + 1) * share, :] = rows
        else:
            send[s - 1, i * share : (i + 1) * share, :] = rows.astype(BF)


def mix_kernel(groups, cw, imgs, step, lat, share, ids, q, k, v, lse, keep, send, scratch):
    heads = cw // HD
    mask, fmask = diag_mask(heads, cw, BF), diag_mask(heads, cw, F32)
    for i in range(imgs):
        rows = slice(i * step, (i + 1) * step)
        for j in range(groups):
            cols = slice(j * cw, (j + 1) * cw)
            qbd = spread(q[i * lat : (i + 1) * lat, cols], heads, mask)
            probs = jnp.exp(dot(k[rows, cols], qbd, NT) - lse[i, 0:1, cols])
            full = dot(probs.astype(BF), v[rows, cols], TN)
            scratch[i, :, cols] = fold(full, heads, lat, fmask)
        send_rows(groups, share, ids, scratch.at[i], i, keep, send)


def back_probs_kernel(groups, cw, imgs, step, lat, share, ids, q, k, v, lse, grad_keep, *refs):
    recv, (gv, grad_all, delta, scratch) = refs[: groups - 1], refs[groups - 1 :]
    heads = cw // HD
    mask = diag_mask(heads, cw, BF)
    for i in range(imgs):
        for s in range(groups):
            start = pl.multiple_of(lax.rem(ids[0] + s, groups) * share, share)
            block = grad_keep if s == 0 else recv[s - 1]
            block = lane_roll(block[i * share : (i + 1) * share, :].astype(F32), s, groups, cw)
            scratch[i, pl.ds(start, share), :] = block
        grad_all[i * lat : (i + 1) * lat, :] = scratch[i].astype(BF)
        rows = slice(i * step, (i + 1) * step)
        for j in range(groups):
            cols = slice(j * cw, (j + 1) * cw)
            qbd = spread(q[i * lat : (i + 1) * lat, cols], heads, mask)
            gbd = spread(grad_all[i * lat : (i + 1) * lat, cols], heads, mask)
            probs = jnp.exp(dot(k[rows, cols], qbd, NT) - lse[i, 0:1, cols])
            delta[i, 0:1, cols] = jnp.sum(probs * dot(v[rows, cols], gbd, NT), axis=0, keepdims=True)
            gv[rows, cols] = dot(probs.astype(BF), gbd).astype(BF)


def back_scores_kernel(
    groups, cw, imgs, step, lat, share, ids, q, k, v, lse, grad_all, delta, gk, gq, keep, send, scratch
):
    heads = cw // HD
    mask, fmask = diag_mask(heads, cw, BF), diag_mask(heads, cw, F32)
    for i in range(imgs):
        rows = slice(i * step, (i + 1) * step)
        for j in range(groups):
            cols = slice(j * cw, (j + 1) * cw)
            qbd = spread(q[i * lat : (i + 1) * lat, cols], heads, mask)
            gbd = spread(grad_all[i * lat : (i + 1) * lat, cols], heads, mask)
            probs = jnp.exp(dot(k[rows, cols], qbd, NT) - lse[i, 0:1, cols])
            grad = dot(v[rows, cols], gbd, NT) - delta[i, 0:1, cols]
            grad = (probs * grad).astype(BF)
            gk[rows, cols] = dot(grad, qbd).astype(BF)
            full = dot(grad, k[rows, cols], TN)
            scratch[i, :, cols] = fold(full, heads, lat, fmask) * (HD**-0.5)
        gq[i * lat : (i + 1) * lat, :] = scratch[i].astype(BF)
        send_rows(groups, share, ids, scratch.at[i], i, keep, send)


def middle_kernel(groups, cw, ids, keep, *refs):
    recv = refs[: groups - 1]
    latents, w, gain, bias = refs[groups - 1 : groups + 3]
    mixed, middle, normed = refs[-3:]
    total = keep[...]
    for s in range(1, groups):
        total = total + lane_roll(recv[s - 1][...].astype(F32), s, groups, cw)
    low = total.astype(BF)
    mixed[...] = low
    value = latents[...].astype(F32).reshape(middle.shape)
    for j in range(groups):
        value = value + dot(low[:, j * cw : (j + 1) * cw], columns(w, j, cw, 3), NT)
    middle[...] = value
    xhat, _ = norm_parts(value)
    normed[...] = (xhat * gain[...] + bias[...]).astype(BF)


def gelu_parts(value):
    cdf = 0.5 * (1.0 + lax.erf(value * (0.5**0.5)))
    pdf = jnp.exp(value * value * -0.5) * 0.3989422804014327
    return value * cdf, cdf + value * pdf


def forward_kernel(terms, ids, *refs):
    normed, final = refs[:terms], refs[terms : 2 * terms]
    up, down, hidden, up_low, ff, mid, normed_t = refs[2 * terms : 2 * terms + 7]
    normed_all, final_all, ff_total, mid_total = refs[2 * terms + 7 :]
    step = pl.program_id(0)

    @pl.when(step == 0)
    def _():
        at = 0
        for left, right in zip(normed, final):
            normed_all[at : at + left.shape[0], :] = left[...]
            final_all[at : at + left.shape[0], :] = right[...]
            at += left.shape[0]

    act, slope = gelu_parts(dot(normed_all[...], up[...]))
    low = act.astype(BF)
    hidden[...] = low
    ff_part = dot(low, down[...], NT)
    low = (dot(final_all[...], down[...]) * slope).astype(BF)
    up_low[...] = low
    mid_part = dot(low, up[...], NT)
    last = pl.num_programs(0) - 1
    width = normed_t.shape[0]
    normed_t[...] = normed_all[:, pl.ds(pl.multiple_of(step * width, width), width)].T

    @pl.when(step == 0)
    def _():
        ff_total[...] = ff_part
        mid_total[...] = mid_part

    @pl.when(step > 0)
    def _():
        ff_total[...] += ff_part
        mid_total[...] += mid_part

    @pl.when(step == last)
    def _():
        ff[...] = ff_total[...].astype(BF)
        mid[...] = mid_total[...].astype(BF)


def middle_back_kernel(groups, cw, ids, part, *refs):
    recv = refs[: groups - 1]
    middle, final, w, gain, grad_mid, mid_low, grad_mixed, gains = refs[groups - 1 :]
    total = part[...].astype(F32)
    for other in recv:
        total = total + other[...].astype(F32)
    back, terms = norm_back(middle[...], gain[...], total)
    gains[0:1, :] = jnp.sum(terms, axis=0, keepdims=True)
    gains[1:2, :] = jnp.sum(total, axis=0, keepdims=True)
    value = final[...].astype(F32) + back
    grad_mid[...] = value
    low = value.astype(BF)
    mid_low[...] = low.T
    for j in range(groups):
        grad_mixed[:, j * cw : (j + 1) * cw] = dot(low, columns(w, j, cw, 3)).astype(BF)


def weight_grad_kernel(terms, rows, ids, *refs):
    left, right, outs = refs[:terms], refs[terms : 2 * terms], refs[2 * terms :]
    value = dot(left[0][...], right[0][...])
    for a, b in zip(left[1:], right[1:]):
        value = value + dot(a[...], b[...])
    if len(outs) == 1:
        outs[0][...] = value.astype(BF)
    else:
        keep, send, total = outs
        total[...] = value
        split_rows(rows, ids, total, keep, send)


def split_rows(rows, ids, total, keep, send):
    for b in range(keep.shape[0]):
        for ref, core in ((keep, ids[3]), (send, 1 - ids[3])):
            start = pl.multiple_of((b * 2 + core) * rows, rows)
            ref[b] = total[pl.ds(start, rows), :].astype(BF)


def weight_grad(ids, left, right, rows, block, split, name):
    depth, width = left[0].shape[0], right[0].shape[1]
    if split:
        outs = [struct((depth // rows // 2, rows, width), BF)] * 2
        spec = pl.BlockSpec((depth // rows // 2, rows, block), lambda i, *_: (0, 0, i))
        specs, scratch = [spec, spec], [pltpu.VMEM((depth, block), F32)]
    else:
        outs = [struct((depth, width), BF)]
        specs, scratch = [pl.BlockSpec((depth, block), lambda i, *_: (0, i))], []
    return call(
        functools.partial(weight_grad_kernel, len(left), rows),
        (width // block,),
        [whole(a) for a in left]
        + [pl.BlockSpec((a.shape[0], block), lambda i, *_: (0, i)) for a in right],
        specs,
        outs,
        scratch,
        ids,
        left + right,
        2 * sum(a.shape[0] for a in right) * depth * width,
        name,
    )


def sum_grad_kernel(plan, rows, ids, *refs):
    keep, send, total = refs[2 * sum(terms for _, _, terms in plan) :]
    first = 0
    for at, width, terms in plan:
        value = dot(refs[first][...], refs[first + 1][...])
        for k in range(first + 2, first + 2 * terms, 2):
            value = value + dot(refs[k][...], refs[k + 1][...])
        total[:, at : at + width] = value
        first += 2 * terms
    split_rows(rows, ids, total, keep, send)


def sum_grad(ids, results, rows, depth, name):
    blocks = max(1, 256 // rows)
    plan, specs, args, at, flops = [], [], [], 0, 0
    for terms in results:
        for left, right in terms:
            size, width = right.shape
            specs.append(pl.BlockSpec((blocks * 2 * rows, size), lambda i, ids: (i, 0)))
            specs.append(whole(right))
            args += [left, right]
            flops += 2 * size * width * depth
        plan.append((at, width, len(terms)))
        at += width
    spec = pl.BlockSpec((blocks, rows, at), lambda i, ids: (i, 0, 0))
    return call(
        functools.partial(sum_grad_kernel, plan, rows),
        (depth // (blocks * 2 * rows),),
        specs,
        [spec, spec],
        [struct((depth // rows // 2, rows, at), BF)] * 2,
        [pltpu.VMEM((blocks * 2 * rows, at), F32)],
        ids,
        args,
        flops,
        name,
    )


def source_back_kernel(
    groups, cw, imgs, patch, share, ids, live, gk, gv, wk, wv, media, latents, cot, keep, *refs
):
    recv, refs = refs[: groups - 1], refs[groups - 1 :]
    grad_mid, m_gain, l_gain, media_grad, latent_grad, gains, total, lat_total, query = refs
    base = pl.program_id(0) * imgs
    step = patch + share
    value = dot(gk[:, :cw], wk[0, :, cw : 2 * cw], NT) + dot(gv[:, :cw], columns(wv, 0, cw, 2), NT)
    for j in range(1, groups):
        cols = slice(j * cw, (j + 1) * cw)
        value = value + dot(gk[:, cols], wk[j, :, cw : 2 * cw], NT)
        value = value + dot(gv[:, cols], columns(wv, j, cw, 2), NT)
    total[...] = value
    asked = keep[...]
    for s in range(1, groups):
        asked = asked + lane_roll(recv[s - 1][...].astype(F32), s, groups, cw)
    query[...] = asked.astype(BF)
    value = dot(query[:, :cw], wk[0, :, :cw], NT)
    for j in range(1, groups):
        value = value + dot(query[:, j * cw : (j + 1) * cw], wk[j, :, :cw], NT)
    lat_total[...] = value

    @pl.when(pl.program_id(0) == 0)
    def _():
        gains[...] = jnp.zeros_like(gains)

    sums = [0.0] * 4
    for i in range(imgs):
        grad = total[i * step : i * step + patch, :]
        back, terms = norm_back(media[i].astype(F32), m_gain[...], grad)
        media_grad[i] = back
        sums[0] += fold_rows(terms)
        sums[1] += fold_rows(grad)
        rows = slice(i * share, (i + 1) * share)
        grad = total[i * step + patch : (i + 1) * step, :] + lat_total[rows, :]
        back, terms = norm_back(latents[i].astype(F32), l_gain[...], grad)
        sums[2] += fold_rows(terms)
        sums[3] += fold_rows(grad)
        latent_grad[i] = jnp.where(
            live[base + i] > 0, grad_mid[rows, :] + back, cot[i].astype(F32)
        )
    for k in range(4):
        gains[k : k + 1, :] += jnp.sum(sums[k], axis=0, keepdims=True)


def make_local(depth_z, groups):
    dp_size = depth_z * 4

    def from_dp(value, s=0, yf=0, cf=0):
        pairs = []
        for dst in range(dp_size):
            z, y, c = dst // 4, dst // 2 % 2, dst % 2
            pairs.append(((z + s) % depth_z * 4 + (y ^ yf) * 2 + (c ^ cf), dst))
        return lax.ppermute(value, "dp", pairs)

    def flip_z(value, bit):
        pairs = [(((dst // 4) ^ bit) * 4 + dst % 4, dst) for dst in range(dp_size)]
        return lax.ppermute(value, "dp", pairs)

    def from_head(value, s):
        return lax.ppermute(value, "head", [((x + s) % groups, x) for x in range(groups)])

    def to_head(value, s):
        return lax.ppermute(value, "head", [(x, (x + s) % groups) for x in range(groups)])

    def plane(value, sx, yf, back, cf=0):
        pairs = []
        for dst in range(dp_size):
            for x in range(groups):
                other = (dst ^ (2 * yf + cf)) * groups + (x + sx) % groups
                mine = dst * groups + x
                pairs.append((mine, other) if back else (other, mine))
        return lax.ppermute(value, ("dp", "head"), pairs)

    others = [(sx, yf) for sx in range(groups) for yf in range(2) if sx or yf]

    def local(
        media_tokens,
        latents,
        cotangent,
        image_counts,
        media_gain,
        media_bias,
        latent_gain,
        latent_bias,
        ff_gain,
        ff_bias,
        w_query,
        w_keyval,
        w_attn_out,
        w_up,
        w_down,
    ):
        images, patches, width = media_tokens.shape
        lat = latents.shape[1]
        rows, cw = w_query.shape
        units = w_up.shape[1]
        patch, share = patches // groups, lat // groups
        step = patch + share
        heads_w = cw * groups
        me = lax.axis_index("head").astype(jnp.int32)
        place = lax.axis_index("dp").astype(jnp.int32)
        z, y, c = place // 4, place // 2 % 2, place % 2
        ids = jnp.stack([me, z, y, c])
        live = (jnp.arange(images, dtype=jnp.int32) < jnp.sum(image_counts)).astype(jnp.int32)
        gains = [
            g.reshape(1, width)
            for g in (media_gain, media_bias, latent_gain, latent_bias, ff_gain, ff_bias)
        ]
        media4 = media_tokens.reshape(images, groups, patch, width)
        lat4 = latents.reshape(images, groups, share, width)
        cot4 = cotangent.reshape(images, groups, share, width)

        part = images // CHUNKS
        own = part * share

        shard = jnp.concatenate([w_query, w_keyval[:, 0], w_keyval[:, 1], w_attn_out.T], axis=1)
        got = [from_dp(shard, s) for s in range(1, depth_z)]
        w_up_all = lax.all_gather(w_up, "dp", axis=0, tiled=True)
        w_down_all = lax.all_gather(w_down.T, "dp", axis=0, tiled=True)
        live_low = live.astype(BF).reshape(images, 1, 1)
        final4 = [
            lax.dynamic_index_in_dim(cot4, (me + s) % groups, 1, keepdims=False) * live_low
            for s in range(groups)
        ]
        final4 = jnp.stack(final4).reshape(groups, images * share, width)
        own_t = final4[0].T
        away_t = final4[1:].reshape((groups - 1) * images * share, width).T
        final4, own_t, away_t = tie((final4, own_t, away_t), shard)
        line = jnp.stack([shard] + tie(got, final4, own_t, away_t))
        parts = {(0, 0): line} | {at: plane(line, *at, False) for at in others}

        imgs = math.gcd(images, math.lcm(128, step) // step)
        src, nlat, src_t, nlat_t = call(
            functools.partial(norm_kernel, imgs, lat, share, patch),
            (images // imgs,),
            [
                pl.BlockSpec((imgs, None, patch, width), lambda i, ids: (i, ids[0], 0, 0)),
                images_of(imgs, lat, width),
            ]
            + [whole(gains[0])] * 4,
            [
                rows_of(imgs * step, width),
                rows_of(imgs * lat, width),
                pl.BlockSpec((width, imgs * step), lambda i, ids: (0, i)),
                pl.BlockSpec((width, imgs * lat), lambda i, ids: (0, i)),
            ],
            [
                struct((images * step, width), BF),
                struct((images * lat, width), BF),
                struct((width, images * step), BF),
                struct((width, images * lat), BF),
            ],
            [pltpu.VMEM((lat, width), F32)],
            tie(ids, line),
            [media4, latents] + gains[:4],
            images * step * width * 12,
            "input_norms",
        )

        pieces, entries = [], []
        for (sx, yf), part_of in parts.items():
            for cf, piece in ((0, part_of), (1, from_dp(tie(part_of, src), cf=1))):
                for s in range(depth_z):
                    entries.append((len(pieces), s, sx, s, yf, cf))
                pieces.append(piece)
        w_attn = assemble(entries, pieces, depth_z, ids, rows, groups, 4 * cw, "place_attn")

        imgs = 4
        attn_macs = images * step * lat * heads_w
        q, k, stats = call(
            functools.partial(project_kernel, groups, cw, imgs, step, lat),
            (images // imgs,),
            [rows_of(imgs * step, width), rows_of(imgs * lat, width), third(w_attn, 2 * cw, 0)],
            [
                rows_of(imgs * lat, heads_w),
                rows_of(imgs * step, heads_w),
                images_of(imgs, 2, heads_w),
            ],
            [
                struct((images * lat, heads_w), BF),
                struct((images * step, heads_w), BF),
                struct((images, 2, heads_w), F32),
            ],
            [],
            ids,
            [src, nlat, w_attn],
            2 * images * (step * width * heads_w + lat * width * heads_w) + 8 * attn_macs,
            "project",
        )
        tops, sums = [stats[:, :1]], [stats[:, 1:]]
        for s in range(1, groups):
            other = jnp.roll(from_head(stats, s), s * cw, axis=2)
            tops.append(other[:, :1])
            sums.append(other[:, 1:])
        v = call(
            functools.partial(values_kernel, groups, cw),
            (images // imgs,),
            [rows_of(imgs * step, width), third(w_attn, cw, 2)],
            [rows_of(imgs * step, heads_w)],
            [struct((images * step, heads_w), BF)],
            [],
            tie(ids, q),
            [src, w_attn],
            2 * images * step * width * heads_w,
            "values",
        )[0]
        top = functools.reduce(jnp.maximum, tops)
        lse = top + jnp.log(sum(t * jnp.exp(m - top) for m, t in zip(tops, sums)))

        imgs = min(imgs, part)
        count = part // imgs

        def attn_specs(ch):
            return [
                rows_of(imgs * lat, heads_w, ch * count),
                rows_of(imgs * step, heads_w, ch * count),
                rows_of(imgs * step, heads_w, ch * count),
                images_of(imgs, 1, heads_w, ch * count),
            ]

        row_sends = [
            rows_of(imgs * share, heads_w),
            pl.BlockSpec((groups - 1, imgs * share, heads_w), lambda i, ids: (0, i, 0)),
        ]
        row_outs = [struct((own, heads_w), F32), struct((groups - 1, own, heads_w), BF)]

        def exchanged(keep, send):
            return [keep] + [to_head(send[s - 1], s) for s in range(groups - 1, 0, -1)]

        mixes, normed, mixed, middle = [], [], None, None
        for ch in range(CHUNKS):
            keep, send = call(
                functools.partial(mix_kernel, groups, cw, imgs, step, lat, share),
                (count,),
                attn_specs(ch),
                row_sends,
                row_outs,
                [pltpu.VMEM((imgs, lat, heads_w), F32)],
                tie(ids, [a[0] for a in mixes]),
                [q, k, v, lse],
                8 * attn_macs / CHUNKS,
                f"mix{ch}",
            )
            mixes.append(exchanged(keep, send))
        for ch in range(CHUNKS):
            lat_spec = pl.BlockSpec(
                (part, None, share, width), lambda i, ids, ch=ch: (ch, ids[0], 0, 0)
            )
            outs = call(
                functools.partial(middle_kernel, groups, cw),
                (1,),
                [whole(a) for a in mixes[ch]]
                + [lat_spec, third(w_attn, cw, 3), whole(gains[4]), whole(gains[5])]
                + ([anywhere()] * 2 if ch else []),
                [fixed_rows(own, heads_w, ch), fixed_rows(own, width, ch), fixed_rows(own, width)],
                [
                    struct((CHUNKS * own, heads_w), BF),
                    struct((CHUNKS * own, width), F32),
                    struct((own, width), BF),
                ],
                [],
                tie(ids, [a[0] for a in normed]),
                mixes[ch] + [lat4, w_attn, gains[4], gains[5]] + ([mixed, middle] if ch else []),
                2 * own * heads_w * width,
                f"middle{ch}",
                {groups + 4: 0, groups + 5: 1} if ch else None,
            )
            mixed, middle = outs[:2]
            normed.append([outs[2]] + [from_head(outs[2], s) for s in range(1, groups)])
        block = min(512, units)

        def feed_forward(terms, ids, name):
            size = len(terms) * own
            return call(
                functools.partial(forward_kernel, len(terms)),
                (units // block,),
                [whole(a) for a, _ in terms]
                + [spec for _, spec in terms]
                + [
                    pl.BlockSpec((width, block), lambda i, ids: (0, i)),
                    pl.BlockSpec((width, block), lambda i, ids: (0, i)),
                ],
                [pl.BlockSpec((size, block), lambda i, ids: (0, i))] * 2
                + [fixed_rows(size, width)] * 2
                + [pl.BlockSpec((width * block // units, size), lambda i, ids: (i, 0))],
                [struct((size, units), BF)] * 2
                + [struct((size, width), BF)] * 2
                + [struct((width, size), BF)],
                [pltpu.VMEM((size, width), BF)] * 2 + [pltpu.VMEM((size, width), F32)] * 2,
                ids,
                [a for a, _ in terms] + [final4] * len(terms) + [w_up_all, w_down_all],
                8 * size * width * units,
                name,
            )

        def final_rows(s, ch):
            return pl.BlockSpec((None, own, width), lambda *_: (s, ch, 0))

        size = CHUNKS * own
        away_ff = feed_forward(
            [(normed[ch][t], final_rows(t, ch)) for t in range(1, groups) for ch in range(CHUNKS)],
            ids,
            "feed_forward_away",
        )
        ff_back, mid_back = [a.reshape(groups - 1, size, width) for a in away_ff[2:4]]
        mid_back = [to_head(mid_back[s - 1], s) for s in range(groups - 1, 0, -1)]
        own_ff = feed_forward(
            [(normed[ch][0], final_rows(0, ch)) for ch in range(CHUNKS)],
            tie(ids, away_ff),
            "feed_forward_own",
        )

        def pick(block, index, axis=0):
            return lax.dynamic_index_in_dim(block, index, axis, keepdims=False).astype(F32)

        def lanes(block, cols):
            if len(cols) == 1 and cols[0] == slice(0, block.shape[-1]):
                return block
            return jnp.concatenate([block[..., c] for c in cols], axis=-1)

        class Sum:
            def __init__(self, keep, recv, cols):
                self.cols = cols
                self.grid = [a.reshape((depth_z, 2) + a.shape[1:]) for a in (keep, recv)]
                self.crossed, self.near = [], []

            def at(self, sx, yy):
                terms = [pick(lanes(a, self.cols[sx]), yy, 1) for a in self.grid]
                return sum(terms + [pick(a, yy, 1) for a in self.crossed])

            def cross(self, late):
                grid = tie(self.grid, late)
                self.away = [
                    sum(lanes(a, self.cols[sx]).astype(F32) for a in grid).astype(BF)
                    for sx in range(1, groups)
                ]
                return self.away

            def across(self):
                self.crossed = [to_head(a, sx) for sx, a in zip(range(1, groups), self.away)]

            def second(self, routes, late=()):
                self.grid, self.crossed = tie((self.grid, self.crossed), late)
                self.routes = routes
                self.away = [self.at(sx, y ^ yf).astype(BF) for sx, yf in routes]
                return self.away

            def sent(self):
                self.near = [plane(a, *to, True) for a, to in zip(self.away, self.routes)]

            def start_z(self):
                base = self.at(0, y)

                def block(zz):
                    return pick(base, zz) + sum(pick(a, zz) for a in self.near)

                self.block, self.left, self.bit = block, depth_z, 1

            def halve(self, late=()):
                turn = tie(z, late)
                mine, block = z // self.bit % 2, self.block
                away_at = 1 - turn // self.bit % 2
                self.left //= 2
                self.held = lambda k: block(2 * k + mine)
                away = [block(2 * k + away_at) for k in range(self.left)]
                self.away = jnp.stack(away).astype(BF)
                return self.away

            def halved(self, late=()):
                near, held = tie(flip_z(self.away, self.bit), late), self.held
                self.block, self.bit = (lambda k: held(k) + pick(near, k)), 2 * self.bit

            def rest(self):
                while self.left > 1:
                    self.halve()
                    self.halved()
                return self.block(0)

            def third(self):
                self.start_z()
                self.away = [self.block((z + s) % depth_z).astype(BF) for s in range(1, depth_z)]
                return self.away

            def last(self):
                got = [from_dp(a, depth_z - s) for s, a in zip(range(1, depth_z), self.away)]
                return self.block(z) + sum(a.astype(F32) for a in got)

        along_y = [(0, 1)]

        def groups_of(*starts):
            return [[slice(a + sx * cw, a + (sx + 1) * cw) for a in starts] for sx in range(groups)]

        up_part = weight_grad(
            tie(ids, own_ff[0]),
            [own_ff[4], away_ff[4]],
            [own_ff[1], away_ff[1]],
            rows,
            block,
            False,
            "grad_up",
        )[0]
        grad_mid, mid_low_t, grad_mixed, ff_gains = call(
            functools.partial(middle_back_kernel, groups, cw),
            (1,),
            [whole(own_ff[3])]
            + [whole(t) for t in mid_back]
            + [whole(middle), pl.BlockSpec((None, size, width), lambda *_: (0, 0, 0))]
            + [third(w_attn, cw, 3), whole(gains[4])],
            [
                fixed_rows(size, width),
                fixed_rows(width, size),
                fixed_rows(size, heads_w),
                fixed_rows(2, width),
            ],
            [
                struct((size, width), F32),
                struct((width, size), BF),
                struct((size, heads_w), BF),
                struct((2, width), F32),
            ],
            [],
            tie(ids, up_part),
            [own_ff[3]] + mid_back + [middle, final4, w_attn, gains[4]],
            2 * size * heads_w * width,
            "middle_back",
        )
        grad_mixed = [grad_mixed] + [from_head(grad_mixed, s) for s in range(1, groups)]

        grad_up = lax.psum_scatter(tie(up_part, mid_back), "dp", scatter_dimension=0, tiled=True)
        down_parts = weight_grad(
            tie(ids, mid_low_t),
            [own_t, away_t],
            [own_ff[0], away_ff[0]],
            rows,
            block,
            True,
            "grad_down",
        )

        count = images // imgs
        gv, grad_all, delta = call(
            functools.partial(back_probs_kernel, groups, cw, imgs, step, lat, share),
            (count,),
            attn_specs(0) + [rows_of(imgs * share, heads_w)] * groups,
            [rows_of(imgs * step, heads_w), rows_of(imgs * lat, heads_w), images_of(imgs, 1, heads_w)],
            [
                struct((images * step, heads_w), BF),
                struct((images * lat, heads_w), BF),
                struct((images, 1, heads_w), F32),
            ],
            [pltpu.VMEM((imgs, lat, heads_w), F32)],
            tie(ids, down_parts[0]),
            [q, k, v, lse] + grad_mixed,
            12 * attn_macs,
            "back_probs",
        )
        recv = from_dp(tie(down_parts[1], gv), cf=1)
        sum_down = Sum(down_parts[0], recv, [[slice(0, units)]])
        ordered = jnp.roll(jnp.concatenate([own_ff[2][None], tie(ff_back, gv)]), me, axis=0)
        ff_sum = lax.psum_scatter(tie(ordered, grad_up), "head", scatter_dimension=0, tiled=True)[0]
        total = delta
        for s in range(1, groups):
            total = total + jnp.roll(from_head(delta, s), s * cw, axis=2)
        value_parts = sum_grad(
            tie(ids, gv),
            [[(mid_low_t, mixed)], [(src_t, gv)]],
            rows,
            width,
            "grad_out_values",
        )
        sum_value = Sum(value_parts[0], from_dp(value_parts[1], cf=1), groups_of(0, heads_w))
        gk, gq, keep, send = call(
            functools.partial(back_scores_kernel, groups, cw, imgs, step, lat, share),
            (count,),
            attn_specs(0) + [rows_of(imgs * lat, heads_w), images_of(imgs, 1, heads_w)],
            [rows_of(imgs * step, heads_w), rows_of(imgs * lat, heads_w)] + row_sends,
            [
                struct((images * step, heads_w), BF),
                struct((images * lat, heads_w), BF),
                struct((size, heads_w), F32),
                struct((groups - 1, size, heads_w), BF),
            ],
            [pltpu.VMEM((imgs, lat, heads_w), F32)],
            tie(ids, value_parts[0], sum_down.second(along_y, value_parts[0]), ordered),
            [q, k, v, lse, grad_all, total],
            16 * attn_macs,
            "back_scores",
        )
        sum_down.sent()
        query_terms = exchanged(keep, send)
        key_parts = sum_grad(
            tie(ids, gk, sum_value.cross(gk)),
            [[(src_t, gk)], [(nlat_t, gq)]],
            rows,
            width,
            "grad_query_keys",
        )
        sum_value.across()
        sum_down.start_z()
        sum_key = Sum(key_parts[0], from_dp(key_parts[1], cf=1), groups_of(0, heads_w))

        def share_rows(size):
            return pl.BlockSpec((imgs, None, size, width), lambda i, ids, live: (i, ids[0], 0, 0))

        before = [sum_key.second(others), sum_value.second(along_y), sum_down.halve()]
        media_grad, latent_grad, gain_terms = call(
            functools.partial(source_back_kernel, groups, cw, imgs, patch, share),
            (count,),
            [rows_of(imgs * step, heads_w)] * 2
            + [third(w_attn, 2 * cw, 0), third(w_attn, cw, 2)]
            + [share_rows(patch), share_rows(share), share_rows(share)]
            + [rows_of(imgs * share, heads_w)] * groups
            + [rows_of(imgs * share, width), whole(gains[0]), whole(gains[2])],
            [images_of(imgs, patch, width), images_of(imgs, share, width), fixed_rows(4, width)],
            [
                struct((images, patch, width), F32),
                struct((images, share, width), F32),
                struct((4, width), F32),
            ],
            [
                pltpu.VMEM((imgs * step, width), F32),
                pltpu.VMEM((imgs * share, width), F32),
                pltpu.VMEM((imgs * share, heads_w), BF),
            ],
            [tie(ids, before, grad_up), live],
            [gk, gv, w_attn, w_attn, media4, lat4, cot4]
            + query_terms
            + [grad_mid, gains[0], gains[2]],
            2 * images * step * width * 2 * heads_w,
            "source_back",
        )
        sum_key.sent()
        sum_value.sent()
        sum_key.near = tie(sum_key.near, media_grad)
        sum_value.near = tie(sum_value.near, media_grad)
        sum_down.halved(media_grad)
        last = [jnp.concatenate(pair, axis=1) for pair in zip(sum_key.third(), sum_value.third())]
        last = [from_dp(a, depth_z - s).astype(F32) for s, a in zip(range(1, depth_z), last)]
        query_key = sum_key.block(z) + sum(a[:, : 2 * cw] for a in last)
        out_value = sum_value.block(z) + sum(a[:, 2 * cw :] for a in last)

        final_lat = middle + ff_sum.astype(F32)
        final_lat = final_lat.reshape(images, share, width)
        lat_own = lax.dynamic_index_in_dim(lat4, me, 1, keepdims=False).astype(F32)
        latents_out = jnp.where(live[:, None, None] > 0, final_lat, lat_own)

        total = jnp.concatenate([gain_terms, ff_gains])
        grad_down = sum_down.rest()
        total = total + from_dp(total, cf=1)
        near = [plane(total, *at, False) for at in others]
        total = total + sum(near)
        bit = 1
        while bit < depth_z:
            total = total + flip_z(total, bit)
            bit *= 2
        norm_grads = total

        return (
            latents_out,
            media_grad,
            latent_grad,
            query_key[:, cw:],
            jnp.stack([query_key[:, :cw], out_value[:, cw:]], axis=1),
            out_value[:, :cw].T,
            grad_up.astype(F32),
            grad_down.T,
            norm_grads,
        )

    return local


def solution(mesh):
    return jax.shard_map(
        make_local(mesh.shape["dp"] // 4, mesh.shape["head"]),
        mesh=mesh,
        in_specs=(
            P("dp", None, None),
            P("dp", None, None),
            P("dp", None, None),
            P("dp"),
            P(),
            P(),
            P(),
            P(),
            P(),
            P(),
            P("dp", "head"),
            P("dp", None, "head"),
            P("head", "dp"),
            P("dp", "head"),
            P("head", "dp"),
        ),
        out_specs=(
            P("dp", "head", None),
            P("dp", "head", None),
            P("dp", "head", None),
            P("dp", "head"),
            P("dp", None, "head"),
            P("head", "dp"),
            P("dp", "head"),
            P("head", "dp"),
            P(),
        ),
        check_vma=False,
    )
```

```python
import functools
import math

import jax
import jax.numpy as jnp
from jax import lax
from jax.experimental import pallas as pl
from jax.experimental.pallas import tpu as pltpu
from jax.sharding import PartitionSpec as P

HD = 64
HEADS = 8
CHUNKS = 2
EPS = 1e-05
BF = jnp.bfloat16
F32 = jnp.float32
MIB = 1024 * 1024
VMEM = 58
SMALL = 40
STREAMED = ("feed_forward_own", "feed_forward_away", "grad_up", "grad_down", "middle_back", "source_back")

NN = (((1,), (0,)), ((), ()))
NT = (((1,), (1,)), ((), ()))
TN = (((0,), (0,)), ((), ()))


def dot(left, right, form=NN):
    return lax.dot_general(left, right, form, preferred_element_type=F32)


def struct(shape, dtype):
    return jax.ShapeDtypeStruct(shape, dtype)


def call(kernel, grid, in_specs, out_specs, out_shape, scratch, ids, args, flops, name, alias=None):
    scalars = ids if isinstance(ids, (list, tuple)) else [ids]
    moved = sum(a.size * a.dtype.itemsize for a in args if a.ndim < 4)
    moved += sum(o.size * jnp.dtype(o.dtype).itemsize for o in out_shape)
    return pl.pallas_call(
        kernel,
        grid_spec=pltpu.PrefetchScalarGridSpec(
            num_scalar_prefetch=len(scalars),
            grid=grid,
            in_specs=in_specs,
            out_specs=out_specs,
            scratch_shapes=scratch,
        ),
        out_shape=out_shape,
        input_output_aliases={len(scalars) + k: v for k, v in (alias or {}).items()},
        compiler_params=pltpu.CompilerParams(
            vmem_limit_bytes=(VMEM if name in STREAMED else SMALL) * MIB,
            dimension_semantics=("arbitrary",) * len(grid)
        ),
        cost_estimate=pl.CostEstimate(
            flops=int(flops), bytes_accessed=int(moved), transcendentals=0
        ),
        name=name,
    )(*scalars, *args)


def whole(array):
    zeros = (0,) * array.ndim
    return pl.BlockSpec(array.shape, lambda *_: zeros)


def rows_of(block, width, first=0):
    return pl.BlockSpec((block, width), lambda i, *_: (i + first, 0))


def fixed_rows(block, width, at=0):
    return pl.BlockSpec((block, width), lambda *_: (at, 0))


def images_of(block, rows, width, first=0):
    return pl.BlockSpec((block, rows, width), lambda i, *_: (i + first, 0, 0))


def third(array, width, at):
    if width % 128:
        return whole(array)
    return pl.BlockSpec(array.shape[:2] + (width,), lambda *_: (0, 0, at))


def columns(ref, group, width, at):
    if ref.shape[2] == width:
        return ref[group]
    return ref[group, :, at * width : (at + 1) * width]


def anywhere():
    return pl.BlockSpec(memory_space=pl.ANY)


def tie(values, *first):
    flat, tree = jax.tree.flatten(values)
    out = lax.optimization_barrier(tuple(flat) + tuple(jax.tree.leaves(first)))
    return jax.tree.unflatten(tree, out[: len(flat)])


def norm_parts(values):
    centre = values - jnp.mean(values, axis=-1, keepdims=True)
    rstd = lax.rsqrt(jnp.mean(centre * centre, axis=-1, keepdims=True) + EPS)
    return centre * rstd, rstd


def norm_back(values, gain, grad):
    xhat, rstd = norm_parts(values)
    scaled = grad * gain
    first = jnp.mean(scaled, axis=-1, keepdims=True)
    second = jnp.mean(scaled * xhat, axis=-1, keepdims=True)
    return rstd * (scaled - first - xhat * second), grad * xhat


def fold_rows(value):
    return jnp.sum(value.reshape(value.shape[0] // 8, 8, value.shape[1]), axis=0)


def norm_kernel(
    imgs, lat, share, patch, ids, media, latents, m_gain, m_bias, l_gain, l_bias, *refs
):
    src, nlat, src_t, nlat_t, keep = refs
    start = pl.multiple_of(ids[0] * share, share)
    step = patch + share
    for i in range(imgs):
        xhat, _ = norm_parts(media[i].astype(F32))
        src[i * step : i * step + patch, :] = (xhat * m_gain[...] + m_bias[...]).astype(BF)
        xhat, _ = norm_parts(latents[i].astype(F32))
        normed = xhat * l_gain[...] + l_bias[...]
        nlat[i * lat : (i + 1) * lat, :] = normed.astype(BF)
        keep[...] = normed
        src[i * step + patch : (i + 1) * step, :] = keep[pl.ds(start, share), :].astype(BF)
    src_t[...] = src[...].T
    nlat_t[...] = nlat[...].T


def assemble(entries, pieces, depth, ids, rows, groups, width, name):
    def kernel(ids_ref, *refs):
        out, sems = refs[len(pieces)], refs[len(pieces) + 1]
        copies = []
        for e, (op, lead, group, s, yf, cf) in enumerate(entries):
            block = lax.rem(ids_ref[1] + s, depth) * 4
            block += lax.rem(ids_ref[2] + yf, 2) * 2 + lax.rem(ids_ref[3] + cf, 2)
            start = pl.multiple_of(block * rows, rows)
            source = refs[op] if lead is None else refs[op].at[lead]
            copies.append(
                pltpu.make_async_copy(source, out.at[group, pl.ds(start, rows), :], sems.at[e])
            )
        for copy in copies:
            copy.start()
        for copy in copies:
            copy.wait()

    return call(
        kernel,
        (1,),
        [anywhere()] * len(pieces),
        [pl.BlockSpec((groups, depth * 4 * rows, width), lambda *_: (0, 0, 0))],
        [struct((groups, depth * 4 * rows, width), BF)],
        [pltpu.SemaphoreType.DMA((len(entries),))],
        ids,
        pieces,
        0,
        name,
    )[0]


def diag_mask(heads, width, dtype):
    row = lax.broadcasted_iota(jnp.int32, (heads * HD, width), 0) // HD
    col = lax.broadcasted_iota(jnp.int32, (heads * HD, width), 1) // HD
    return jnp.where(row == col, 1.0, 0.0).astype(dtype)


def spread(block, heads, mask):
    return jnp.concatenate([block] * heads, axis=0) * mask


def fold(full, heads, lat, mask):
    full = full * mask
    total = full[:lat]
    for h in range(1, heads):
        total = total + full[h * lat : (h + 1) * lat]
    return total


def lane_roll(values, s, groups, cw):
    if s == 0:
        return values
    if cw % 128 == 0:
        cut = (groups - s) * cw
        return jnp.concatenate([values[:, cut:], values[:, :cut]], axis=1)
    return pltpu.roll(values, s * cw, 1)


def project_kernel(groups, cw, imgs, step, lat, ids, src, nlat, w, q, k, stats):
    heads = cw // HD
    for j in range(groups):
        k[:, j * cw : (j + 1) * cw] = dot(src[...], w[j, :, cw : 2 * cw]).astype(BF)
        q[:, j * cw : (j + 1) * cw] = (dot(nlat[...], w[j, :, :cw]) * (HD**-0.5)).astype(BF)
    mask = diag_mask(heads, cw, BF)
    for i in range(imgs):
        for j in range(groups):
            cols = slice(j * cw, (j + 1) * cw)
            qbd = spread(q[i * lat : (i + 1) * lat, cols], heads, mask)
            score = dot(k[i * step : (i + 1) * step, cols], qbd, NT)
            top = jnp.max(score, axis=0, keepdims=True)
            stats[i, 0:1, cols] = top
            stats[i, 1:2, cols] = jnp.sum(jnp.exp(score - top), axis=0, keepdims=True)


def values_kernel(groups, cw, ids, src, w, v):
    for j in range(groups):
        v[:, j * cw : (j + 1) * cw] = dot(src[...], columns(w, j, cw, 2)).astype(BF)


def send_rows(groups, share, ids, scratch, i, keep, send):
    for s in range(groups):
        start = pl.multiple_of(lax.rem(ids[0] + s, groups) * share, share)
        rows = scratch[pl.ds(start, share), :]
        if s == 0:
            keep[i * share : (i + 1) * share, :] = rows
        else:
            send[s - 1, i * share : (i + 1) * share, :] = rows.astype(BF)


def mix_kernel(groups, cw, imgs, step, lat, share, ids, q, k, v, lse, keep, send, scratch):
    heads = cw // HD
    mask, fmask = diag_mask(heads, cw, BF), diag_mask(heads, cw, F32)
    for i in range(imgs):
        rows = slice(i * step, (i + 1) * step)
        for j in range(groups):
            cols = slice(j * cw, (j + 1) * cw)
            qbd = spread(q[i * lat : (i + 1) * lat, cols], heads, mask)
            probs = jnp.exp(dot(k[rows, cols], qbd, NT) - lse[i, 0:1, cols])
            full = dot(probs.astype(BF), v[rows, cols], TN)
            scratch[i, :, cols] = fold(full, heads, lat, fmask)
        send_rows(groups, share, ids, scratch.at[i], i, keep, send)


def back_probs_kernel(groups, cw, imgs, step, lat, share, ids, q, k, v, lse, grad_keep, *refs):
    recv, (gv, grad_all, delta, scratch) = refs[: groups - 1], refs[groups - 1 :]
    heads = cw // HD
    mask = diag_mask(heads, cw, BF)
    for i in range(imgs):
        for s in range(groups):
            start = pl.multiple_of(lax.rem(ids[0] + s, groups) * share, share)
            block = grad_keep if s == 0 else recv[s - 1]
            block = lane_roll(block[i * share : (i + 1) * share, :].astype(F32), s, groups, cw)
            scratch[i, pl.ds(start, share), :] = block
        grad_all[i * lat : (i + 1) * lat, :] = scratch[i].astype(BF)
        rows = slice(i * step, (i + 1) * step)
        for j in range(groups):
            cols = slice(j * cw, (j + 1) * cw)
            qbd = spread(q[i * lat : (i + 1) * lat, cols], heads, mask)
            gbd = spread(grad_all[i * lat : (i + 1) * lat, cols], heads, mask)
            probs = jnp.exp(dot(k[rows, cols], qbd, NT) - lse[i, 0:1, cols])
            delta[i, 0:1, cols] = jnp.sum(probs * dot(v[rows, cols], gbd, NT), axis=0, keepdims=True)
            gv[rows, cols] = dot(probs.astype(BF), gbd).astype(BF)


def back_scores_kernel(
    groups, cw, imgs, step, lat, share, ids, q, k, v, lse, grad_all, delta, gk, gq, keep, send, scratch
):
    heads = cw // HD
    mask, fmask = diag_mask(heads, cw, BF), diag_mask(heads, cw, F32)
    for i in range(imgs):
        rows = slice(i * step, (i + 1) * step)
        for j in range(groups):
            cols = slice(j * cw, (j + 1) * cw)
            qbd = spread(q[i * lat : (i + 1) * lat, cols], heads, mask)
            gbd = spread(grad_all[i * lat : (i + 1) * lat, cols], heads, mask)
            probs = jnp.exp(dot(k[rows, cols], qbd, NT) - lse[i, 0:1, cols])
            grad = dot(v[rows, cols], gbd, NT) - delta[i, 0:1, cols]
            grad = (probs * grad).astype(BF)
            gk[rows, cols] = dot(grad, qbd).astype(BF)
            full = dot(grad, k[rows, cols], TN)
            scratch[i, :, cols] = fold(full, heads, lat, fmask) * (HD**-0.5)
        gq[i * lat : (i + 1) * lat, :] = scratch[i].astype(BF)
        send_rows(groups, share, ids, scratch.at[i], i, keep, send)


def middle_kernel(groups, cw, ids, keep, *refs):
    recv = refs[: groups - 1]
    latents, w, gain, bias = refs[groups - 1 : groups + 3]
    mixed, middle, normed = refs[-3:]
    total = keep[...]
    for s in range(1, groups):
        total = total + lane_roll(recv[s - 1][...].astype(F32), s, groups, cw)
    low = total.astype(BF)
    mixed[...] = low
    value = latents[...].astype(F32).reshape(middle.shape)
    for j in range(groups):
        value = value + dot(low[:, j * cw : (j + 1) * cw], columns(w, j, cw, 3), NT)
    middle[...] = value
    xhat, _ = norm_parts(value)
    normed[...] = (xhat * gain[...] + bias[...]).astype(BF)


def gelu_parts(value):
    cdf = 0.5 * (1.0 + lax.erf(value * (0.5**0.5)))
    pdf = jnp.exp(value * value * -0.5) * 0.3989422804014327
    return value * cdf, cdf + value * pdf


def forward_kernel(terms, ids, *refs):
    normed, final = refs[:terms], refs[terms : 2 * terms]
    up, down, hidden, up_low, ff, mid, normed_t = refs[2 * terms : 2 * terms + 7]
    normed_all, final_all, ff_total, mid_total = refs[2 * terms + 7 :]
    step = pl.program_id(0)

    @pl.when(step == 0)
    def _():
        at = 0
        for left, right in zip(normed, final):
            normed_all[at : at + left.shape[0], :] = left[...]
            final_all[at : at + left.shape[0], :] = right[...]
            at += left.shape[0]

    act, slope = gelu_parts(dot(normed_all[...], up[...]))
    low = act.astype(BF)
    hidden[...] = low
    ff_part = dot(low, down[...], NT)
    low = (dot(final_all[...], down[...]) * slope).astype(BF)
    up_low[...] = low
    mid_part = dot(low, up[...], NT)
    last = pl.num_programs(0) - 1
    width = normed_t.shape[0]
    normed_t[...] = normed_all[:, pl.ds(pl.multiple_of(step * width, width), width)].T

    @pl.when(step == 0)
    def _():
        ff_total[...] = ff_part
        mid_total[...] = mid_part

    @pl.when(step > 0)
    def _():
        ff_total[...] += ff_part
        mid_total[...] += mid_part

    @pl.when(step == last)
    def _():
        ff[...] = ff_total[...].astype(BF)
        mid[...] = mid_total[...].astype(BF)


def middle_back_kernel(groups, cw, ids, part, *refs):
    recv = refs[: groups - 1]
    middle, final, w, gain, grad_mid, mid_low, grad_mixed, gains = refs[groups - 1 :]
    total = part[...].astype(F32)
    for other in recv:
        total = total + other[...].astype(F32)
    back, terms = norm_back(middle[...], gain[...], total)
    gains[0:1, :] = jnp.sum(terms, axis=0, keepdims=True)
    gains[1:2, :] = jnp.sum(total, axis=0, keepdims=True)
    value = final[...].astype(F32) + back
    grad_mid[...] = value
    low = value.astype(BF)
    mid_low[...] = low.T
    for j in range(groups):
        grad_mixed[:, j * cw : (j + 1) * cw] = dot(low, columns(w, j, cw, 3)).astype(BF)


def weight_grad_kernel(terms, rows, ids, *refs):
    left, right, outs = refs[:terms], refs[terms : 2 * terms], refs[2 * terms :]
    value = dot(left[0][...], right[0][...])
    for a, b in zip(left[1:], right[1:]):
        value = value + dot(a[...], b[...])
    if len(outs) == 1:
        outs[0][...] = value.astype(BF)
    else:
        keep, send, total = outs
        total[...] = value
        split_rows(rows, ids, total, keep, send)


def split_rows(rows, ids, total, keep, send):
    for b in range(keep.shape[0]):
        for ref, core in ((keep, ids[3]), (send, 1 - ids[3])):
            start = pl.multiple_of((b * 2 + core) * rows, rows)
            ref[b] = total[pl.ds(start, rows), :].astype(BF)


def weight_grad(ids, left, right, rows, block, split, name):
    depth, width = left[0].shape[0], right[0].shape[1]
    if split:
        outs = [struct((depth // rows // 2, rows, width), BF)] * 2
        spec = pl.BlockSpec((depth // rows // 2, rows, block), lambda i, *_: (0, 0, i))
        specs, scratch = [spec, spec], [pltpu.VMEM((depth, block), F32)]
    else:
        outs = [struct((depth, width), BF)]
        specs, scratch = [pl.BlockSpec((depth, block), lambda i, *_: (0, i))], []
    return call(
        functools.partial(weight_grad_kernel, len(left), rows),
        (width // block,),
        [whole(a) for a in left]
        + [pl.BlockSpec((a.shape[0], block), lambda i, *_: (0, i)) for a in right],
        specs,
        outs,
        scratch,
        ids,
        left + right,
        2 * sum(a.shape[0] for a in right) * depth * width,
        name,
    )


def sum_grad_kernel(plan, rows, ids, *refs):
    keep, send, total = refs[2 * sum(terms for _, _, terms in plan) :]
    first = 0
    for at, width, terms in plan:
        value = dot(refs[first][...], refs[first + 1][...])
        for k in range(first + 2, first + 2 * terms, 2):
            value = value + dot(refs[k][...], refs[k + 1][...])
        total[:, at : at + width] = value
        first += 2 * terms
    split_rows(rows, ids, total, keep, send)


def sum_grad(ids, results, rows, depth, name):
    blocks = max(1, 256 // rows)
    plan, specs, args, at, flops = [], [], [], 0, 0
    for terms in results:
        for left, right in terms:
            size, width = right.shape
            specs.append(pl.BlockSpec((blocks * 2 * rows, size), lambda i, ids: (i, 0)))
            specs.append(whole(right))
            args += [left, right]
            flops += 2 * size * width * depth
        plan.append((at, width, len(terms)))
        at += width
    spec = pl.BlockSpec((blocks, rows, at), lambda i, ids: (i, 0, 0))
    return call(
        functools.partial(sum_grad_kernel, plan, rows),
        (depth // (blocks * 2 * rows),),
        specs,
        [spec, spec],
        [struct((depth // rows // 2, rows, at), BF)] * 2,
        [pltpu.VMEM((blocks * 2 * rows, at), F32)],
        ids,
        args,
        flops,
        name,
    )


def source_back_kernel(
    groups, cw, imgs, patch, share, ids, live, gk, gv, wk, wv, media, latents, cot, keep, *refs
):
    recv, refs = refs[: groups - 1], refs[groups - 1 :]
    grad_mid, m_gain, l_gain, media_grad, latent_grad, gains, total, lat_total, query = refs
    base = pl.program_id(0) * imgs
    step = patch + share
    value = dot(gk[:, :cw], wk[0, :, cw : 2 * cw], NT) + dot(gv[:, :cw], columns(wv, 0, cw, 2), NT)
    for j in range(1, groups):
        cols = slice(j * cw, (j + 1) * cw)
        value = value + dot(gk[:, cols], wk[j, :, cw : 2 * cw], NT)
        value = value + dot(gv[:, cols], columns(wv, j, cw, 2), NT)
    total[...] = value
    asked = keep[...]
    for s in range(1, groups):
        asked = asked + lane_roll(recv[s - 1][...].astype(F32), s, groups, cw)
    query[...] = asked.astype(BF)
    value = dot(query[:, :cw], wk[0, :, :cw], NT)
    for j in range(1, groups):
        value = value + dot(query[:, j * cw : (j + 1) * cw], wk[j, :, :cw], NT)
    lat_total[...] = value

    @pl.when(pl.program_id(0) == 0)
    def _():
        gains[...] = jnp.zeros_like(gains)

    sums = [0.0] * 4
    for i in range(imgs):
        grad = total[i * step : i * step + patch, :]
        back, terms = norm_back(media[i].astype(F32), m_gain[...], grad)
        media_grad[i] = back
        sums[0] += fold_rows(terms)
        sums[1] += fold_rows(grad)
        rows = slice(i * share, (i + 1) * share)
        grad = total[i * step + patch : (i + 1) * step, :] + lat_total[rows, :]
        back, terms = norm_back(latents[i].astype(F32), l_gain[...], grad)
        sums[2] += fold_rows(terms)
        sums[3] += fold_rows(grad)
        latent_grad[i] = jnp.where(
            live[base + i] > 0, grad_mid[rows, :] + back, cot[i].astype(F32)
        )
    for k in range(4):
        gains[k : k + 1, :] += jnp.sum(sums[k], axis=0, keepdims=True)


def make_local(depth_z, groups):
    dp_size = depth_z * 4

    def from_dp(value, s=0, yf=0, cf=0):
        pairs = []
        for dst in range(dp_size):
            z, y, c = dst // 4, dst // 2 % 2, dst % 2
            pairs.append(((z + s) % depth_z * 4 + (y ^ yf) * 2 + (c ^ cf), dst))
        return lax.ppermute(value, "dp", pairs)

    def flip_z(value, bit):
        pairs = [(((dst // 4) ^ bit) * 4 + dst % 4, dst) for dst in range(dp_size)]
        return lax.ppermute(value, "dp", pairs)

    def from_head(value, s):
        return lax.ppermute(value, "head", [((x + s) % groups, x) for x in range(groups)])

    def to_head(value, s):
        return lax.ppermute(value, "head", [(x, (x + s) % groups) for x in range(groups)])

    def plane(value, sx, yf, back, cf=0):
        pairs = []
        for dst in range(dp_size):
            for x in range(groups):
                other = (dst ^ (2 * yf + cf)) * groups + (x + sx) % groups
                mine = dst * groups + x
                pairs.append((mine, other) if back else (other, mine))
        return lax.ppermute(value, ("dp", "head"), pairs)

    others = [(sx, yf) for sx in range(groups) for yf in range(2) if sx or yf]

    def local(
        media_tokens,
        latents,
        cotangent,
        image_counts,
        media_gain,
        media_bias,
        latent_gain,
        latent_bias,
        ff_gain,
        ff_bias,
        w_query,
        w_keyval,
        w_attn_out,
        w_up,
        w_down,
    ):
        images, patches, width = media_tokens.shape
        lat = latents.shape[1]
        rows, cw = w_query.shape
        units = w_up.shape[1]
        patch, share = patches // groups, lat // groups
        step = patch + share
        heads_w = cw * groups
        me = lax.axis_index("head").astype(jnp.int32)
        place = lax.axis_index("dp").astype(jnp.int32)
        z, y, c = place // 4, place // 2 % 2, place % 2
        ids = jnp.stack([me, z, y, c])
        live = (jnp.arange(images, dtype=jnp.int32) < jnp.sum(image_counts)).astype(jnp.int32)
        gains = [
            g.reshape(1, width)
            for g in (media_gain, media_bias, latent_gain, latent_bias, ff_gain, ff_bias)
        ]
        media4 = media_tokens.reshape(images, groups, patch, width)
        lat4 = latents.reshape(images, groups, share, width)
        cot4 = cotangent.reshape(images, groups, share, width)

        part = images // CHUNKS
        own = part * share

        shard = jnp.concatenate([w_query, w_keyval[:, 0], w_keyval[:, 1], w_attn_out.T], axis=1)
        got = [from_dp(shard, s) for s in range(1, depth_z)]
        w_up_all = lax.all_gather(w_up, "dp", axis=0, tiled=True)
        w_down_all = lax.all_gather(w_down.T, "dp", axis=0, tiled=True)
        live_low = live.astype(BF).reshape(images, 1, 1)
        final4 = [
            lax.dynamic_index_in_dim(cot4, (me + s) % groups, 1, keepdims=False) * live_low
            for s in range(groups)
        ]
        final4 = jnp.stack(final4).reshape(groups, images * share, width)
        own_t = final4[0].T
        away_t = final4[1:].reshape((groups - 1) * images * share, width).T
        final4, own_t, away_t = tie((final4, own_t, away_t), shard)
        line = jnp.stack([shard] + tie(got, final4, own_t, away_t))
        parts = {(0, 0): line} | {at: plane(line, *at, False) for at in others}

        imgs = math.gcd(images, math.lcm(128, step) // step)
        src, nlat, src_t, nlat_t = call(
            functools.partial(norm_kernel, imgs, lat, share, patch),
            (images // imgs,),
            [
                pl.BlockSpec((imgs, None, patch, width), lambda i, ids: (i, ids[0], 0, 0)),
                images_of(imgs, lat, width),
            ]
            + [whole(gains[0])] * 4,
            [
                rows_of(imgs * step, width),
                rows_of(imgs * lat, width),
                pl.BlockSpec((width, imgs * step), lambda i, ids: (0, i)),
                pl.BlockSpec((width, imgs * lat), lambda i, ids: (0, i)),
            ],
            [
                struct((images * step, width), BF),
                struct((images * lat, width), BF),
                struct((width, images * step), BF),
                struct((width, images * lat), BF),
            ],
            [pltpu.VMEM((lat, width), F32)],
            tie(ids, line),
            [media4, latents] + gains[:4],
            images * step * width * 12,
            "input_norms",
        )

        pieces, entries = [], []
        for (sx, yf), part_of in parts.items():
            for cf, piece in ((0, part_of), (1, from_dp(tie(part_of, src), cf=1))):
                for s in range(depth_z):
                    entries.append((len(pieces), s, sx, s, yf, cf))
                pieces.append(piece)
        w_attn = assemble(entries, pieces, depth_z, ids, rows, groups, 4 * cw, "place_attn")

        imgs = 4
        attn_macs = images * step * lat * heads_w
        q, k, stats = call(
            functools.partial(project_kernel, groups, cw, imgs, step, lat),
            (images // imgs,),
            [rows_of(imgs * step, width), rows_of(imgs * lat, width), third(w_attn, 2 * cw, 0)],
            [
                rows_of(imgs * lat, heads_w),
                rows_of(imgs * step, heads_w),
                images_of(imgs, 2, heads_w),
            ],
            [
                struct((images * lat, heads_w), BF),
                struct((images * step, heads_w), BF),
                struct((images, 2, heads_w), F32),
            ],
            [],
            ids,
            [src, nlat, w_attn],
            2 * images * (step * width * heads_w + lat * width * heads_w) + 8 * attn_macs,
            "project",
        )
        tops, sums = [stats[:, :1]], [stats[:, 1:]]
        for s in range(1, groups):
            other = jnp.roll(from_head(stats, s), s * cw, axis=2)
            tops.append(other[:, :1])
            sums.append(other[:, 1:])
        v = call(
            functools.partial(values_kernel, groups, cw),
            (images // imgs,),
            [rows_of(imgs * step, width), third(w_attn, cw, 2)],
            [rows_of(imgs * step, heads_w)],
            [struct((images * step, heads_w), BF)],
            [],
            tie(ids, q),
            [src, w_attn],
            2 * images * step * width * heads_w,
            "values",
        )[0]
        top = functools.reduce(jnp.maximum, tops)
        lse = top + jnp.log(sum(t * jnp.exp(m - top) for m, t in zip(tops, sums)))

        imgs = min(imgs, part)
        count = part // imgs

        def attn_specs(ch):
            return [
                rows_of(imgs * lat, heads_w, ch * count),
                rows_of(imgs * step, heads_w, ch * count),
                rows_of(imgs * step, heads_w, ch * count),
                images_of(imgs, 1, heads_w, ch * count),
            ]

        row_sends = [
            rows_of(imgs * share, heads_w),
            pl.BlockSpec((groups - 1, imgs * share, heads_w), lambda i, ids: (0, i, 0)),
        ]
        row_outs = [struct((own, heads_w), F32), struct((groups - 1, own, heads_w), BF)]

        def exchanged(keep, send):
            return [keep] + [to_head(send[s - 1], s) for s in range(groups - 1, 0, -1)]

        mixes, normed, mixed, middle = [], [], None, None
        for ch in range(CHUNKS):
            keep, send = call(
                functools.partial(mix_kernel, groups, cw, imgs, step, lat, share),
                (count,),
                attn_specs(ch),
                row_sends,
                row_outs,
                [pltpu.VMEM((imgs, lat, heads_w), F32)],
                tie(ids, [a[0] for a in mixes]),
                [q, k, v, lse],
                8 * attn_macs / CHUNKS,
                f"mix{ch}",
            )
            mixes.append(exchanged(keep, send))
        for ch in range(CHUNKS):
            lat_spec = pl.BlockSpec(
                (part, None, share, width), lambda i, ids, ch=ch: (ch, ids[0], 0, 0)
            )
            outs = call(
                functools.partial(middle_kernel, groups, cw),
                (1,),
                [whole(a) for a in mixes[ch]]
                + [lat_spec, third(w_attn, cw, 3), whole(gains[4]), whole(gains[5])]
                + ([anywhere()] * 2 if ch else []),
                [fixed_rows(own, heads_w, ch), fixed_rows(own, width, ch), fixed_rows(own, width)],
                [
                    struct((CHUNKS * own, heads_w), BF),
                    struct((CHUNKS * own, width), F32),
                    struct((own, width), BF),
                ],
                [],
                tie(ids, [a[0] for a in normed]),
                mixes[ch] + [lat4, w_attn, gains[4], gains[5]] + ([mixed, middle] if ch else []),
                2 * own * heads_w * width,
                f"middle{ch}",
                {groups + 4: 0, groups + 5: 1} if ch else None,
            )
            mixed, middle = outs[:2]
            normed.append([outs[2]] + [from_head(outs[2], s) for s in range(1, groups)])
        block = min(512, units)

        def feed_forward(terms, ids, name):
            size = len(terms) * own
            return call(
                functools.partial(forward_kernel, len(terms)),
                (units // block,),
                [whole(a) for a, _ in terms]
                + [spec for _, spec in terms]
                + [
                    pl.BlockSpec((width, block), lambda i, ids: (0, i)),
                    pl.BlockSpec((width, block), lambda i, ids: (0, i)),
                ],
                [pl.BlockSpec((size, block), lambda i, ids: (0, i))] * 2
                + [fixed_rows(size, width)] * 2
                + [pl.BlockSpec((width * block // units, size), lambda i, ids: (i, 0))],
                [struct((size, units), BF)] * 2
                + [struct((size, width), BF)] * 2
                + [struct((width, size), BF)],
                [pltpu.VMEM((size, width), BF)] * 2 + [pltpu.VMEM((size, width), F32)] * 2,
                ids,
                [a for a, _ in terms] + [final4] * len(terms) + [w_up_all, w_down_all],
                8 * size * width * units,
                name,
            )

        def final_rows(s, ch):
            return pl.BlockSpec((None, own, width), lambda *_: (s, ch, 0))

        size = CHUNKS * own
        away_ff = feed_forward(
            [(normed[ch][t], final_rows(t, ch)) for t in range(1, groups) for ch in range(CHUNKS)],
            ids,
            "feed_forward_away",
        )
        ff_back, mid_back = [a.reshape(groups - 1, size, width) for a in away_ff[2:4]]
        mid_back = [to_head(mid_back[s - 1], s) for s in range(groups - 1, 0, -1)]
        own_ff = feed_forward(
            [(normed[ch][0], final_rows(0, ch)) for ch in range(CHUNKS)],
            tie(ids, away_ff),
            "feed_forward_own",
        )

        def pick(block, index, axis=0):
            return lax.dynamic_index_in_dim(block, index, axis, keepdims=False).astype(F32)

        def lanes(block, cols):
            if len(cols) == 1 and cols[0] == slice(0, block.shape[-1]):
                return block
            return jnp.concatenate([block[..., c] for c in cols], axis=-1)

        class Sum:
            def __init__(self, keep, recv, cols):
                self.cols = cols
                self.grid = [a.reshape((depth_z, 2) + a.shape[1:]) for a in (keep, recv)]
                self.crossed, self.near = [], []

            def at(self, sx, yy):
                terms = [pick(lanes(a, self.cols[sx]), yy, 1) for a in self.grid]
                return sum(terms + [pick(a, yy, 1) for a in self.crossed])

            def cross(self, late):
                grid = tie(self.grid, late)
                self.away = [
                    sum(lanes(a, self.cols[sx]).astype(F32) for a in grid).astype(BF)
                    for sx in range(1, groups)
                ]
                return self.away

            def across(self):
                self.crossed = [to_head(a, sx) for sx, a in zip(range(1, groups), self.away)]

            def second(self, routes, late=()):
                self.grid, self.crossed = tie((self.grid, self.crossed), late)
                self.routes = routes
                self.away = [self.at(sx, y ^ yf).astype(BF) for sx, yf in routes]
                return self.away

            def sent(self):
                self.near = [plane(a, *to, True) for a, to in zip(self.away, self.routes)]

            def start_z(self):
                base = self.at(0, y)

                def block(zz):
                    return pick(base, zz) + sum(pick(a, zz) for a in self.near)

                self.block, self.left, self.bit = block, depth_z, 1

            def halve(self, late=()):
                turn = tie(z, late)
                mine, block = z // self.bit % 2, self.block
                away_at = 1 - turn // self.bit % 2
                self.left //= 2
                self.held = lambda k: block(2 * k + mine)
                away = [block(2 * k + away_at) for k in range(self.left)]
                self.away = jnp.stack(away).astype(BF)
                return self.away

            def halved(self, late=()):
                near, held = tie(flip_z(self.away, self.bit), late), self.held
                self.block, self.bit = (lambda k: held(k) + pick(near, k)), 2 * self.bit

            def rest(self):
                while self.left > 1:
                    self.halve()
                    self.halved()
                return self.block(0)

            def third(self):
                self.start_z()
                self.away = [self.block((z + s) % depth_z).astype(BF) for s in range(1, depth_z)]
                return self.away

            def last(self):
                got = [from_dp(a, depth_z - s) for s, a in zip(range(1, depth_z), self.away)]
                return self.block(z) + sum(a.astype(F32) for a in got)

        along_y = [(0, 1)]

        def groups_of(*starts):
            return [[slice(a + sx * cw, a + (sx + 1) * cw) for a in starts] for sx in range(groups)]

        up_part = weight_grad(
            tie(ids, own_ff[0]),
            [own_ff[4], away_ff[4]],
            [own_ff[1], away_ff[1]],
            rows,
            block,
            False,
            "grad_up",
        )[0]
        grad_mid, mid_low_t, grad_mixed, ff_gains = call(
            functools.partial(middle_back_kernel, groups, cw),
            (1,),
            [whole(own_ff[3])]
            + [whole(t) for t in mid_back]
            + [whole(middle), pl.BlockSpec((None, size, width), lambda *_: (0, 0, 0))]
            + [third(w_attn, cw, 3), whole(gains[4])],
            [
                fixed_rows(size, width),
                fixed_rows(width, size),
                fixed_rows(size, heads_w),
                fixed_rows(2, width),
            ],
            [
                struct((size, width), F32),
                struct((width, size), BF),
                struct((size, heads_w), BF),
                struct((2, width), F32),
            ],
            [],
            tie(ids, up_part),
            [own_ff[3]] + mid_back + [middle, final4, w_attn, gains[4]],
            2 * size * heads_w * width,
            "middle_back",
        )
        grad_mixed = [grad_mixed] + [from_head(grad_mixed, s) for s in range(1, groups)]

        grad_up = lax.psum_scatter(tie(up_part, mid_back), "dp", scatter_dimension=0, tiled=True)
        down_parts = weight_grad(
            tie(ids, mid_low_t),
            [own_t, away_t],
            [own_ff[0], away_ff[0]],
            rows,
            block,
            True,
            "grad_down",
        )

        count = images // imgs
        gv, grad_all, delta = call(
            functools.partial(back_probs_kernel, groups, cw, imgs, step, lat, share),
            (count,),
            attn_specs(0) + [rows_of(imgs * share, heads_w)] * groups,
            [rows_of(imgs * step, heads_w), rows_of(imgs * lat, heads_w), images_of(imgs, 1, heads_w)],
            [
                struct((images * step, heads_w), BF),
                struct((images * lat, heads_w), BF),
                struct((images, 1, heads_w), F32),
            ],
            [pltpu.VMEM((imgs, lat, heads_w), F32)],
            tie(ids, down_parts[0]),
            [q, k, v, lse] + grad_mixed,
            12 * attn_macs,
            "back_probs",
        )
        recv = from_dp(tie(down_parts[1], gv), cf=1)
        sum_down = Sum(down_parts[0], recv, [[slice(0, units)]])
        ordered = jnp.roll(jnp.concatenate([own_ff[2][None], tie(ff_back, gv)]), me, axis=0)
        ff_sum = lax.psum_scatter(tie(ordered, grad_up), "head", scatter_dimension=0, tiled=True)[0]
        total = delta
        for s in range(1, groups):
            total = total + jnp.roll(from_head(delta, s), s * cw, axis=2)
        value_parts = sum_grad(
            tie(ids, gv),
            [[(mid_low_t, mixed)], [(src_t, gv)]],
            rows,
            width,
            "grad_out_values",
        )
        sum_value = Sum(value_parts[0], from_dp(value_parts[1], cf=1), groups_of(0, heads_w))
        gk, gq, keep, send = call(
            functools.partial(back_scores_kernel, groups, cw, imgs, step, lat, share),
            (count,),
            attn_specs(0) + [rows_of(imgs * lat, heads_w), images_of(imgs, 1, heads_w)],
            [rows_of(imgs * step, heads_w), rows_of(imgs * lat, heads_w)] + row_sends,
            [
                struct((images * step, heads_w), BF),
                struct((images * lat, heads_w), BF),
                struct((size, heads_w), F32),
                struct((groups - 1, size, heads_w), BF),
            ],
            [pltpu.VMEM((imgs, lat, heads_w), F32)],
            tie(ids, value_parts[0], sum_down.second(along_y, value_parts[0]), ordered),
            [q, k, v, lse, grad_all, total],
            16 * attn_macs,
            "back_scores",
        )
        sum_down.sent()
        query_terms = exchanged(keep, send)
        key_parts = sum_grad(
            tie(ids, gk, sum_value.cross(gk)),
            [[(src_t, gk)], [(nlat_t, gq)]],
            rows,
            width,
            "grad_query_keys",
        )
        sum_value.across()
        sum_down.start_z()
        sum_key = Sum(key_parts[0], from_dp(key_parts[1], cf=1), groups_of(0, heads_w))

        def share_rows(size):
            return pl.BlockSpec((imgs, None, size, width), lambda i, ids, live: (i, ids[0], 0, 0))

        before = [sum_key.second(others), sum_value.second(along_y), sum_down.halve()]
        media_grad, latent_grad, gain_terms = call(
            functools.partial(source_back_kernel, groups, cw, imgs, patch, share),
            (count,),
            [rows_of(imgs * step, heads_w)] * 2
            + [third(w_attn, 2 * cw, 0), third(w_attn, cw, 2)]
            + [share_rows(patch), share_rows(share), share_rows(share)]
            + [rows_of(imgs * share, heads_w)] * groups
            + [rows_of(imgs * share, width), whole(gains[0]), whole(gains[2])],
            [images_of(imgs, patch, width), images_of(imgs, share, width), fixed_rows(4, width)],
            [
                struct((images, patch, width), F32),
                struct((images, share, width), F32),
                struct((4, width), F32),
            ],
            [
                pltpu.VMEM((imgs * step, width), F32),
                pltpu.VMEM((imgs * share, width), F32),
                pltpu.VMEM((imgs * share, heads_w), BF),
            ],
            [tie(ids, before, grad_up), live],
            [gk, gv, w_attn, w_attn, media4, lat4, cot4]
            + query_terms
            + [grad_mid, gains[0], gains[2]],
            2 * images * step * width * 2 * heads_w,
            "source_back",
        )
        sum_key.sent()
        sum_value.sent()
        sum_key.near = tie(sum_key.near, media_grad)
        sum_value.near = tie(sum_value.near, media_grad)
        sum_down.halved(media_grad)
        last = [jnp.concatenate(pair, axis=1) for pair in zip(sum_key.third(), sum_value.third())]
        last = [from_dp(a, depth_z - s).astype(F32) for s, a in zip(range(1, depth_z), last)]
        query_key = sum_key.block(z) + sum(a[:, : 2 * cw] for a in last)
        out_value = sum_value.block(z) + sum(a[:, 2 * cw :] for a in last)

        final_lat = middle + ff_sum.astype(F32)
        final_lat = final_lat.reshape(images, share, width)
        lat_own = lax.dynamic_index_in_dim(lat4, me, 1, keepdims=False).astype(F32)
        latents_out = jnp.where(live[:, None, None] > 0, final_lat, lat_own)

        total = jnp.concatenate([gain_terms, ff_gains])
        grad_down = sum_down.rest()
        total = total + from_dp(total, cf=1)
        near = [plane(total, *at, False) for at in others]
        total = total + sum(near)
        bit = 1
        while bit < depth_z:
            if 2 * bit == depth_z:
                total = tie(total, grad_down, latents_out)
            total = total + flip_z(total, bit)
            bit *= 2
        norm_grads = total

        return (
            latents_out,
            media_grad,
            latent_grad,
            query_key[:, cw:],
            jnp.stack([query_key[:, :cw], out_value[:, cw:]], axis=1),
            out_value[:, :cw].T,
            grad_up.astype(F32),
            grad_down.T,
            norm_grads,
        )

    return local


def solution(mesh):
    return jax.shard_map(
        make_local(mesh.shape["dp"] // 4, mesh.shape["head"]),
        mesh=mesh,
        in_specs=(
            P("dp", None, None),
            P("dp", None, None),
            P("dp", None, None),
            P("dp"),
            P(),
            P(),
            P(),
            P(),
            P(),
            P(),
            P("dp", "head"),
            P("dp", None, "head"),
            P("head", "dp"),
            P("dp", "head"),
            P("head", "dp"),
        ),
        out_specs=(
            P("dp", "head", None),
            P("dp", "head", None),
            P("dp", "head", None),
            P("dp", "head"),
            P("dp", None, "head"),
            P("head", "dp"),
            P("dp", "head"),
            P("head", "dp"),
            P(),
        ),
        check_vma=False,
    )
```
